32 devices in a mesh: prow: 8 (over z, y), pcol: 4 (over x, core).
Axes of the slice: x: 2, y: 2, z: 4, core: 2. Of those that a mesh axis runs over, the one named last changes fastest.
Arguments:
- right_side: bfloat16 [3, 8, 256, 128], P(None, 'prow'), may hold values from -6 to 6
- lower_blocks: bfloat16 [3, 8, 256, 2048], P(None, 'prow', None, 'pcol'), may hold values from -0.125 to 0.125
- upper_blocks: bfloat16 [3, 8, 256, 2048], P(None, 'prow', None, 'pcol'), may hold values from -0.125 to 0.125
- lower_inverse: bfloat16 [3, 8, 256, 256], P(None, 'prow'), as said below
- upper_inverse: bfloat16 [3, 8, 256, 256], P(None, 'prow'), as said below
- pattern: int32 [3, 8, 8], replicated, may hold values 0 or 1
Outputs:
- solution: bfloat16 [3, 8, 256, 128], P(None, 'prow')
The draws below stay inside these ranges and needn't reach their ends.
Inputs may be any that keep to these rules, and one draw needn't show every extreme that they name: `lower_inverse`: each block is lower triangular with its diagonal between 0.6 and 1.4. `upper_inverse`: each block is upper triangular with its diagonal between 0.6 and 1.4.
All inputs are finite; a program needn't handle non-finite values.
Results may differ from the reference program's by a relative error of at most 0.007.
Values may be sent and summed in bfloat16 or wider, within the bound.
No kernel may reach another device: no remote copies, remote signals or barrier semaphores. Data moves between devices by JAX's collectives and lax.ppermute only.
A program may use at most 64 MiB of HBM per device.

```python
import math
import jax
import jax.numpy as jnp
from jax import lax

B = 256
LEV = 3
NR = 8
PAIRS = 3
W = 128


def triangle_blocks(key, upper_side):
    first_key, second_key = jax.random.split(key)
    diagonal = jax.random.uniform(first_key, (LEV, NR, B), jnp.float32, 0.6, 1.4)
    offside = jax.random.normal(second_key, (LEV, NR, B, B), jnp.float32) * (0.8 / math.sqrt(B))
    row_ids = jnp.arange(B)[:, None]
    col_ids = jnp.arange(B)[None, :]
    if upper_side:
        keep_mask = col_ids > row_ids
    else:
        keep_mask = col_ids < row_ids
    identity = (row_ids == col_ids).astype(jnp.float32)
    matrix = jnp.where(keep_mask, offside, 0.0) + identity * diagonal[..., None]
    return matrix.astype(jnp.bfloat16)


def draw_lower_inverse(key, part):
    return triangle_blocks(jax.random.fold_in(key, 11), False)


def draw_upper_inverse(key, part):
    return triangle_blocks(jax.random.fold_in(key, 23), True)


def set_ends(array, stream_key, least, top_value):
    longest = array.shape.index(max(array.shape))
    spots = []
    for shift in (0, 1):
        where = [jax.random.randint(jax.random.fold_in(stream_key, axis), (), 0, length) for axis, length in enumerate(array.shape)]
        where[longest] = (where[longest] + shift) % array.shape[longest]
        spots.append(tuple(where))
    return array.at[spots[0]].set(least).at[spots[1]].set(top_value)


def steps_of(key, shape, cuts, low, high):
    factor_of = 1.0
    for dim, shards_of in cuts:
        heights = jax.random.uniform(jax.random.fold_in(jax.random.fold_in(key, 6), dim), (shards_of,), jnp.float32, low / len(cuts), high / len(cuts))
        factor_of = factor_of * jnp.repeat(jnp.exp(heights), shape[dim] // shards_of).reshape((-1,) + (1,) * (len(shape) - 1 - dim))
    return factor_of


def gaussian(own_key, extent, scale, reach, pieces=(), kind=jnp.bfloat16):
    values = scale * jax.random.normal(own_key, extent, jnp.float32)
    if pieces:
        values = values * steps_of(own_key, extent, pieces, -0.22, 0.18)
    return jnp.clip(values, -reach, reach).astype(kind)


def setup_inputs(seed: int = 0) -> dict:
    arg_keys = jax.random.split(jax.random.key(seed), 7)
    right_side = gaussian(arg_keys[0], (LEV, NR, B, W), 1.0, 6.0, ((1, 8),))
    lower_blocks = gaussian(arg_keys[1], (PAIRS, NR, B, NR * B), ((LEV - 1) * NR * B // 2) ** -0.5, 0.125, ((1, 8), (3, 4)))
    upper_blocks = gaussian(arg_keys[2], (PAIRS, NR, B, NR * B), ((LEV - 1) * NR * B // 2) ** -0.5, 0.125, ((1, 8), (3, 4)))
    lower_inverse = draw_lower_inverse(jax.random.fold_in(arg_keys[6], 71), 0)
    upper_inverse = draw_upper_inverse(jax.random.fold_in(arg_keys[6], 71), 0)
    pattern = set_ends((jax.random.randint(arg_keys[5], (PAIRS, NR, NR), 0, 2) < 1).astype(jnp.int32), jax.random.fold_in(arg_keys[5], 1), 0, 1)
    return {"right_side": right_side, "lower_blocks": lower_blocks, "upper_blocks": upper_blocks, "lower_inverse": lower_inverse, "upper_inverse": upper_inverse, "pattern": pattern}


def pair_index(later, earlier):
    return later * (later - 1) // 2 + earlier


def masked_matrix(blocks, keep_mask):
    expanded = jnp.repeat(jnp.repeat(keep_mask > 0, B, axis=0), B, axis=1)
    flat = blocks.reshape(NR * B, NR * B)
    return jnp.where(expanded, flat, jnp.zeros((), flat.dtype))


def apply_inverse(inverse, values):
    return jnp.einsum("rij,rjw->riw", inverse.astype(jnp.float32), values, precision=lax.Precision.HIGHEST)


def reference(right_side, lower_blocks, upper_blocks, lower_inverse, upper_inverse, pattern):
    solved = []
    for level_now in range(LEV):
        summed = jnp.zeros((NR * B, W), jnp.float32)
        for earlier in range(level_now):
            pair_now = pair_index(level_now, earlier)
            matrix = masked_matrix(lower_blocks[pair_now], pattern[pair_now])
            summed = summed + jnp.dot(matrix, solved[earlier].reshape(NR * B, W), preferred_element_type=jnp.float32)
        values = right_side[level_now].astype(jnp.float32) - summed.reshape(NR, B, W)
        solved.append(apply_inverse(lower_inverse[level_now], values).astype(jnp.bfloat16))
    results = [None] * LEV
    for level_now in reversed(range(LEV)):
        summed = jnp.zeros((NR * B, W), jnp.float32)
        for later in range(level_now + 1, LEV):
            pair_now = pair_index(later, level_now)
            matrix = masked_matrix(upper_blocks[pair_now], pattern[pair_now].T)
            summed = summed + jnp.dot(matrix, results[later].reshape(NR * B, W), preferred_element_type=jnp.float32)
        values = solved[level_now].astype(jnp.float32) - summed.reshape(NR, B, W)
        results[level_now] = apply_inverse(upper_inverse[level_now], values).astype(jnp.bfloat16)
    return jnp.stack(results)
```

```python
import jax
import jax.numpy as jnp
from jax import lax
from jax.sharding import PartitionSpec as P

CORES = 2


def pair_index(later, earlier):
    return later * (later - 1) // 2 + earlier


def make_body(rows, cols):
    chips = cols // CORES

    def flat(row, chip, core):
        return row * cols + chip * CORES + core

    def every():
        return [
            (row, chip, core)
            for row in range(rows)
            for chip in range(chips)
            for core in range(CORES)
        ]

    def send(value, source_of):
        pairs = [(flat(*source_of(*place)), flat(*place)) for place in every()]
        return lax.ppermute(value, ("prow", "pcol"), pairs)

    def other_core(value):
        return send(value, lambda row, chip, core: (row, chip, 1 - core))

    def body(right_side, lower_blocks, upper_blocks, lower_inverse, upper_inverse, pattern):
        levels = right_side.shape[0]
        block_size = right_side.shape[2]
        width_cols = right_side.shape[3]
        half = width_cols // CORES
        blocks_core = lower_blocks.shape[3] // block_size
        blocks_chip = blocks_core * CORES
        row_index = lax.axis_index("prow")
        col_index = lax.axis_index("pcol")
        chip_index = col_index // CORES
        core_index = col_index % CORES
        pairs = lower_blocks.shape[0]

        roll_by = (row_index + core_index * (blocks_chip - blocks_core)) % blocks_chip
        slots = chip_index * blocks_chip + (jnp.arange(blocks_chip) + row_index) % blocks_chip

        def whole(blocks, pair_now, keep):
            mine = blocks[pair_now, 0]
            both = jnp.concatenate([mine, other_core(mine)], axis=1)
            both = jnp.concatenate([both, both], axis=1)
            rolled = lax.dynamic_slice_in_dim(
                both, roll_by * block_size, blocks_chip * block_size, 1
            )
            keep = jnp.repeat(keep.astype(rolled.dtype), block_size)
            return rolled * keep[None, :]

        order_lower = [pair_index(a, e) for a in range(levels) for e in range(a)]
        order_upper = [pair_index(a, e) for e in reversed(range(levels)) for a in range(e + 1, levels)]
        lower = {}
        upper = {}
        for p in order_lower:
            lower[p] = whole(lower_blocks, p, pattern[p, row_index][slots])
        for p in order_upper:
            upper[p] = whole(upper_blocks, p, pattern[p][:, row_index][slots])

        panel = jnp.swapaxes(right_side[:, 0].astype(jnp.float32), 1, 2)

        def apply(inverse, values):
            return lax.dot_general(
                values,
                inverse.astype(jnp.float32),
                (((1,), (1,)), ((), ())),
                precision=lax.Precision.HIGHEST,
            ).astype(jnp.bfloat16)

        def own(values):
            return lax.dynamic_slice_in_dim(values, core_index * half, half, 0)

        def spread(value):
            parts = [
                send(
                    value,
                    lambda row, chip, core, k=k: (
                        chip * blocks_chip + (k + row) % blocks_chip,
                        row // blocks_chip,
                        core,
                    ),
                )
                for k in range(blocks_chip)
            ]
            return jnp.concatenate(parts, axis=1)

        def times(fetched, matrix):
            return lax.dot_general(
                fetched, matrix, (((1,), (1,)), ((), ())), preferred_element_type=jnp.float32
            )

        def total(partial_value):
            summed = partial_value
            for shift in range(1, chips):
                summed = summed + send(
                    partial_value,
                    lambda row, chip, core, m=shift: (row, (chip + m) % chips, core),
                )
            return summed

        def total_whole(partial_value):
            mine = total(partial_value)
            other = None
            for shift in range(chips):
                part = send(
                    partial_value,
                    lambda row, chip, core, m=shift: (row, (chip + m) % chips, 1 - core),
                )
                other = part if other is None else other + part
            return join(mine, other)

        def join(mine, other):
            first = jnp.where(core_index == 0, mine, other)
            second = jnp.where(core_index == 0, other, mine)
            return jnp.concatenate([first, second], axis=0)

        first_whole = apply(lower_inverse[0, 0], panel[0])
        solved = [None] * levels
        fetched = [None] * levels
        solved[0] = own(first_whole)
        fetched[0] = spread(solved[0])
        for level_now in range(1, levels):
            partial_value = None
            for earlier in range(level_now):
                product = times(fetched[earlier], lower[pair_index(level_now, earlier)])
                partial_value = product if partial_value is None else partial_value + product
            solved[level_now] = apply(
                lower_inverse[level_now, 0], own(panel[level_now]) - total(partial_value)
            )
            if level_now + 1 < levels:
                fetched[level_now] = spread(solved[level_now])
        results = [None] * levels
        fetched = [None] * levels
        for level_now in reversed(range(levels)):
            partial_value = None
            for later in range(level_now + 1, levels):
                product = times(fetched[later], upper[pair_index(later, level_now)])
                partial_value = product if partial_value is None else partial_value + product
            if level_now == 0:
                base = first_whole.astype(jnp.float32)
                if partial_value is not None:
                    base = base - total_whole(partial_value)
                results[0] = apply(upper_inverse[0, 0], base)
                continue
            base = solved[level_now].astype(jnp.float32)
            if partial_value is not None:
                base = base - total(partial_value)
            result = apply(upper_inverse[level_now, 0], base)
            fetched[level_now] = spread(result)
            results[level_now] = join(result, other_core(result))
        return jnp.swapaxes(jnp.stack(results), 1, 2)[:, None]

    return body


def solution(mesh):
    placed = (
        P(None, "prow", None, None),
        P(None, "prow", None, "pcol"),
        P(None, "prow", None, "pcol"),
        P(None, "prow", None, None),
        P(None, "prow", None, None),
        P(),
    )
    return jax.shard_map(
        make_body(mesh.shape["prow"], mesh.shape["pcol"]),
        mesh=mesh,
        in_specs=placed,
        out_specs=P(None, "prow", None, None),
        check_vma=False,
    )
```

```python
import jax
import jax.numpy as jnp
from jax import lax
from jax.sharding import PartitionSpec as P

CORES = 2


def pair_index(later, earlier):
    return later * (later - 1) // 2 + earlier


def split(values):
    high = values.astype(jnp.bfloat16)
    low = (values - high.astype(jnp.float32)).astype(jnp.bfloat16)
    return high, low


def make_body(rows, cols):
    chips = cols // CORES

    def flat(row, chip, core):
        return row * cols + chip * CORES + core

    def send(value, source_of):
        places = [(a, b, c) for a in range(rows) for b in range(chips) for c in range(CORES)]
        pairs = [(flat(*source_of(*place)), flat(*place)) for place in places]
        return lax.ppermute(value, ("prow", "pcol"), pairs)

    def other_core(value):
        return send(value, lambda row, chip, core: (row, chip, 1 - core))

    def other_chip(value, shift):
        return send(value, lambda row, chip, core: (row, (chip - shift) % chips, core))

    def body(right_side, lower_blocks, upper_blocks, lower_inverse, upper_inverse, pattern):
        levels = right_side.shape[0]
        block_size = right_side.shape[2]
        width_cols = right_side.shape[3]
        half = width_cols // CORES
        strip = block_size // chips
        group = lower_blocks.shape[3] // block_size
        row_index = lax.axis_index("prow")
        col_index = lax.axis_index("pcol")
        chip_index = col_index // CORES
        core_index = col_index % CORES

        def mine_of(values, chip):
            return lax.dynamic_slice_in_dim(values, chip * strip, strip, values.ndim - 1)

        def relay(blocks, keep):
            keep = lax.dynamic_slice_in_dim(keep, col_index * group, group, 0)
            blocks = blocks.reshape(block_size, group, block_size).transpose(1, 0, 2)
            blocks = blocks * keep.astype(blocks.dtype)[:, None, None]
            pieces = [mine_of(blocks, chip_index)]
            for shift in range(1, chips):
                pieces.append(
                    other_chip(mine_of(blocks, (chip_index + shift) % chips), shift)
                )
            pieces = jnp.stack(pieces)
            order = (chip_index - jnp.arange(chips)) % chips
            if chips == 2:
                pieces = jnp.where(chip_index == 0, pieces, pieces[::-1])
            else:
                pieces = pieces[order]
            other = other_core(pieces)
            both = jnp.where(
                core_index == 0, jnp.stack([pieces, other], 1), jnp.stack([other, pieces], 1)
            )
            return both.reshape(cols * group, block_size, strip).transpose(1, 0, 2).reshape(
                block_size, cols * group * strip
            )

        def exact(left, right):
            return jnp.dot(left, right, preferred_element_type=jnp.float32)

        def fold(left, matrix):
            return split(sum(exact(part, matrix) for part in left))

        def fold_panel(left, values):
            return lax.dot_general(
                values, left, (((1,), (1,)), ((), ())), precision=lax.Precision.HIGHEST
            )

        def times(fetched, matrix):
            return sum(
                lax.dot_general(
                    fetched, part, (((1,), (1,)), ((), ())), preferred_element_type=jnp.float32
                )
                for part in matrix
            )

        def spread(value):
            sent = jnp.broadcast_to(value[None], (rows,) + value.shape)
            got = lax.all_to_all(sent, "prow", 0, 0, tiled=True)
            return got.transpose(1, 0, 2).reshape(value.shape[0], rows * value.shape[1])

        def total(partial_value):
            summed = mine_of(partial_value, chip_index)
            for shift in range(1, chips):
                summed = summed + other_chip(
                    mine_of(partial_value, (chip_index + shift) % chips), shift
                )
            return summed

        pattern = pattern.astype(jnp.bfloat16)
        keep_lower = lax.dynamic_index_in_dim(pattern, row_index, 1, keepdims=False)
        keep_upper = lax.dynamic_index_in_dim(pattern, row_index, 2, keepdims=False)
        pairs_lower = [pair_index(a, e) for a in range(levels) for e in range(a)]
        pairs_upper = [
            pair_index(a, e) for e in reversed(range(levels)) for a in range(e + 1, levels)
        ]
        lower = {p: relay(lower_blocks[p, 0], keep_lower[p]) for p in pairs_lower}
        upper = {p: relay(upper_blocks[p, 0], keep_upper[p]) for p in pairs_upper}

        panel = jnp.swapaxes(right_side[:, 0].astype(jnp.float32), 1, 2)
        top = levels - 1
        lower_f32 = lower_inverse[:, 0].astype(jnp.float32)
        upper_f32 = upper_inverse[:, 0].astype(jnp.float32)
        start = [fold_panel(lower_f32[k], panel[k]) for k in range(levels)]
        start[0] = start[0].astype(jnp.bfloat16).astype(jnp.float32)
        ends = [fold_panel(upper_f32[k], start[k]) for k in range(levels)]

        def own(values):
            return lax.dynamic_slice_in_dim(values, core_index * half, half, 0)

        to_forward = {}
        to_backward = {}
        for later in range(1, levels):
            joined = exact(upper_inverse[later, 0], lower_inverse[later, 0])
            high, low = split(joined)
            rest = (joined - high.astype(jnp.float32) - low.astype(jnp.float32)).astype(jnp.bfloat16)
            for earlier in range(later):
                p = pair_index(later, earlier)
                if later < top:
                    to_forward[p] = fold([lower_inverse[later, 0]], lower[p])
                to_backward[p] = fold([high, low, rest], lower[p])
        upper = {
            pair_index(a, e): fold([upper_inverse[e, 0]], upper[pair_index(a, e)])
            for a in range(levels)
            for e in range(a)
        }

        fetched = [None] * levels
        for level_now in range(top):
            value = own(mine_of(start[level_now], chip_index))
            if level_now > 0:
                value = value - total(
                    sum(
                        times(fetched[e], to_forward[pair_index(level_now, e)])
                        for e in range(level_now)
                    )
                )
            fetched[level_now] = spread(value.astype(jnp.bfloat16))

        back = [None] * levels
        results = [None] * levels

        def join(mine, other):
            first = jnp.where(core_index == 0, mine, other)
            second = jnp.where(core_index == 0, other, mine)
            return jnp.concatenate([first, second], axis=0)

        for level_now in reversed(range(levels)):
            partial_value = 0.0
            for earlier in range(level_now):
                partial_value = partial_value + times(
                    fetched[earlier], to_backward[pair_index(level_now, earlier)]
                )
            for later in range(level_now + 1, levels):
                partial_value = partial_value + times(
                    back[later], upper[pair_index(later, level_now)]
                )
            if level_now > 0:
                value = own(mine_of(ends[level_now], chip_index)) - total(partial_value)
                value = value.astype(jnp.bfloat16)
                back[level_now] = spread(value)
                parts = [value] + [other_chip(value, shift) for shift in range(1, chips)]
                inverse_order = (chip_index - jnp.arange(chips)) % chips
                whole = jnp.stack(parts)[inverse_order]
                whole = whole.transpose(1, 0, 2).reshape(half, block_size)
                results[level_now] = join(whole, other_core(whole))
            else:
                mine = partial_value
                other = other_core(partial_value)
                for shift in range(1, chips):
                    mine = mine + other_chip(partial_value, shift)
                    other = other + send(
                        partial_value,
                        lambda row, chip, core, m=shift: (row, (chip - m) % chips, 1 - core),
                    )
                results[0] = (ends[0] - join(mine, other)).astype(jnp.bfloat16)
        return jnp.swapaxes(jnp.stack(results), 1, 2)[:, None]

    return body


def solution(mesh):
    placed = (
        P(None, "prow", None, None),
        P(None, "prow", None, "pcol"),
        P(None, "prow", None, "pcol"),
        P(None, "prow", None, None),
        P(None, "prow", None, None),
        P(),
    )
    return jax.shard_map(
        make_body(mesh.shape["prow"], mesh.shape["pcol"]),
        mesh=mesh,
        in_specs=placed,
        out_specs=P(None, "prow", None, None),
        check_vma=False,
    )
```

```python
import jax
import jax.numpy as jnp
from jax import lax
from jax.sharding import PartitionSpec as P

CORES = 2


def pair_index(later, earlier):
    return later * (later - 1) // 2 + earlier


def split(values):
    high = values.astype(jnp.bfloat16)
    low = (values - high.astype(jnp.float32)).astype(jnp.bfloat16)
    return high, low


def make_body(rows, cols):
    chips = cols // CORES

    def flat(row, chip, core):
        return row * cols + chip * CORES + core

    def send(value, source_of):
        places = [(a, b, c) for a in range(rows) for b in range(chips) for c in range(CORES)]
        pairs = [(flat(*source_of(*place)), flat(*place)) for place in places]
        return lax.ppermute(value, ("prow", "pcol"), pairs)

    def other_core(value):
        return send(value, lambda row, chip, core: (row, chip, 1 - core))

    def other_chip(value, shift):
        return send(value, lambda row, chip, core: (row, (chip - shift) % chips, core))

    def body(right_side, lower_blocks, upper_blocks, lower_inverse, upper_inverse, pattern):
        levels = right_side.shape[0]
        block_size = right_side.shape[2]
        width_cols = right_side.shape[3]
        half = width_cols // CORES
        strip = block_size // chips
        group = lower_blocks.shape[3] // block_size
        row_index = lax.axis_index("prow")
        col_index = lax.axis_index("pcol")
        chip_index = col_index // CORES
        core_index = col_index % CORES

        def mine_of(values, chip):
            return lax.dynamic_slice_in_dim(values, chip * strip, strip, values.ndim - 1)

        def relay(blocks, keep):
            keep = lax.dynamic_slice_in_dim(keep, col_index * group, group, 0)
            blocks = blocks.reshape(block_size, group, block_size).transpose(1, 0, 2)
            blocks = blocks * keep.astype(blocks.dtype)[:, None, None]
            pieces = [mine_of(blocks, chip_index)]
            for shift in range(1, chips):
                pieces.append(
                    other_chip(mine_of(blocks, (chip_index + shift) % chips), shift)
                )
            pieces = jnp.stack(pieces)
            order = (chip_index - jnp.arange(chips)) % chips
            if chips == 2:
                pieces = jnp.where(chip_index == 0, pieces, pieces[::-1])
            else:
                pieces = pieces[order]
            other = other_core(pieces)
            both = jnp.where(
                core_index == 0, jnp.stack([pieces, other], 1), jnp.stack([other, pieces], 1)
            )
            return both.reshape(cols * group, block_size, strip).transpose(1, 0, 2).reshape(
                block_size, cols * group * strip
            )

        def exact(left, right):
            return jnp.dot(left, right, preferred_element_type=jnp.float32)

        def fold(left, matrix):
            return split(sum(exact(part, matrix) for part in left))

        def fold_panel(left, values):
            return lax.dot_general(
                values, left, (((1,), (1,)), ((), ())), precision=lax.Precision.HIGHEST
            )

        def times(fetched, matrix):
            return sum(
                lax.dot_general(
                    fetched, part, (((1,), (1,)), ((), ())), preferred_element_type=jnp.float32
                )
                for part in matrix
            )

        def spread(value):
            got = lax.all_gather(value, "prow", axis=0)
            return got.transpose(1, 0, 2).reshape(value.shape[0], rows * value.shape[1])

        def total(partial_value):
            summed = mine_of(partial_value, chip_index)
            for shift in range(1, chips):
                summed = summed + other_chip(
                    mine_of(partial_value, (chip_index + shift) % chips), shift
                )
            return summed

        pattern = pattern.astype(jnp.bfloat16)
        keep_lower = lax.dynamic_index_in_dim(pattern, row_index, 1, keepdims=False)
        keep_upper = lax.dynamic_index_in_dim(pattern, row_index, 2, keepdims=False)
        pairs_lower = [pair_index(a, e) for a in range(levels) for e in range(a)]
        pairs_upper = [
            pair_index(a, e) for e in reversed(range(levels)) for a in range(e + 1, levels)
        ]
        lower = {p: relay(lower_blocks[p, 0], keep_lower[p]) for p in pairs_lower}
        upper = {p: relay(upper_blocks[p, 0], keep_upper[p]) for p in pairs_upper}

        panel = jnp.swapaxes(right_side[:, 0].astype(jnp.float32), 1, 2)
        top = levels - 1
        lower_f32 = lower_inverse[:, 0].astype(jnp.float32)
        upper_f32 = upper_inverse[:, 0].astype(jnp.float32)
        start = [fold_panel(lower_f32[k], panel[k]) for k in range(levels)]
        start[0] = start[0].astype(jnp.bfloat16).astype(jnp.float32)
        ends = [fold_panel(upper_f32[k], start[k]) for k in range(levels)]

        def own(values):
            return lax.dynamic_slice_in_dim(values, core_index * half, half, 0)

        to_forward = {}
        to_backward = {}
        for later in range(1, levels):
            joined = exact(upper_inverse[later, 0], lower_inverse[later, 0])
            high, low = split(joined)
            rest = (joined - high.astype(jnp.float32) - low.astype(jnp.float32)).astype(jnp.bfloat16)
            for earlier in range(later):
                p = pair_index(later, earlier)
                if later < top:
                    to_forward[p] = fold([lower_inverse[later, 0]], lower[p])
                to_backward[p] = fold([high, low, rest], lower[p])
        upper = {
            pair_index(a, e): fold([upper_inverse[e, 0]], upper[pair_index(a, e)])
            for a in range(levels)
            for e in range(a)
        }

        fetched = [None] * levels
        for level_now in range(top):
            value = own(mine_of(start[level_now], chip_index))
            if level_now > 0:
                value = value - total(
                    sum(
                        times(fetched[e], to_forward[pair_index(level_now, e)])
                        for e in range(level_now)
                    )
                )
            fetched[level_now] = spread(value.astype(jnp.bfloat16))

        back = [None] * levels
        results = [None] * levels

        def join(mine, other):
            first = jnp.where(core_index == 0, mine, other)
            second = jnp.where(core_index == 0, other, mine)
            return jnp.concatenate([first, second], axis=0)

        for level_now in reversed(range(levels)):
            partial_value = 0.0
            for earlier in range(level_now):
                partial_value = partial_value + times(
                    fetched[earlier], to_backward[pair_index(level_now, earlier)]
                )
            for later in range(level_now + 1, levels):
                partial_value = partial_value + times(
                    back[later], upper[pair_index(later, level_now)]
                )
            if level_now > 0:
                value = own(mine_of(ends[level_now], chip_index)) - total(partial_value)
                value = value.astype(jnp.bfloat16)
                back[level_now] = spread(value)
                parts = [value] + [other_chip(value, shift) for shift in range(1, chips)]
                inverse_order = (chip_index - jnp.arange(chips)) % chips
                whole = jnp.stack(parts)[inverse_order]
                whole = whole.transpose(1, 0, 2).reshape(half, block_size)
                results[level_now] = join(whole, other_core(whole))
            else:
                mine = partial_value
                other = other_core(partial_value)
                for shift in range(1, chips):
                    mine = mine + other_chip(partial_value, shift)
                    other = other + send(
                        partial_value,
                        lambda row, chip, core, m=shift: (row, (chip - m) % chips, 1 - core),
                    )
                results[0] = (ends[0] - join(mine, other)).astype(jnp.bfloat16)
        return jnp.swapaxes(jnp.stack(results), 1, 2)[:, None]

    return body


def solution(mesh):
    placed = (
        P(None, "prow", None, None),
        P(None, "prow", None, "pcol"),
        P(None, "prow", None, "pcol"),
        P(None, "prow", None, None),
        P(None, "prow", None, None),
        P(),
    )
    return jax.shard_map(
        make_body(mesh.shape["prow"], mesh.shape["pcol"]),
        mesh=mesh,
        in_specs=placed,
        out_specs=P(None, "prow", None, None),
        check_vma=False,
    )
```

```python
import functools

import jax
import jax.numpy as jnp
from jax import lax
from jax.experimental import pallas as pl
from jax.experimental.pallas import tpu as pltpu
from jax.sharding import PartitionSpec as P

CORES = 2
VMEM_BYTES = 40 * 1024 * 1024


def pair_index(later, earlier):
    return later * (later - 1) // 2 + earlier


def exact(left, right):
    return jnp.dot(left, right, preferred_element_type=jnp.float32)


def split(values, count):
    parts = []
    for _ in range(count):
        part = values.astype(jnp.bfloat16)
        parts.append(part)
        values = values - part.astype(jnp.float32)
    return parts


def call(kernel, shapes, operands, scalars=0, scratch=()):
    specs = [
        pl.BlockSpec(memory_space=pltpu.SMEM if place < scalars else pltpu.VMEM)
        for place in range(len(operands))
    ]
    return pl.pallas_call(
        kernel,
        out_shape=shapes,
        in_specs=specs,
        out_specs=jax.tree.map(lambda _: pl.BlockSpec(memory_space=pltpu.VMEM), shapes),
        scratch_shapes=list(scratch),
        compiler_params=pltpu.CompilerParams(vmem_limit_bytes=VMEM_BYTES),
    )(*operands)


def half_of(values, turned, half, core):
    turned[...] = values.T
    return turned[pl.ds(pl.multiple_of(core * half, half), half), :]


def first_kernel(half, spot, rhs, inverse, out, turned):
    out[...] = half_of(exact(inverse[...], rhs[...]), turned, half, spot[2]).astype(out.dtype)


def panel_kernel(half, levels, spot, first, rhs, lower, upper, *rest):
    outs, turned = rest[:-1], rest[-1]
    core = spot[2]
    mine = spot[1] == 0
    upper_now = upper[0].astype(jnp.bfloat16)
    value = lax.dot_general(
        first[...], upper_now, (((1,), (1,)), ((), ())), preferred_element_type=jnp.float32
    )
    outs[0][...] = jnp.where(mine, value, 0.0)
    for level in range(1, levels):
        start = exact(lower[level], rhs[level])
        end = sum(exact(upper[level], part) for part in split(start, 3))
        outs[level][...] = jnp.where(mine, half_of(end, turned, half, core), 0.0)
        if level < levels - 1:
            value = half_of(start, turned, half, core)
            outs[levels + level - 1][...] = jnp.where(mine, value, 0.0)


def fold_kernel(picks, lefts, group, spot, pattern, *refs):
    count = max(pick[2] for pick in picks) + 1
    inverses = refs[: 2 * count]
    refs = refs[2 * count :]
    outs = refs[-len(picks) :]
    pieces = refs[: -len(picks)]
    row, chip, core, depth = spot[0], spot[1], spot[2], spot[3]
    place = chip * CORES + core
    sides = []
    for left in range(count):
        a, b = inverses[2 * left][...], inverses[2 * left + 1][...]
        sides.append(split(exact(a, b), 3) if lefts[left] == "both" else [a])
    for q, piece in enumerate(pieces):
        source = place ^ q
        block = source * group + chip
        slot = source ^ depth
        for pick, out in zip(picks, outs):
            where, pair, left, is_upper = pick
            keep = pattern[pair, block, row] if is_upper else pattern[pair, row, block]
            matrix = piece[where]
            matrix = jnp.where(keep > 0, matrix, jnp.zeros_like(matrix))
            folded = sum(exact(part, matrix) for part in sides[left]).T
            for index, part in enumerate(split(folded, 2)):
                out[slot, index] = part


def step_kernel(slots, base, *refs):
    out = refs[-1]
    refs = refs[:-1]
    total = base[...]
    for term in range(len(refs) // (slots + 1)):
        blocks = refs[term * (slots + 1) :][:slots]
        matrix = refs[term * (slots + 1) + slots]
        for slot in range(slots):
            block = blocks[slot][...]
            for part in range(2):
                total = total - exact(block, matrix[slot, part])
    out[...] = total


def last_kernel(levels, spot, *refs):
    out, turned = refs[-2], refs[-1]
    half = turned.shape[0] // CORES
    core = spot[2]
    mine_at = pl.ds(pl.multiple_of(core * half, half), half)
    other_at = pl.ds(pl.multiple_of((1 - core) * half, half), half)
    place = 0
    for level in range(levels - 1, 0, -1):
        turned[mine_at, :] = refs[place][...].astype(jnp.float32)
        turned[other_at, :] = refs[place + 1][...].astype(jnp.float32)
        out[level] = turned[...].T.astype(out.dtype)
        place += 2
    sums = refs[place:-2]
    count = len(sums) // CORES
    turned[mine_at, :] = sum(part[...] for part in sums[:count])
    turned[other_at, :] = sum(part[...] for part in sums[count:])
    out[0] = turned[...].T.astype(out.dtype)


def make_body(rows, cols):
    chips = cols // CORES
    lines = chips
    depths = rows // lines
    assert depths == cols and lines == chips

    def send(value, source_of):
        pairs = []
        for z in range(depths):
            for y in range(lines):
                for x in range(chips):
                    for core in range(CORES):
                        a, b, c, d = source_of(z, y, x, core)
                        pairs.append(
                            (
                                (a * lines + b) * cols + c * CORES + d,
                                (z * lines + y) * cols + x * CORES + core,
                            )
                        )
        return lax.ppermute(value, ("prow", "pcol"), pairs)

    def body(right_side, lower_blocks, upper_blocks, lower_inverse, upper_inverse, pattern):
        levels, _, size, width = right_side.shape
        half = width // CORES
        group = lower_blocks.shape[3] // size
        assert group == chips
        row = lax.axis_index("prow")
        col = lax.axis_index("pcol")
        chip = col // CORES
        spot = jnp.stack([row, chip, col % CORES, row // lines]).astype(jnp.int32)
        rhs, lower, upper = right_side[:, 0], lower_inverse[:, 0], upper_inverse[:, 0]
        top = levels - 1
        piece = jax.ShapeDtypeStruct((half, size), jnp.float32)
        chunk = jax.ShapeDtypeStruct((half, size), jnp.bfloat16)
        turned = pltpu.VMEM((width, size), jnp.float32)

        def relay(blocks):
            pick = lambda which: lax.dynamic_slice_in_dim(blocks, which * size, size, 2)
            near = [pick(chip)]
            near += [
                send(pick(chip ^ b), lambda z, y, x, core, b=b: (z, y, x ^ b, core))
                for b in range(1, chips)
            ]
            far = [send(value, lambda z, y, x, core: (z, y, x, 1 - core)) for value in near]
            return [value for pair in zip(near, far) for value in pair]

        def fold(picks, lefts, inverses, pieces):
            shape = jax.ShapeDtypeStruct((depths, 2, size, size), jnp.bfloat16)
            return call(
                functools.partial(fold_kernel, picks, lefts, group),
                [shape] * len(picks),
                [spot, pattern] + inverses + pieces,
                scalars=2,
            )

        def across(value):
            return [value] + [
                send(value, lambda z, y, x, core, m=m: (z ^ m, y, x, core))
                for m in range(1, depths)
            ]

        def gather(partial_value):
            parts = [
                send(partial_value, lambda z, y, x, core, b=b: (z, x, y ^ b, core))
                for b in range(chips)
            ]
            return sum(parts).astype(jnp.bfloat16)

        def step(base, terms):
            operands = [base]
            for blocks, matrix in terms:
                operands += blocks + [matrix]
            return call(functools.partial(step_kernel, depths), piece, operands)

        first = call(
            functools.partial(first_kernel, half),
            chunk,
            [spot, rhs[0], lower[0]],
            scalars=1,
            scratch=[turned],
        )
        low_one = relay(lower_blocks[:1, 0])
        fetched = {}
        fetched[0] = [
            send(first, lambda z, y, x, core, m=m: (z ^ m, x, y, core)) for m in range(depths)
        ]
        low_rest = relay(lower_blocks[1:, 0])
        high_all = relay(upper_blocks[:, 0])

        panels = call(
            functools.partial(panel_kernel, half, levels),
            [piece] * (2 * levels - 2),
            [spot, first, rhs, lower, upper],
            scalars=1,
            scratch=[turned],
        )
        ends, starts = panels[:levels], [None] + list(panels[levels:])

        forward, backward = {}, {}
        for later in range(1, levels):
            pieces = low_one if later == 1 else low_rest
            offset = 0 if later == 1 else 1
            pairs = [pair_index(later, e) for e in range(later)]
            if later < top:
                picks = tuple((p - offset, p, 0, False) for p in pairs)
                found = fold(picks, ("one",), [lower[later], lower[later]], pieces)
                forward.update(zip(pairs, found))
            picks = tuple((p - offset, p, 0, False) for p in pairs)
            found = fold(picks, ("both",), [upper[later], lower[later]], pieces)
            backward.update(zip(pairs, found))
        upward = {}
        for earlier in reversed(range(top)):
            pairs = [pair_index(a, earlier) for a in range(earlier + 1, levels)]
            picks = tuple((p, p, 0, True) for p in pairs)
            found = fold(picks, ("one",), [upper[earlier], upper[earlier]], high_all)
            upward.update(zip(pairs, found))

        for level in range(1, top):
            value = starts[level]
            for earlier in range(level):
                value = step(value, [(fetched[earlier], forward[pair_index(level, earlier)])])
            fetched[level] = across(gather(value))

        back, results = {}, []
        for level in reversed(range(levels)):
            value = ends[level]
            for earlier in range(level):
                value = step(value, [(fetched[earlier], backward[pair_index(level, earlier)])])
            for later in reversed(range(level + 1, levels)):
                value = step(value, [(back[later], upward[pair_index(later, level)])])
            if level > 0:
                solved = gather(value)
                back[level] = across(solved)
                mine = send(solved, lambda z, y, x, core: (z, x, y, core))
                results += [mine, send(mine, lambda z, y, x, core: (z, y, x, 1 - core))]
        sums = [
            value
            if b == 0 and other == 0
            else send(value, lambda z, y, x, core, b=b, o=other: (z, y, x ^ b, core ^ o))
            for other in range(CORES)
            for b in range(chips)
        ]
        out = call(
            functools.partial(last_kernel, levels),
            jax.ShapeDtypeStruct((levels, size, width), jnp.bfloat16),
            [spot] + results + sums,
            scalars=1,
            scratch=[turned],
        )
        return out[:, None]

    return body


def solution(mesh):
    placed = (
        P(None, "prow", None, None),
        P(None, "prow", None, "pcol"),
        P(None, "prow", None, "pcol"),
        P(None, "prow", None, None),
        P(None, "prow", None, None),
        P(),
    )
    return jax.shard_map(
        make_body(mesh.shape["prow"], mesh.shape["pcol"]),
        mesh=mesh,
        in_specs=placed,
        out_specs=P(None, "prow", None, None),
        check_vma=False,
    )
```

```python
import functools

import jax
import jax.numpy as jnp
from jax import lax
from jax.experimental import pallas as pl
from jax.experimental.pallas import tpu as pltpu
from jax.sharding import PartitionSpec as P

CORES = 2
ROW, CHIP, CORE, DEPTH, LINE = range(5)
VMEM_BYTES = 40 * 1024 * 1024


def pair_index(later, earlier):
    return later * (later - 1) // 2 + earlier


def exact(left, right):
    return jnp.dot(left, right, preferred_element_type=jnp.float32)


def split(values, count):
    parts = []
    for _ in range(count):
        part = values.astype(jnp.bfloat16)
        parts.append(part)
        values = values - part.astype(jnp.float32)
    return parts


def call(kernel, shapes, operands, scalars=0, scratch=()):
    specs = [
        pl.BlockSpec(memory_space=pltpu.SMEM if place < scalars else pltpu.VMEM)
        for place in range(len(operands))
    ]
    return pl.pallas_call(
        kernel,
        out_shape=shapes,
        in_specs=specs,
        out_specs=jax.tree.map(lambda _: pl.BlockSpec(memory_space=pltpu.VMEM), shapes),
        scratch_shapes=list(scratch),
        compiler_params=pltpu.CompilerParams(vmem_limit_bytes=VMEM_BYTES),
    )(*operands)


def share_of(values, turned, share, chip):
    turned[...] = values.T
    return turned[pl.ds(pl.multiple_of(chip * share, share), share), :]


def first_kernel(share, spot, rhs, inverse, out, turned):
    out[...] = share_of(exact(inverse[...], rhs[...]), turned, share, spot[CHIP]).astype(out.dtype)


def panel_kernel(share, levels, spot, first, rhs, lower, upper, *rest):
    outs, turned = rest[:-1], rest[-1]
    chip = spot[CHIP]
    mine = spot[CORE] == 0
    value = lax.dot_general(
        first[...], upper[0], (((1,), (1,)), ((), ())), preferred_element_type=jnp.float32
    )
    outs[0][...] = jnp.where(mine, value, 0.0)
    for level in range(1, levels):
        start = exact(lower[level], rhs[level])
        end = sum(exact(upper[level], part) for part in split(start, 3))
        outs[level][...] = jnp.where(mine, share_of(end, turned, share, chip), 0.0)
        if level < levels - 1:
            value = share_of(start, turned, share, chip)
            outs[levels + level - 1][...] = jnp.where(mine, value, 0.0)


def pack_kernel(size, spot, blocks, same, cross):
    core = spot[CORE]
    for index in range(same.shape[1]):
        for out, parity in ((same, core), (cross, 1 - core)):
            start = pl.multiple_of((CORES * index + parity) * size, size)
            out[:, index] = blocks[:, :, pl.ds(start, size)]


def fold_kernel(picks, lefts, group, lines, spot, pattern, *refs):
    count = len(lefts)
    inverses = refs[: 2 * count]
    refs = refs[2 * count :]
    outs = refs[-len(picks) :]
    pieces = refs[: -len(picks)]
    row, chip, core = spot[ROW], spot[CHIP], spot[CORE]
    depth, line = spot[DEPTH], spot[LINE]
    place = chip * CORES + core
    sides = []
    for left in range(count):
        a, b = inverses[2 * left][...], inverses[2 * left + 1][...]
        sides.append(split(exact(a, b), 3) if lefts[left] == "both" else [a])
    for q, piece in enumerate(pieces):
        for index in range(group // CORES):
            block = (place ^ q) * group + CORES * index + core
            deep, across = block // lines, block % lines
            slot = (deep ^ depth) * (lines // CORES) + ((across // CORES) ^ (line // CORES))
            for pick, out in zip(picks, outs):
                where, pair, left, is_upper = pick
                keep = pattern[pair, block, row] if is_upper else pattern[pair, row, block]
                matrix = piece[where, index]
                matrix = jnp.where(keep > 0, matrix, jnp.zeros_like(matrix))
                folded = sum(exact(part, matrix) for part in sides[left]).T
                for turn, part in enumerate(split(folded, 2)):
                    out[slot, turn] = part


def step_kernel(depths, base, *refs):
    out = refs[-1]
    refs = refs[:-1]
    total = base[...]
    share = total.shape[0]
    for term in range(len(refs) // (depths + 1)):
        blocks = refs[term * (depths + 1) :][:depths]
        matrix = refs[term * (depths + 1) + depths]
        each = matrix.shape[0] // depths
        for depth in range(depths):
            for index in range(each):
                block = blocks[depth][index * share : (index + 1) * share, :]
                for part in range(2):
                    total = total - exact(block, matrix[depth * each + index, part])
    out[...] = total


def last_kernel(levels, chips, spot, *refs):
    out, turned = refs[-2], refs[-1]
    share = turned.shape[0] // chips
    chip = spot[CHIP]
    at = [pl.ds(pl.multiple_of((chip ^ b) * share, share), share) for b in range(chips)]
    for level in range(1, levels):
        for b in range(chips):
            part = refs[b][(level - 1) * share : level * share, :]
            turned[at[b], :] = part.astype(jnp.float32)
        out[level] = turned[...].T.astype(out.dtype)
    sums = refs[chips:-2]
    for b in range(chips):
        turned[at[b], :] = sum(part[...] for part in sums[b * CORES : (b + 1) * CORES])
    out[0] = turned[...].T.astype(out.dtype)


def make_body(rows, cols):
    chips = cols // CORES
    lines = chips
    depths = rows // lines
    wide = lines // CORES

    def send(value, source_of):
        pairs = []
        for z in range(depths):
            for y in range(lines):
                for x in range(chips):
                    for core in range(CORES):
                        source = source_of(z, y, x, core)
                        if source is None:
                            continue
                        a, b, c, d = source
                        pairs.append(
                            (
                                (a * lines + b) * cols + c * CORES + d,
                                (z * lines + y) * cols + x * CORES + core,
                            )
                        )
        return lax.ppermute(value, ("prow", "pcol"), pairs)

    def body(right_side, lower_blocks, upper_blocks, lower_inverse, upper_inverse, pattern):
        levels, _, size, width = right_side.shape
        share = width // chips
        group = lower_blocks.shape[3] // size
        row = lax.axis_index("prow")
        col = lax.axis_index("pcol")
        line, core = row % lines, col % CORES
        spot = jnp.stack([row, col // CORES, core, row // lines, line]).astype(jnp.int32)
        rhs, lower, upper = right_side[:, 0], lower_inverse[:, 0], upper_inverse[:, 0]
        top = levels - 1
        piece = jax.ShapeDtypeStruct((share, size), jnp.float32)
        chunk = jax.ShapeDtypeStruct((share, size), jnp.bfloat16)
        turned = pltpu.VMEM((width, size), jnp.float32)

        def relay(blocks):
            shape = (blocks.shape[0], group // CORES, size, size)
            same, cross = call(
                functools.partial(pack_kernel, size),
                [jax.ShapeDtypeStruct(shape, jnp.bfloat16)] * 2,
                [spot, blocks],
                scalars=1,
            )
            return [same] + [
                send(
                    cross if q % CORES else same,
                    lambda z, y, x, core, q=q: (z, y, x ^ (q // CORES), core ^ (q % CORES)),
                )
                for q in range(1, cols)
            ]

        def fold(picks, lefts, inverses, pieces):
            shape = jax.ShapeDtypeStruct((depths * wide, 2, size, size), jnp.bfloat16)
            return call(
                functools.partial(fold_kernel, picks, lefts, group, lines),
                [shape] * len(picks),
                [spot, pattern] + inverses + pieces,
                scalars=2,
            )

        def across(value):
            found = {0: value}
            for m in [m for m in range(2, depths)] + [1]:
                found[m] = send(value, lambda z, y, x, core, m=m: (z ^ m, y, x, core))
            return [found[m] for m in range(depths)]

        def meet(value, b):
            return send(
                value,
                lambda z, y, x, core: (z, core + CORES * ((y ^ b) // CORES), x, (y ^ b) % CORES),
            )

        def gather(partial_value):
            parts = [meet(partial_value, b) for b in range(lines)]
            sums = [sum(parts[CORES * j : CORES * (j + 1)]) for j in range(wide)]
            return jnp.concatenate(sums, axis=0).astype(jnp.bfloat16)

        def gather_first(value):
            parts = [meet(value, CORES * j) for j in range(wide)]
            return jnp.concatenate(parts, axis=0)

        def step(base, terms):
            operands = [base]
            for blocks, matrix in terms:
                operands += blocks + [matrix]
            return call(functools.partial(step_kernel, depths), piece, operands)

        first = call(
            functools.partial(first_kernel, share),
            chunk,
            [spot, rhs[0], lower[0]],
            scalars=1,
            scratch=[turned],
        )
        first, lower_blocks, upper_blocks = lax.optimization_barrier(
            (first, lower_blocks, upper_blocks)
        )
        fetched = {}
        met = gather_first(first)
        low_one = relay(lower_blocks[:1, 0])
        fetched[0] = across(met)
        low_rest = relay(lower_blocks[1:, 0])
        high_all = relay(upper_blocks[:, 0])

        panels = call(
            functools.partial(panel_kernel, share, levels),
            [piece] * (2 * levels - 2),
            [spot, first, rhs, lower, upper],
            scalars=1,
            scratch=[turned],
        )
        ends, starts = panels[:levels], [None] + list(panels[levels:])

        forward, backward = {}, {}
        for later in range(1, levels):
            pieces = low_one if later == 1 else low_rest
            offset = 0 if later == 1 else 1
            pairs = [pair_index(later, e) for e in range(later)]
            picks = tuple((p - offset, p, 0, False) for p in pairs)
            if later < top:
                found = fold(picks, ("one",), [lower[later], lower[later]], pieces)
                forward.update(zip(pairs, found))
            found = fold(picks, ("both",), [upper[later], lower[later]], pieces)
            backward.update(zip(pairs, found))
        upward = {}
        for earlier in reversed(range(top)):
            pairs = [pair_index(a, earlier) for a in range(earlier + 1, levels)]
            picks = tuple((p, p, 0, True) for p in pairs)
            found = fold(picks, ("one",), [upper[earlier], upper[earlier]], high_all)
            upward.update(zip(pairs, found))

        for level in range(1, top):
            value = starts[level]
            for earlier in range(level):
                value = step(value, [(fetched[earlier], forward[pair_index(level, earlier)])])
            fetched[level] = across(gather(value))

        back, solved = {}, {}
        for level in reversed(range(levels)):
            value = ends[level]
            for earlier in range(level):
                value = step(value, [(fetched[earlier], backward[pair_index(level, earlier)])])
            for later in reversed(range(level + 1, levels)):
                value = step(value, [(back[later], upward[pair_index(later, level)])])
            if level > 0:
                solved[level] = gather(value)
                back[level] = across(solved[level])
        sums = [
            value
            if b == 0 and other == 0
            else send(value, lambda z, y, x, core, b=b, o=other: (z, y, x ^ b, core ^ o))
            for b in range(chips)
            for other in range(CORES)
        ]
        held = jnp.concatenate([solved[k][:share] for k in range(1, levels)], axis=0)
        moved = send(
            held,
            lambda z, y, x, core: (z, y, x, 1 - core) if y % CORES != core else None,
        )
        mine = jnp.where(line % CORES == core, held, moved)
        results = [mine] + [
            send(mine, lambda z, y, x, core, b=b: (z, y, x ^ b, core)) for b in range(1, chips)
        ]
        out = call(
            functools.partial(last_kernel, levels, chips),
            jax.ShapeDtypeStruct((levels, size, width), jnp.bfloat16),
            [spot] + results + sums,
            scalars=1,
            scratch=[turned],
        )
        return out[:, None]

    return body


def solution(mesh):
    placed = (
        P(None, "prow", None, None),
        P(None, "prow", None, "pcol"),
        P(None, "prow", None, "pcol"),
        P(None, "prow", None, None),
        P(None, "prow", None, None),
        P(),
    )
    return jax.shard_map(
        make_body(mesh.shape["prow"], mesh.shape["pcol"]),
        mesh=mesh,
        in_specs=placed,
        out_specs=P(None, "prow", None, None),
        check_vma=False,
    )
```

```python
import functools

import jax
import jax.numpy as jnp
from jax import lax
from jax.experimental import pallas as pl
from jax.experimental.pallas import tpu as pltpu
from jax.sharding import PartitionSpec as P

CORES = 2
ROW, CHIP, CORE, DEPTH, LINE = range(5)
VMEM_BYTES = 40 * 1024 * 1024


def pair_index(later, earlier):
    return later * (later - 1) // 2 + earlier


def exact(left, right):
    return jnp.dot(left, right, preferred_element_type=jnp.float32)


def split(values, count):
    parts = []
    for _ in range(count):
        part = values.astype(jnp.bfloat16)
        parts.append(part)
        values = values - part.astype(jnp.float32)
    return parts


def level_of(array, level):
    shape = (1,) + array.shape[1:]
    return array, pl.BlockSpec(shape, lambda step: (level,) + (0,) * (len(shape) - 1))


def call(kernel, shapes, operands, scalars=0, scratch=()):
    arrays, specs = [], []
    for place, operand in enumerate(operands):
        if isinstance(operand, tuple):
            array, spec = operand
        else:
            array = operand
            space = pltpu.SMEM if place < scalars else pltpu.VMEM
            spec = pl.BlockSpec(memory_space=space)
        arrays.append(array)
        specs.append(spec)
    return pl.pallas_call(
        kernel,
        grid=(1,),
        out_shape=shapes,
        in_specs=specs,
        out_specs=jax.tree.map(lambda _: pl.BlockSpec(memory_space=pltpu.VMEM), shapes),
        scratch_shapes=list(scratch),
        compiler_params=pltpu.CompilerParams(vmem_limit_bytes=VMEM_BYTES),
    )(*arrays)


def share_of(values, turned, share, chip):
    turned[...] = values.T
    return turned[pl.ds(pl.multiple_of(chip * share, share), share), :]


def first_kernel(share, spot, rhs, inverse, out, turned):
    value = exact(inverse[0, 0], rhs[0, 0])
    out[...] = share_of(value, turned, share, spot[CHIP]).astype(out.dtype)


def panel_kernel(share, levels, spot, first, rhs, lower, upper, *rest):
    outs, turned = rest[:-1], rest[-1]
    chip = spot[CHIP]
    mine = spot[CORE] == 0
    value = lax.dot_general(
        first[...], upper[0, 0], (((1,), (1,)), ((), ())), preferred_element_type=jnp.float32
    )
    outs[0][...] = jnp.where(mine, value, 0.0)
    for level in range(1, levels):
        start = exact(lower[level, 0], rhs[level, 0])
        end = sum(exact(upper[level, 0], part) for part in split(start, 3))
        outs[level][...] = jnp.where(mine, share_of(end, turned, share, chip), 0.0)
        if level < levels - 1:
            value = share_of(start, turned, share, chip)
            outs[levels + level - 1][...] = jnp.where(mine, value, 0.0)


def fold_kernel(picks, left_count, spot, pattern, *refs):
    outs = refs[-len(picks) :]
    pieces = refs[left_count : -len(picks)]
    row, chip, core = spot[ROW], spot[CHIP], spot[CORE]
    depth, line = spot[DEPTH], spot[LINE]
    size = outs[0].shape[-1]
    group = pieces[0].shape[-1] // size
    if left_count == 1:
        sides = [refs[0][0, 0]]
    else:
        sides = split(exact(refs[0][0, 0], refs[1][0, 0]), 3)
    for index, piece in enumerate(pieces):
        turn = index ^ chip
        deep = depth ^ (core * len(pieces) + turn)
        for across in range(group):
            block = deep * group + across
            slot = (across ^ line) * len(pieces) + turn
            columns = slice(across * size, (across + 1) * size)
            for pick, out in zip(picks, outs):
                where, pair, is_upper = pick
                keep = pattern[pair, block, row] if is_upper else pattern[pair, row, block]
                matrix = piece[where, 0, :, columns]
                matrix = jnp.where(keep > 0, matrix, jnp.zeros_like(matrix))
                folded = sum(exact(part, matrix) for part in sides).T
                for low, part in enumerate(split(folded, 2)):
                    out[slot, low] = part


def step_kernel(lines, base, *refs):
    out = refs[-1]
    refs = refs[:-1]
    total = base[...]
    share = total.shape[0]
    for term in range(len(refs) // (lines + 1)):
        stacks = refs[term * (lines + 1) :][:lines]
        matrix = refs[term * (lines + 1) + lines]
        each = matrix.shape[0] // lines
        for line in range(lines):
            for index in range(each):
                block = stacks[line][index * share : (index + 1) * share, :]
                for low in range(2):
                    total = total - exact(block, matrix[line * each + index, low])
    out[...] = total


def last_kernel(levels, chips, spot, *refs):
    out, turned = refs[-2], refs[-1]
    share = turned.shape[0] // chips
    chip = spot[CHIP]
    at = [pl.ds(pl.multiple_of((chip ^ b) * share, share), share) for b in range(chips)]
    for level in range(levels):
        for b in range(chips):
            if level > 0:
                part = refs[b][(level - 1) * share : level * share, :]
            else:
                part = refs[chips + b][...]
            turned[at[b], :] = part.astype(jnp.float32)
        out[level, 0] = turned[...].T.astype(out.dtype)


def make_body(rows, cols):
    chips = cols // CORES
    lines = chips
    depths = rows // lines
    near = depths // CORES
    assert near == chips

    def send(value, source_of):
        pairs = []
        for z in range(depths):
            for y in range(lines):
                for x in range(chips):
                    for core in range(CORES):
                        source = source_of(z, y, x, core)
                        if source is None:
                            continue
                        a, b, c, d = source
                        pairs.append(
                            (
                                (a * lines + b) * cols + c * CORES + d,
                                (z * lines + y) * cols + x * CORES + core,
                            )
                        )
        return lax.ppermute(value, ("prow", "pcol"), pairs)

    def after(value, *signs):
        return lax.optimization_barrier((value,) + signs)[0]

    def body(right_side, lower_blocks, upper_blocks, lower_inverse, upper_inverse, pattern):
        levels, _, size, width = right_side.shape
        share = width // chips
        row = lax.axis_index("prow")
        col = lax.axis_index("pcol")
        line, core = row % lines, col % CORES
        spot = jnp.stack([row, col // CORES, core, row // lines, line]).astype(jnp.int32)
        top = levels - 1
        piece = jax.ShapeDtypeStruct((share, size), jnp.float32)
        chunk = jax.ShapeDtypeStruct((share, size), jnp.bfloat16)
        turned = pltpu.VMEM((width, size), jnp.float32)

        def relay(blocks):
            def source(z, y, x, core, i):
                place = z ^ (core * near + (i ^ x))
                return z, y, place // CORES, place % CORES

            return [send(blocks, functools.partial(source, i=i)) for i in range(near)]

        def fold(picks, inverses, pieces):
            shape = jax.ShapeDtypeStruct((near * lines, 2, size, size), jnp.bfloat16)
            return call(
                functools.partial(fold_kernel, picks, len(inverses)),
                [shape] * len(picks),
                [spot, pattern] + inverses + pieces,
                scalars=2,
            )

        def deep(value):
            parts = []
            for t in range(near):

                def source(z, y, x, core, t=t):
                    m = core * near + t
                    return (z ^ m, y, x, core) if m else None

                parts.append(send(value, source))
            parts[0] = jnp.where(core == 0, value, parts[0])
            return jnp.concatenate(parts, axis=0)

        def wide(stack):
            return [stack] + [
                send(stack, lambda z, y, x, core, e=e: (z, y ^ e, x, core)) for e in range(1, lines)
            ]

        def settle(partial_value):
            other = send(partial_value, lambda z, y, x, core: (z, y, x, 1 - core))
            return (partial_value + other).astype(jnp.bfloat16)

        def collect(value):
            return [value] + [
                send(value, lambda z, y, x, core, b=b: (z, y, x ^ b, core)) for b in range(1, chips)
            ]

        def step(base, terms):
            operands = [base]
            for stacks, matrix in terms:
                operands += stacks + [matrix]
            return call(functools.partial(step_kernel, lines), piece, operands)

        first = call(
            functools.partial(first_kernel, share),
            chunk,
            [spot, level_of(right_side, 0), level_of(lower_inverse, 0)],
            scalars=1,
            scratch=[turned],
        )
        fetched, back, solved = {}, {}, {}
        stack = deep(first)
        moved = {("low", 1): relay(lower_blocks[:1])}
        fetched[0] = wide(stack)
        moved["low", 2] = relay(after(lower_blocks, stack)[1:])
        last_pair = pair_index(top, top - 1)

        panels = call(
            functools.partial(panel_kernel, share, levels),
            [piece] * (2 * levels - 2),
            [spot, first, right_side, lower_inverse, upper_inverse],
            scalars=1,
            scratch=[turned],
        )
        ends, starts = panels[:levels], [None] + list(panels[levels:])

        def fold_lower(later, pieces, both):
            offset = 0 if later == 1 else 1
            pairs = [pair_index(later, e) for e in range(later)]
            picks = tuple((p - offset, p, False) for p in pairs)
            inverses = [level_of(lower_inverse, later)]
            if both:
                inverses = [level_of(upper_inverse, later)] + inverses
            return dict(zip(pairs, fold(picks, inverses, pieces)))

        def fold_upper(earlier, pieces, pairs, offset):
            picks = tuple((p - offset, p, True) for p in pairs)
            inverses = [level_of(upper_inverse, earlier)]
            return dict(zip(pairs, fold(picks, inverses, pieces)))

        forward, backward, upward = {}, {}, {}
        for level in range(1, top):
            forward.update(fold_lower(level, moved["low", min(level, 2)], False))
            value = starts[level]
            for earlier in range(level):
                value = step(value, [(fetched[earlier], forward[pair_index(level, earlier)])])
            found = settle(value)
            stack = deep(found)
            if level == 1:
                moved["high", 0] = relay(after(upper_blocks, found)[last_pair:])
                moved["high", 1] = relay(after(upper_blocks, stack)[:last_pair])
            fetched[level] = wide(stack)
        for level in range(1, levels):
            backward.update(fold_lower(level, moved["low", min(level, 2)], True))

        for level in reversed(range(levels)):
            value = ends[level]
            for earlier in range(level):
                value = step(value, [(fetched[earlier], backward[pair_index(level, earlier)])])
            for later in reversed(range(level + 1, levels)):
                pair = pair_index(later, level)
                if pair == last_pair:
                    upward.update(fold_upper(level, moved["high", 0], [pair], last_pair))
                else:
                    upward.update(fold_upper(level, moved["high", 1], [pair], 0))
                value = step(value, [(back[later], upward[pair])])
            solved[level] = settle(value)
            if level > 0:
                stack = deep(solved[level])
                back[level] = wide(stack)
        results = collect(jnp.concatenate([solved[k] for k in range(1, levels)], axis=0))
        results += collect(solved[0])
        return call(
            functools.partial(last_kernel, levels, chips),
            jax.ShapeDtypeStruct((levels, 1, size, width), jnp.bfloat16),
            [spot] + results,
            scalars=1,
            scratch=[turned],
        )

    return body


def solution(mesh):
    placed = (
        P(None, "prow", None, None),
        P(None, "prow", None, "pcol"),
        P(None, "prow", None, "pcol"),
        P(None, "prow", None, None),
        P(None, "prow", None, None),
        P(),
    )
    return jax.shard_map(
        make_body(mesh.shape["prow"], mesh.shape["pcol"]),
        mesh=mesh,
        in_specs=placed,
        out_specs=P(None, "prow", None, None),
        check_vma=False,
    )
```

```python
import functools

import jax
import jax.numpy as jnp
from jax import lax
from jax.experimental import pallas as pl
from jax.experimental.pallas import tpu as pltpu
from jax.sharding import PartitionSpec as P

CORES = 2
ROW, CHIP, CORE, DEPTH, LINE = range(5)
VMEM_BYTES = 40 * 1024 * 1024
FULL_BYTES = 58 * 1024 * 1024


def pair_index(later, earlier):
    return later * (later - 1) // 2 + earlier


def exact(left, right):
    return jnp.dot(left, right, preferred_element_type=jnp.float32)


def split(values, count):
    parts = []
    for _ in range(count):
        part = values.astype(jnp.bfloat16)
        parts.append(part)
        values = values - part.astype(jnp.float32)
    return parts


def level_of(array, level):
    shape = (1,) + array.shape[1:]
    return array, pl.BlockSpec(shape, lambda step: (level,) + (0,) * (len(shape) - 1))


def call(kernel, shapes, operands, scalars=0, scratch=(), room=VMEM_BYTES):
    arrays, specs = [], []
    for place, operand in enumerate(operands):
        if isinstance(operand, tuple):
            array, spec = operand
        else:
            array = operand
            space = pltpu.SMEM if place < scalars else pltpu.VMEM
            spec = pl.BlockSpec(memory_space=space)
        arrays.append(array)
        specs.append(spec)
    return pl.pallas_call(
        kernel,
        grid=(1,),
        out_shape=shapes,
        in_specs=specs,
        out_specs=jax.tree.map(lambda _: pl.BlockSpec(memory_space=pltpu.VMEM), shapes),
        scratch_shapes=list(scratch),
        compiler_params=pltpu.CompilerParams(vmem_limit_bytes=room),
    )(*arrays)


def share_of(values, turned, share, chip):
    turned[...] = values.T
    return turned[pl.ds(pl.multiple_of(chip * share, share), share), :]


def first_kernel(share, spot, rhs, inverse, out, turned):
    value = exact(inverse[0, 0], rhs[0, 0])
    out[...] = share_of(value, turned, share, spot[CHIP]).astype(out.dtype)


def panel_kernel(share, levels, spot, first, rhs, lower, upper, *rest):
    outs, turned = rest[:-1], rest[-1]
    chip = spot[CHIP]
    mine = spot[CORE] == 0
    value = lax.dot_general(
        first[...], upper[0, 0], (((1,), (1,)), ((), ())), preferred_element_type=jnp.float32
    )
    outs[0][...] = jnp.where(mine, value, 0.0)
    for level in range(1, levels):
        start = exact(lower[level, 0], rhs[level, 0])
        end = sum(exact(upper[level, 0], part) for part in split(start, 3))
        outs[level][...] = jnp.where(mine, share_of(end, turned, share, chip), 0.0)
        if level < levels - 1:
            value = share_of(start, turned, share, chip)
            outs[levels + level - 1][...] = jnp.where(mine, value, 0.0)


def fold_kernel(picks, left_count, spot, pattern, *refs):
    outs = refs[-len(picks) :]
    pieces = refs[left_count : -len(picks)]
    row, chip, core = spot[ROW], spot[CHIP], spot[CORE]
    depth, line = spot[DEPTH], spot[LINE]
    size = outs[0].shape[-1]
    group = pieces[0].shape[-1] // size
    if left_count == 1:
        sides = [refs[0][0, 0]]
    else:
        sides = split(exact(refs[0][0, 0], refs[1][0, 0]), 3)
    for index, piece in enumerate(pieces):
        deep = (chip ^ index) * CORES + core
        turn = (deep // CORES) ^ (depth // CORES)
        for across in range(group):
            block = deep * group + across
            slot = (across ^ line) * len(pieces) + turn
            columns = slice(across * size, (across + 1) * size)
            for pick, out in zip(picks, outs):
                here, there, pair, is_upper = pick
                keep = pattern[pair, block, row] if is_upper else pattern[pair, row, block]
                matrix = piece[there if index else here, 0, :, columns]
                matrix = jnp.where(keep > 0, matrix, jnp.zeros_like(matrix))
                folded = sum(exact(part, matrix) for part in sides).T
                for low, part in enumerate(split(folded, 2)):
                    out[slot, low] = part


def step_kernel(lines, base, *refs):
    out = refs[-1]
    refs = refs[:-1]
    total = base[...]
    share = total.shape[0]
    for term in range(len(refs) // (lines + 1)):
        stacks = refs[term * (lines + 1) :][:lines]
        matrix = refs[term * (lines + 1) + lines]
        each = matrix.shape[0] // lines
        for line in range(lines):
            for index in range(each):
                block = stacks[line][index * share : (index + 1) * share, :]
                for low in range(2):
                    total = total - exact(block, matrix[line * each + index, low])
    out[...] = total


def last_kernel(levels, chips, spot, *refs):
    out, turned = refs[-2], refs[-1]
    share = turned.shape[0] // chips
    chip = spot[CHIP]
    at = [pl.ds(pl.multiple_of((chip ^ b) * share, share), share) for b in range(chips)]
    for level in range(levels):
        for b in range(chips):
            if level > 0:
                part = refs[b][(level - 1) * share : level * share, :]
            else:
                part = refs[chips + b][...]
            turned[at[b], :] = part.astype(jnp.float32)
        out[level, 0] = turned[...].T.astype(out.dtype)


def make_body(rows, cols):
    chips = cols // CORES
    lines = chips
    depths = rows // lines
    near = depths // CORES
    assert near == chips

    def send(value, source_of):
        pairs = []
        for z in range(depths):
            for y in range(lines):
                for x in range(chips):
                    for core in range(CORES):
                        source = source_of(z, y, x, core)
                        if source is None:
                            continue
                        a, b, c, d = source
                        pairs.append(
                            (
                                (a * lines + b) * cols + c * CORES + d,
                                (z * lines + y) * cols + x * CORES + core,
                            )
                        )
        return lax.ppermute(value, ("prow", "pcol"), pairs)

    def after(value, *signs):
        return lax.optimization_barrier((value,) + signs)[0]

    def body(right_side, lower_blocks, upper_blocks, lower_inverse, upper_inverse, pattern):
        levels, _, size, width = right_side.shape
        share = width // chips
        row = lax.axis_index("prow")
        col = lax.axis_index("pcol")
        line, core = row % lines, col % CORES
        spot = jnp.stack([row, col // CORES, core, row // lines, line]).astype(jnp.int32)
        top = levels - 1
        piece = jax.ShapeDtypeStruct((share, size), jnp.float32)
        chunk = jax.ShapeDtypeStruct((share, size), jnp.bfloat16)
        turned = pltpu.VMEM((width, size), jnp.float32)

        def relay(blocks):
            return [
                send(blocks, lambda z, y, x, core, b=b: (z, y, x ^ b, core))
                for b in range(1, chips)
            ]

        def fold(picks, inverses, pieces):
            shape = jax.ShapeDtypeStruct((near * lines, 2, size, size), jnp.bfloat16)
            return call(
                functools.partial(fold_kernel, picks, len(inverses)),
                [shape] * len(picks),
                [spot, pattern] + inverses + pieces,
                scalars=2,
            )

        def deep(value):
            found = [value]
            for m in range(1, depths):

                def source(z, y, x, core, m=m):
                    return (z ^ m, y, x, core) if (z ^ m) % CORES == core else None

                found.append(send(value, source))
            parts = [
                jnp.where((row // lines) % CORES == core, found[m], found[m + 1])
                for m in range(0, depths, CORES)
            ]
            return jnp.concatenate(parts, axis=0)

        def wide(stack):
            return [stack] + [
                send(stack, lambda z, y, x, core, e=e: (z, y ^ e, x, core)) for e in range(1, lines)
            ]

        def settle(partial_value):
            other = send(partial_value, lambda z, y, x, core: (z, y, x, 1 - core))
            return (partial_value + other).astype(jnp.bfloat16)

        def collect(value):
            return [value] + [
                send(value, lambda z, y, x, core, b=b: (z, y, x ^ b, core)) for b in range(1, chips)
            ]

        def step(base, terms):
            operands = [base]
            for stacks, matrix in terms:
                operands += stacks + [matrix]
            return call(functools.partial(step_kernel, lines), piece, operands)

        near_one = lower_blocks[:1]
        moved = {("low", 1): relay(near_one)}
        first = call(
            functools.partial(first_kernel, share),
            chunk,
            [after(spot, near_one), level_of(right_side, 0), level_of(lower_inverse, 0)],
            scalars=1,
            scratch=[turned],
            room=FULL_BYTES,
        )
        moved["low", 2] = relay(lower_blocks[1:])
        moved["high", 0] = relay(upper_blocks[pair_index(levels - 1, levels - 2) :])
        moved["high", 1] = relay(upper_blocks[: pair_index(levels - 1, levels - 2)])
        fetched, back, solved = {}, {}, {}
        last_pair = pair_index(top, top - 1)
        fetched[0] = wide(deep(first))

        panels = call(
            functools.partial(panel_kernel, share, levels),
            [piece] * (2 * levels - 2),
            [spot, first, right_side, lower_inverse, upper_inverse],
            scalars=1,
            scratch=[turned],
        )
        ends, starts = panels[:levels], [None] + list(panels[levels:])

        def fold_lower(later, pieces, both):
            blocks = lower_blocks
            offset = 0 if later == 1 else 1
            pairs = [pair_index(later, e) for e in range(later)]
            picks = tuple((p, p - offset, p, False) for p in pairs)
            inverses = [level_of(lower_inverse, later)]
            if both:
                inverses = [level_of(upper_inverse, later)] + inverses
            return dict(zip(pairs, fold(picks, inverses, [blocks] + pieces)))

        def fold_upper(earlier, pieces, pairs, offset):
            blocks = upper_blocks
            picks = tuple((p, p - offset, p, True) for p in pairs)
            inverses = [level_of(upper_inverse, earlier)]
            return dict(zip(pairs, fold(picks, inverses, [blocks] + pieces)))

        forward, backward, upward = {}, {}, {}
        for level in range(1, top):
            forward.update(fold_lower(level, moved["low", min(level, 2)], False))
            value = starts[level]
            for earlier in range(level):
                value = step(value, [(fetched[earlier], forward[pair_index(level, earlier)])])
            found = settle(value)
            stack = deep(found)
            fetched[level] = wide(stack)
        for level in range(1, levels):
            backward.update(fold_lower(level, moved["low", min(level, 2)], True))

        for level in reversed(range(levels)):
            value = ends[level]
            for earlier in range(level):
                value = step(value, [(fetched[earlier], backward[pair_index(level, earlier)])])
            for later in reversed(range(level + 1, levels)):
                pair = pair_index(later, level)
                if pair == last_pair:
                    upward.update(fold_upper(level, moved["high", 0], [pair], last_pair))
                else:
                    upward.update(fold_upper(level, moved["high", 1], [pair], 0))
                value = step(value, [(back[later], upward[pair])])
            solved[level] = settle(value)
            if level > 0:
                stack = deep(solved[level])
                back[level] = wide(stack)
        results = collect(jnp.concatenate([solved[k] for k in range(1, levels)], axis=0))
        results += collect(solved[0])
        return call(
            functools.partial(last_kernel, levels, chips),
            jax.ShapeDtypeStruct((levels, 1, size, width), jnp.bfloat16),
            [spot] + results,
            scalars=1,
            scratch=[turned],
        )

    return body


def solution(mesh):
    placed = (
        P(None, "prow", None, None),
        P(None, "prow", None, "pcol"),
        P(None, "prow", None, "pcol"),
        P(None, "prow", None, None),
        P(None, "prow", None, None),
        P(),
    )
    return jax.shard_map(
        make_body(mesh.shape["prow"], mesh.shape["pcol"]),
        mesh=mesh,
        in_specs=placed,
        out_specs=P(None, "prow", None, None),
        check_vma=False,
    )
```

```python
import functools

import jax
import jax.numpy as jnp
from jax import lax
from jax.experimental import pallas as pl
from jax.experimental.pallas import tpu as pltpu
from jax.sharding import PartitionSpec as P

CORES = 2
ROW, CHIP, CORE, DEPTH, LINE = range(5)
VMEM_BYTES = 40 * 1024 * 1024
FULL_BYTES = 58 * 1024 * 1024


def pair_index(later, earlier):
    return later * (later - 1) // 2 + earlier


def exact(left, right):
    return jnp.dot(left, right, preferred_element_type=jnp.float32)


def split(values, count):
    parts = []
    for _ in range(count):
        part = values.astype(jnp.bfloat16)
        parts.append(part)
        values = values - part.astype(jnp.float32)
    return parts


def level_of(array, level):
    shape = (1,) + array.shape[1:]
    return array, pl.BlockSpec(shape, lambda step: (level,) + (0,) * (len(shape) - 1))


def call(kernel, shapes, operands, scalars=0, scratch=(), room=VMEM_BYTES):
    arrays, specs = [], []
    for place, operand in enumerate(operands):
        if isinstance(operand, tuple):
            array, spec = operand
        else:
            array = operand
            space = pltpu.SMEM if place < scalars else pltpu.VMEM
            spec = pl.BlockSpec(memory_space=space)
        arrays.append(array)
        specs.append(spec)
    return pl.pallas_call(
        kernel,
        grid=(1,),
        out_shape=shapes,
        in_specs=specs,
        out_specs=jax.tree.map(lambda _: pl.BlockSpec(memory_space=pltpu.VMEM), shapes),
        scratch_shapes=list(scratch),
        compiler_params=pltpu.CompilerParams(vmem_limit_bytes=room),
    )(*arrays)


def share_of(values, turned, share, chip):
    turned[...] = values.T
    return turned[pl.ds(pl.multiple_of(chip * share, share), share), :]


def first_kernel(share, spot, rhs, inverse, out, turned):
    value = exact(inverse[0, 0], rhs[0, 0])
    out[...] = share_of(value, turned, share, spot[CHIP]).astype(out.dtype)


def panel_kernel(share, levels, spot, first, rhs, lower, upper, *rest):
    outs, turned = rest[:-1], rest[-1]
    chip = spot[CHIP]
    mine = spot[CORE] == 0
    value = lax.dot_general(
        first[...], upper[0, 0], (((1,), (1,)), ((), ())), preferred_element_type=jnp.float32
    )
    outs[0][...] = jnp.where(mine, value, 0.0)
    for level in range(1, levels):
        start = exact(lower[level, 0], rhs[level, 0])
        end = sum(exact(upper[level, 0], part) for part in split(start, 3))
        outs[level][...] = jnp.where(mine, share_of(end, turned, share, chip), 0.0)
        if level < levels - 1:
            value = share_of(start, turned, share, chip)
            outs[levels + level - 1][...] = jnp.where(mine, value, 0.0)


def fold_kernel(picks, left_count, spot, pattern, *refs):
    outs = refs[-len(picks) :]
    pieces = refs[left_count : -len(picks)]
    row, chip, core = spot[ROW], spot[CHIP], spot[CORE]
    depth, line = spot[DEPTH], spot[LINE]
    size = outs[0].shape[-1]
    group = pieces[0].shape[-1] // size
    if left_count == 1:
        sides = [refs[0][0, 0]]
    else:
        sides = split(exact(refs[0][0, 0], refs[1][0, 0]), 3)
    for index, piece in enumerate(pieces):
        deep = (chip ^ index) * CORES + core
        turn = (deep // CORES) ^ (depth // CORES)
        for across in range(group):
            block = deep * group + across
            slot = (across ^ line) * len(pieces) + turn
            columns = slice(across * size, (across + 1) * size)
            for pick, out in zip(picks, outs):
                here, there, pair, is_upper = pick
                keep = pattern[pair, block, row] if is_upper else pattern[pair, row, block]
                matrix = piece[there if index else here, 0, :, columns]
                matrix = jnp.where(keep > 0, matrix, jnp.zeros_like(matrix))
                folded = sum(exact(part, matrix) for part in sides).T
                for low, part in enumerate(split(folded, 2)):
                    out[slot, low] = part


def step_kernel(lines, base, *refs):
    out = refs[-1]
    refs = refs[:-1]
    total = base[...]
    share = total.shape[0]
    for term in range(len(refs) // (lines + 1)):
        stacks = refs[term * (lines + 1) :][:lines]
        matrix = refs[term * (lines + 1) + lines]
        each = matrix.shape[0] // lines
        for line in range(lines):
            for index in range(each):
                block = stacks[line][index * share : (index + 1) * share, :]
                for low in range(2):
                    total = total - exact(block, matrix[line * each + index, low])
    out[...] = total


def last_kernel(levels, chips, spot, *refs):
    out, turned = refs[-2], refs[-1]
    share = turned.shape[0] // chips
    chip = spot[CHIP]
    at = [pl.ds(pl.multiple_of((chip ^ b) * share, share), share) for b in range(chips)]
    for level in range(levels):
        for b in range(chips):
            if level > 0:
                part = refs[b][(level - 1) * share : level * share, :]
            else:
                part = refs[chips + b][...]
            turned[at[b], :] = part.astype(jnp.float32)
        out[level, 0] = turned[...].T.astype(out.dtype)


def make_body(rows, cols):
    chips = cols // CORES
    lines = chips
    depths = rows // lines
    near = depths // CORES
    assert near == chips

    def send(value, source_of):
        pairs = []
        for z in range(depths):
            for y in range(lines):
                for x in range(chips):
                    for core in range(CORES):
                        a, b, c, d = source_of(z, y, x, core)
                        pairs.append(
                            (
                                (a * lines + b) * cols + c * CORES + d,
                                (z * lines + y) * cols + x * CORES + core,
                            )
                        )
        return lax.ppermute(value, ("prow", "pcol"), pairs)

    def after(value, *signs):
        return lax.optimization_barrier((value,) + signs)[0]

    def body(right_side, lower_blocks, upper_blocks, lower_inverse, upper_inverse, pattern):
        levels, _, size, width = right_side.shape
        share = width // chips
        row = lax.axis_index("prow")
        col = lax.axis_index("pcol")
        line, core = row % lines, col % CORES
        spot = jnp.stack([row, col // CORES, core, row // lines, line]).astype(jnp.int32)
        top = levels - 1
        piece = jax.ShapeDtypeStruct((share, size), jnp.float32)
        chunk = jax.ShapeDtypeStruct((share, size), jnp.bfloat16)
        turned = pltpu.VMEM((width, size), jnp.float32)

        def relay(blocks):
            return [
                send(blocks, lambda z, y, x, core, b=b: (z, y, x ^ b, core))
                for b in range(1, chips)
            ]

        def fold(picks, inverses, pieces):
            shape = jax.ShapeDtypeStruct((near * lines, 2, size, size), jnp.bfloat16)
            return call(
                functools.partial(fold_kernel, picks, len(inverses)),
                [shape] * len(picks),
                [spot, pattern] + inverses + pieces,
                scalars=2,
            )

        def deep(value):
            found = [value]
            for m in range(1, depths):
                found.append(send(value, lambda z, y, x, core, m=m: (z ^ m, y, x, core)))
            parts = [
                jnp.where((row // lines) % CORES == core, found[m], found[m + 1])
                for m in range(0, depths, CORES)
            ]
            return jnp.concatenate(parts, axis=0)

        def wide(stack):
            return [stack] + [
                send(stack, lambda z, y, x, core, e=e: (z, y ^ e, x, core)) for e in range(1, lines)
            ]

        def settle(partial_value):
            other = send(partial_value, lambda z, y, x, core: (z, y, x, 1 - core))
            return (partial_value + other).astype(jnp.bfloat16)

        def collect(value):
            return [value] + [
                send(value, lambda z, y, x, core, b=b: (z, y, x ^ b, core)) for b in range(1, chips)
            ]

        def step(base, terms):
            operands = [base]
            for stacks, matrix in terms:
                operands += stacks + [matrix]
            return call(functools.partial(step_kernel, lines), piece, operands)

        near_one = lower_blocks[:1]
        moved = {("low", 1): relay(near_one)}
        first = call(
            functools.partial(first_kernel, share),
            chunk,
            [after(spot, near_one), level_of(right_side, 0), level_of(lower_inverse, 0)],
            scalars=1,
            scratch=[turned],
            room=FULL_BYTES,
        )
        moved["low", 2] = relay(lower_blocks[1:])
        moved["high", 0] = relay(upper_blocks[pair_index(levels - 1, levels - 2) :])
        moved["high", 1] = relay(upper_blocks[: pair_index(levels - 1, levels - 2)])
        fetched, back, solved = {}, {}, {}
        last_pair = pair_index(top, top - 1)
        fetched[0] = wide(deep(first))

        panels = call(
            functools.partial(panel_kernel, share, levels),
            [piece] * (2 * levels - 2),
            [spot, first, right_side, lower_inverse, upper_inverse],
            scalars=1,
            scratch=[turned],
        )
        ends, starts = panels[:levels], [None] + list(panels[levels:])

        def fold_lower(later, pieces, both):
            blocks = lower_blocks
            offset = 0 if later == 1 else 1
            pairs = [pair_index(later, e) for e in range(later)]
            picks = tuple((p, p - offset, p, False) for p in pairs)
            inverses = [level_of(lower_inverse, later)]
            if both:
                inverses = [level_of(upper_inverse, later)] + inverses
            return dict(zip(pairs, fold(picks, inverses, [blocks] + pieces)))

        def fold_upper(earlier, pieces, pairs, offset):
            blocks = upper_blocks
            picks = tuple((p, p - offset, p, True) for p in pairs)
            inverses = [level_of(upper_inverse, earlier)]
            return dict(zip(pairs, fold(picks, inverses, [blocks] + pieces)))

        forward, backward, upward = {}, {}, {}
        for level in range(1, top):
            forward.update(fold_lower(level, moved["low", min(level, 2)], False))
            value = starts[level]
            for earlier in range(level):
                value = step(value, [(fetched[earlier], forward[pair_index(level, earlier)])])
            found = settle(value)
            stack = deep(found)
            fetched[level] = wide(stack)
        for level in range(1, levels):
            backward.update(fold_lower(level, moved["low", min(level, 2)], True))

        for level in reversed(range(levels)):
            value = ends[level]
            if level == 0:
                results = collect(jnp.concatenate([solved[k] for k in range(1, levels)], axis=0))
                value = after(value, *results)
            for earlier in range(level):
                value = step(value, [(fetched[earlier], backward[pair_index(level, earlier)])])
            for later in reversed(range(level + 1, levels)):
                pair = pair_index(later, level)
                if pair == last_pair:
                    upward.update(fold_upper(level, moved["high", 0], [pair], last_pair))
                else:
                    upward.update(fold_upper(level, moved["high", 1], [pair], 0))
                value = step(value, [(back[later], upward[pair])])
            solved[level] = settle(value)
            if level > 0:
                stack = deep(solved[level])
                back[level] = wide(stack)
        results += collect(solved[0])
        return call(
            functools.partial(last_kernel, levels, chips),
            jax.ShapeDtypeStruct((levels, 1, size, width), jnp.bfloat16),
            [spot] + results,
            scalars=1,
            scratch=[turned],
        )

    return body


def solution(mesh):
    placed = (
        P(None, "prow", None, None),
        P(None, "prow", None, "pcol"),
        P(None, "prow", None, "pcol"),
        P(None, "prow", None, None),
        P(None, "prow", None, None),
        P(),
    )
    return jax.shard_map(
        make_body(mesh.shape["prow"], mesh.shape["pcol"]),
        mesh=mesh,
        in_specs=placed,
        out_specs=P(None, "prow", None, None),
        check_vma=False,
    )
```

```python
import functools

import jax
import jax.numpy as jnp
from jax import lax
from jax.experimental import pallas as pl
from jax.experimental.pallas import tpu as pltpu
from jax.sharding import PartitionSpec as P

CORES = 2
ROW, CHIP, CORE, DEPTH, LINE = range(5)
VMEM_BYTES = 40 * 1024 * 1024
FULL_BYTES = 58 * 1024 * 1024


def pair_index(later, earlier):
    return later * (later - 1) // 2 + earlier


def exact(left, right):
    return jnp.dot(left, right, preferred_element_type=jnp.float32)


def split(values, count):
    parts = []
    for _ in range(count):
        part = values.astype(jnp.bfloat16)
        parts.append(part)
        values = values - part.astype(jnp.float32)
    return parts


def level_of(array, level):
    shape = (1,) + array.shape[1:]
    return array, pl.BlockSpec(shape, lambda step: (level,) + (0,) * (len(shape) - 1))


def call(kernel, shapes, operands, scalars=0, scratch=(), room=VMEM_BYTES):
    arrays, specs = [], []
    for place, operand in enumerate(operands):
        if isinstance(operand, tuple):
            array, spec = operand
        else:
            array = operand
            space = pltpu.SMEM if place < scalars else pltpu.VMEM
            spec = pl.BlockSpec(memory_space=space)
        arrays.append(array)
        specs.append(spec)
    return pl.pallas_call(
        kernel,
        grid=(1,),
        out_shape=shapes,
        in_specs=specs,
        out_specs=jax.tree.map(lambda _: pl.BlockSpec(memory_space=pltpu.VMEM), shapes),
        scratch_shapes=list(scratch),
        compiler_params=pltpu.CompilerParams(vmem_limit_bytes=room),
    )(*arrays)


def share_of(values, turned, share, chip):
    turned[...] = values.T
    return turned[pl.ds(pl.multiple_of(chip * share, share), share), :]


def first_kernel(share, spot, rhs, inverse, out, turned):
    value = exact(inverse[0, 0], rhs[0, 0])
    out[...] = share_of(value, turned, share, spot[CHIP]).astype(out.dtype)


def panel_kernel(share, levels, spot, first, rhs, lower, upper, *rest):
    outs, turned = rest[:-1], rest[-1]
    chip = spot[CHIP]
    mine = spot[CORE] == 0
    value = lax.dot_general(
        first[...], upper[0, 0], (((1,), (1,)), ((), ())), preferred_element_type=jnp.float32
    )
    outs[0][...] = jnp.where(mine, value, 0.0)
    for level in range(1, levels):
        start = exact(lower[level, 0], rhs[level, 0])
        end = sum(exact(upper[level, 0], part) for part in split(start, 3))
        outs[level][...] = jnp.where(mine, share_of(end, turned, share, chip), 0.0)
        if level < levels - 1:
            value = share_of(start, turned, share, chip)
            outs[levels + level - 1][...] = jnp.where(mine, value, 0.0)


def fold_kernel(picks, left_count, spot, pattern, *refs):
    outs = refs[-len(picks) :]
    pieces = refs[left_count : -len(picks)]
    row, chip, core = spot[ROW], spot[CHIP], spot[CORE]
    depth, line = spot[DEPTH], spot[LINE]
    size = outs[0].shape[-1]
    group = pieces[0].shape[-1] // size
    if left_count == 1:
        sides = [refs[0][0, 0]]
    else:
        sides = split(exact(refs[0][0, 0], refs[1][0, 0]), 3)
    for index, piece in enumerate(pieces):
        deep = (chip ^ index) * CORES + core
        turn = (deep // CORES) ^ (depth // CORES)
        for across in range(group):
            block = deep * group + across
            slot = (across ^ line) * len(pieces) + turn
            columns = slice(across * size, (across + 1) * size)
            for pick, out in zip(picks, outs):
                here, there, pair, is_upper = pick
                keep = pattern[pair, block, row] if is_upper else pattern[pair, row, block]
                matrix = piece[there if index else here, 0, :, columns]
                matrix = jnp.where(keep > 0, matrix, jnp.zeros_like(matrix))
                folded = sum(exact(part, matrix) for part in sides).T
                for low, part in enumerate(split(folded, 2)):
                    out[slot, low] = part


def step_kernel(lines, base, *refs):
    out = refs[-1]
    refs = refs[:-1]
    total = base[...]
    share = total.shape[0]
    for term in range(len(refs) // (lines + 1)):
        stacks = refs[term * (lines + 1) :][:lines]
        matrix = refs[term * (lines + 1) + lines]
        each = matrix.shape[0] // lines
        for line in range(lines):
            for index in range(each):
                block = stacks[line][index * share : (index + 1) * share, :]
                for low in range(2):
                    total = total - exact(block, matrix[line * each + index, low])
    out[...] = total


def last_kernel(levels, chips, spot, *refs):
    out, turned = refs[-2], refs[-1]
    share = turned.shape[0] // chips
    chip = spot[CHIP]
    at = [pl.ds(pl.multiple_of((chip ^ b) * share, share), share) for b in range(chips)]
    for level in range(levels):
        for b in range(chips):
            if level > 0:
                part = refs[b][(level - 1) * share : level * share, :]
            else:
                part = refs[chips + b][...]
            turned[at[b], :] = part.astype(jnp.float32)
        out[level, 0] = turned[...].T.astype(out.dtype)


def make_body(rows, cols):
    chips = cols // CORES
    lines = chips
    depths = rows // lines
    near = depths // CORES
    assert near == chips

    def send(value, source_of):
        pairs = []
        for z in range(depths):
            for y in range(lines):
                for x in range(chips):
                    for core in range(CORES):
                        a, b, c, d = source_of(z, y, x, core)
                        pairs.append(
                            (
                                (a * lines + b) * cols + c * CORES + d,
                                (z * lines + y) * cols + x * CORES + core,
                            )
                        )
        return lax.ppermute(value, ("prow", "pcol"), pairs)

    def after(value, *signs):
        return lax.optimization_barrier((value,) + signs)[0]

    def body(right_side, lower_blocks, upper_blocks, lower_inverse, upper_inverse, pattern):
        levels, _, size, width = right_side.shape
        share = width // chips
        row = lax.axis_index("prow")
        col = lax.axis_index("pcol")
        line, core = row % lines, col % CORES
        spot = jnp.stack([row, col // CORES, core, row // lines, line]).astype(jnp.int32)
        top = levels - 1
        piece = jax.ShapeDtypeStruct((share, size), jnp.float32)
        chunk = jax.ShapeDtypeStruct((share, size), jnp.bfloat16)
        turned = pltpu.VMEM((width, size), jnp.float32)

        def relay(blocks):
            return [
                send(blocks, lambda z, y, x, core, b=b: (z, y, x ^ b, core))
                for b in range(1, chips)
            ]

        def fold(picks, inverses, pieces):
            shape = jax.ShapeDtypeStruct((near * lines, 2, size, size), jnp.bfloat16)
            return call(
                functools.partial(fold_kernel, picks, len(inverses)),
                [shape] * len(picks),
                [spot, pattern] + inverses + pieces,
                scalars=2,
            )

        def deep(value):
            found = [value]
            for m in range(1, depths):
                found.append(send(value, lambda z, y, x, core, m=m: (z ^ m, y, x, core)))
            parts = [
                jnp.where((row // lines) % CORES == core, found[m], found[m + 1])
                for m in range(0, depths, CORES)
            ]
            return jnp.concatenate(parts, axis=0)

        def wide(stack):
            return [stack] + [
                send(stack, lambda z, y, x, core, e=e: (z, y ^ e, x, core)) for e in range(1, lines)
            ]

        def settle(partial_value):
            other = send(partial_value, lambda z, y, x, core: (z, y, x, 1 - core))
            return (partial_value + other).astype(jnp.bfloat16)

        def collect(value):
            return [value] + [
                send(value, lambda z, y, x, core, b=b: (z, y, x ^ b, core)) for b in range(1, chips)
            ]

        def step(base, terms):
            operands = [base]
            for stacks, matrix in terms:
                operands += stacks + [matrix]
            return call(functools.partial(step_kernel, lines), piece, operands)

        near_one = lower_blocks[:1]
        moved = {("low", 1): relay(near_one)}
        first = call(
            functools.partial(first_kernel, share),
            chunk,
            [spot, level_of(right_side, 0), level_of(lower_inverse, 0)],
            scalars=1,
            scratch=[turned],
            room=FULL_BYTES,
        )
        moved["low", 2] = relay(lower_blocks[1:])
        moved["high", 0] = relay(upper_blocks[pair_index(levels - 1, levels - 2) :])
        moved["high", 1] = relay(upper_blocks[: pair_index(levels - 1, levels - 2)])
        panels = call(
            functools.partial(panel_kernel, share, levels),
            [piece] * (2 * levels - 2),
            [spot, first, right_side, lower_inverse, upper_inverse],
            scalars=1,
            scratch=[turned],
        )
        ends, starts = panels[:levels], [None] + list(panels[levels:])

        def fold_lower(later, both):
            offset = 0 if later == 1 else 1
            pairs = [pair_index(later, e) for e in range(later)]
            picks = tuple((p, p - offset, p, False) for p in pairs)
            inverses = [level_of(lower_inverse, later)]
            if both:
                inverses = [level_of(upper_inverse, later)] + inverses
            pieces = [lower_blocks] + moved["low", min(later, 2)]
            return dict(zip(pairs, fold(picks, inverses, pieces)))

        def fold_upper(later, earlier):
            pair = pair_index(later, earlier)
            last = later == levels - 1 and earlier == levels - 2
            picks = ((pair, 0 if last else pair, pair, True),)
            pieces = [upper_blocks] + moved["high", 0 if last else 1]
            return fold(picks, [level_of(upper_inverse, earlier)], pieces)[0]

        fetched, back, solved = {}, {}, {}
        forward, backward, upward = {}, {}, {}
        forward.update(fold_lower(1, False))
        stack = after(deep(first), forward[0], *panels)
        fetched[0] = wide(stack)
        for level in range(1, top):
            if level > 1:
                forward.update(fold_lower(level, False))
            value = starts[level]
            for earlier in range(level):
                value = step(value, [(fetched[earlier], forward[pair_index(level, earlier)])])
            found = settle(value)
            if level == 1:
                found = after(found, *moved["low", 2])
                stack = deep(found)
                for later in range(1, levels):
                    backward.update(fold_lower(later, True))
                stack = after(stack, *backward.values(), *moved["high", 0])
            else:
                stack = deep(found)
            fetched[level] = wide(stack)

        for level in reversed(range(levels)):
            value = ends[level]
            if level == 0:
                results = collect(jnp.concatenate([solved[k] for k in range(1, levels)], axis=0))
                value = after(value, *results)
            for earlier in range(level):
                value = step(value, [(fetched[earlier], backward[pair_index(level, earlier)])])
            for later in reversed(range(level + 1, levels)):
                value = step(value, [(back[later], upward[later, level])])
            solved[level] = settle(value)
            if level > 0:
                found = solved[level]
                if level == top:
                    found = after(found, *moved["high", 1])
                folded = []
                for later in range(level, levels):
                    upward[later, level - 1] = fold_upper(later, level - 1)
                    folded.append(upward[later, level - 1])
                stack = after(deep(found), *folded)
                back[level] = wide(stack)
        results += collect(solved[0])
        return call(
            functools.partial(last_kernel, levels, chips),
            jax.ShapeDtypeStruct((levels, 1, size, width), jnp.bfloat16),
            [spot] + results,
            scalars=1,
            scratch=[turned],
        )

    return body


def solution(mesh):
    placed = (
        P(None, "prow", None, None),
        P(None, "prow", None, "pcol"),
        P(None, "prow", None, "pcol"),
        P(None, "prow", None, None),
        P(None, "prow", None, None),
        P(),
    )
    return jax.shard_map(
        make_body(mesh.shape["prow"], mesh.shape["pcol"]),
        mesh=mesh,
        in_specs=placed,
        out_specs=P(None, "prow", None, None),
        check_vma=False,
    )
```

```python
import functools

import jax
import jax.numpy as jnp
from jax import lax
from jax.experimental import pallas as pl
from jax.experimental.pallas import tpu as pltpu
from jax.sharding import PartitionSpec as P

CORES = 2
ROW, CHIP, CORE, DEPTH, LINE = range(5)
VMEM_BYTES = 40 * 1024 * 1024
FULL_BYTES = 58 * 1024 * 1024


def pair_index(later, earlier):
    return later * (later - 1) // 2 + earlier


def exact(left, right):
    return jnp.dot(left, right, preferred_element_type=jnp.float32)


def split(values, count):
    parts = []
    for _ in range(count):
        part = values.astype(jnp.bfloat16)
        parts.append(part)
        values = values - part.astype(jnp.float32)
    return parts


def level_of(array, level):
    shape = (1,) + array.shape[1:]
    return array, pl.BlockSpec(shape, lambda step: (level,) + (0,) * (len(shape) - 1))


def call(kernel, shapes, operands, scalars=0, scratch=(), room=VMEM_BYTES):
    arrays, specs = [], []
    for place, operand in enumerate(operands):
        if isinstance(operand, tuple):
            array, spec = operand
        else:
            array = operand
            space = pltpu.SMEM if place < scalars else pltpu.VMEM
            spec = pl.BlockSpec(memory_space=space)
        arrays.append(array)
        specs.append(spec)
    return pl.pallas_call(
        kernel,
        grid=(1,),
        out_shape=shapes,
        in_specs=specs,
        out_specs=jax.tree.map(lambda _: pl.BlockSpec(memory_space=pltpu.VMEM), shapes),
        scratch_shapes=list(scratch),
        compiler_params=pltpu.CompilerParams(vmem_limit_bytes=room),
    )(*arrays)


def share_of(values, turned, share, chip):
    turned[...] = values.T
    return turned[pl.ds(pl.multiple_of(chip * share, share), share), :]


def first_kernel(share, spot, rhs, inverse, out, turned):
    value = exact(inverse[0, 0], rhs[0, 0])
    out[...] = share_of(value, turned, share, spot[CHIP]).astype(out.dtype)


def panel_kernel(share, levels, spot, first, rhs, lower, upper, *rest):
    outs, turned = rest[:-1], rest[-1]
    chip = spot[CHIP]
    mine = spot[CORE] == 0
    value = lax.dot_general(
        first[...], upper[0, 0], (((1,), (1,)), ((), ())), preferred_element_type=jnp.float32
    )
    outs[0][...] = jnp.where(mine, value, 0.0)
    for level in range(1, levels):
        start = exact(lower[level, 0], rhs[level, 0])
        end = sum(exact(upper[level, 0], part) for part in split(start, 3))
        outs[level][...] = jnp.where(mine, share_of(end, turned, share, chip), 0.0)
        if level < levels - 1:
            value = share_of(start, turned, share, chip)
            outs[levels + level - 1][...] = jnp.where(mine, value, 0.0)


def fold_kernel(picks, left_count, spot, pattern, *refs):
    outs = refs[-len(picks) :]
    pieces = refs[left_count : -len(picks)]
    row, chip, core = spot[ROW], spot[CHIP], spot[CORE]
    depth, line = spot[DEPTH], spot[LINE]
    size = outs[0].shape[-1]
    group = pieces[0].shape[-1] // size
    if left_count == 1:
        sides = [refs[0][0, 0]]
    else:
        sides = split(exact(refs[0][0, 0], refs[1][0, 0]), 3)
    for index, piece in enumerate(pieces):
        deep = (chip ^ index) * CORES + core
        turn = (deep // CORES) ^ (depth // CORES)
        for across in range(group):
            block = deep * group + across
            slot = (across ^ line) * len(pieces) + turn
            columns = slice(across * size, (across + 1) * size)
            for pick, out in zip(picks, outs):
                pair, is_upper = pick
                keep = pattern[pair, block, row] if is_upper else pattern[pair, row, block]
                matrix = piece[pair, 0, :, columns]
                matrix = jnp.where(keep > 0, matrix, jnp.zeros_like(matrix))
                folded = sum(exact(part, matrix) for part in sides).T
                for low, part in enumerate(split(folded, 2)):
                    out[slot, low] = part


def step_kernel(lines, base, *refs):
    out = refs[-1]
    refs = refs[:-1]
    total = base[...]
    share = total.shape[0]
    for term in range(len(refs) // (lines + 1)):
        stacks = refs[term * (lines + 1) :][:lines]
        matrix = refs[term * (lines + 1) + lines]
        each = matrix.shape[0] // lines
        for line in range(lines):
            for index in range(each):
                block = stacks[line][index * share : (index + 1) * share, :]
                for low in range(2):
                    total = total - exact(block, matrix[line * each + index, low])
    out[...] = total


def last_kernel(levels, chips, spot, *refs):
    out, turned = refs[-2], refs[-1]
    share = turned.shape[0] // chips
    chip = spot[CHIP]
    at = [pl.ds(pl.multiple_of((chip ^ b) * share, share), share) for b in range(chips)]
    for level in range(levels):
        for b in range(chips):
            if level > 0:
                part = refs[b][(level - 1) * share : level * share, :]
            else:
                part = refs[chips + b][...]
            turned[at[b], :] = part.astype(jnp.float32)
        out[level, 0] = turned[...].T.astype(out.dtype)


def make_body(rows, cols):
    chips = cols // CORES
    lines = chips
    depths = rows // lines
    near = depths // CORES
    assert near == chips

    def send(value, source_of):
        pairs = []
        for z in range(depths):
            for y in range(lines):
                for x in range(chips):
                    for core in range(CORES):
                        a, b, c, d = source_of(z, y, x, core)
                        pairs.append(
                            (
                                (a * lines + b) * cols + c * CORES + d,
                                (z * lines + y) * cols + x * CORES + core,
                            )
                        )
        return lax.ppermute(value, ("prow", "pcol"), pairs)

    def after(value, *signs):
        return lax.optimization_barrier((value,) + signs)[0]

    def body(right_side, lower_blocks, upper_blocks, lower_inverse, upper_inverse, pattern):
        levels, _, size, width = right_side.shape
        share = width // chips
        row = lax.axis_index("prow")
        col = lax.axis_index("pcol")
        line, core = row % lines, col % CORES
        spot = jnp.stack([row, col // CORES, core, row // lines, line]).astype(jnp.int32)
        top = levels - 1
        piece = jax.ShapeDtypeStruct((share, size), jnp.float32)
        chunk = jax.ShapeDtypeStruct((share, size), jnp.bfloat16)
        turned = pltpu.VMEM((width, size), jnp.float32)

        def relay(blocks):
            return [
                send(blocks, lambda z, y, x, core, b=b: (z, y, x ^ b, core))
                for b in range(1, chips)
            ]

        def fold(picks, inverses, pieces, sign):
            shape = jax.ShapeDtypeStruct((near * lines, 2, size, size), jnp.bfloat16)
            return call(
                functools.partial(fold_kernel, picks, len(inverses)),
                [shape] * len(picks),
                [after(spot, sign), pattern] + inverses + pieces,
                scalars=2,
            )

        def deep(value, work=None):
            found = [value]
            for m in range(1, depths):
                found.append(send(value, lambda z, y, x, core, m=m: (z ^ m, y, x, core)))
            parts = [
                jnp.where((row // lines) % CORES == core, found[m], found[m + 1])
                for m in range(0, depths, CORES)
            ]
            stack = jnp.concatenate(parts, axis=0)
            return after(stack, *work(found[1])) if work else stack

        def wide(stack):
            return [stack] + [
                send(stack, lambda z, y, x, core, e=e: (z, y ^ e, x, core)) for e in range(1, lines)
            ]

        def settle(partial_value):
            other = send(partial_value, lambda z, y, x, core: (z, y, x, 1 - core))
            return (partial_value + other).astype(jnp.bfloat16)

        def collect(value):
            return [value] + [
                send(value, lambda z, y, x, core, b=b: (z, y, x ^ b, core)) for b in range(1, chips)
            ]

        def step(base, terms):
            operands = [base]
            for stacks, matrix in terms:
                operands += stacks + [matrix]
            return call(functools.partial(step_kernel, lines), piece, operands)

        first = call(
            functools.partial(first_kernel, share),
            chunk,
            [spot, level_of(right_side, 0), level_of(lower_inverse, 0)],
            scalars=1,
            scratch=[turned],
            room=FULL_BYTES,
        )
        panels = call(
            functools.partial(panel_kernel, share, levels),
            [piece] * (2 * levels - 2),
            [spot, first, right_side, lower_inverse, upper_inverse],
            scalars=1,
            scratch=[turned],
        )
        ends, starts = panels[:levels], [None] + list(panels[levels:])

        low_all = relay(lower_blocks)
        high_all = relay(after(upper_blocks, *low_all))

        def fold_lower(later, both, sign):
            pairs = [pair_index(later, e) for e in range(later)]
            picks = tuple((pair, False) for pair in pairs)
            inverses = [level_of(lower_inverse, later)]
            if both:
                inverses = [level_of(upper_inverse, later)] + inverses
            found = dict(zip(pairs, fold(picks, inverses, [lower_blocks] + low_all, sign)))
            (backward if both else forward).update(found)
            return list(found.values())

        def fold_upper(later, earlier, sign):
            picks = ((pair_index(later, earlier), True),)
            inverses = [level_of(upper_inverse, earlier)]
            found = fold(picks, inverses, [upper_blocks] + high_all, sign)[0]
            upward[later, earlier] = found
            return [found]

        fetched, back, solved = {}, {}, {}
        forward, backward, upward = {}, {}, {}
        stack = deep(first, lambda sign: panels)
        fetched[0] = wide(stack)
        for level in range(1, top):
            fold_lower(level, False, stack)
            value = starts[level]
            for earlier in range(level):
                value = step(value, [(fetched[earlier], forward[pair_index(level, earlier)])])
            stack = deep(settle(value), lambda sign: fold_lower(level, True, sign))
            fetched[level] = wide(stack)
        fold_lower(top, True, stack)

        for level in reversed(range(levels)):
            value = ends[level]
            if level == 0:
                results = collect(jnp.concatenate([solved[k] for k in range(1, levels)], axis=0))
                value = after(value, *results)
            for earlier in range(level):
                value = step(value, [(fetched[earlier], backward[pair_index(level, earlier)])])
            for later in reversed(range(level + 1, levels)):
                value = step(value, [(back[later], upward[later, level])])
            solved[level] = settle(value)
            if level > 0:
                work = None
                if level < top:
                    work = lambda sign: fold_upper(top, level - 1, sign)
                found = solved[level]
                if level == top:
                    found = after(found, *high_all)
                stack = deep(found, work)
                back[level] = wide(stack)
                for later in range(level, levels):
                    if (later, level - 1) not in upward:
                        fold_upper(later, level - 1, stack)
        results += collect(solved[0])
        return call(
            functools.partial(last_kernel, levels, chips),
            jax.ShapeDtypeStruct((levels, 1, size, width), jnp.bfloat16),
            [spot] + results,
            scalars=1,
            scratch=[turned],
        )

    return body


def solution(mesh):
    placed = (
        P(None, "prow", None, None),
        P(None, "prow", None, "pcol"),
        P(None, "prow", None, "pcol"),
        P(None, "prow", None, None),
        P(None, "prow", None, None),
        P(),
    )
    return jax.shard_map(
        make_body(mesh.shape["prow"], mesh.shape["pcol"]),
        mesh=mesh,
        in_specs=placed,
        out_specs=P(None, "prow", None, None),
        check_vma=False,
    )
```

```python
import functools

import jax
import jax.numpy as jnp
from jax import lax
from jax.experimental import pallas as pl
from jax.experimental.pallas import tpu as pltpu
from jax.sharding import PartitionSpec as P

CORES = 2
ROW, CHIP, CORE, DEPTH, LINE = range(5)
VMEM_BYTES = 40 * 1024 * 1024
FULL_BYTES = 58 * 1024 * 1024


def pair_index(later, earlier):
    return later * (later - 1) // 2 + earlier


def exact(left, right):
    return jnp.dot(left, right, preferred_element_type=jnp.float32)


def split(values, count):
    parts = []
    for _ in range(count):
        part = values.astype(jnp.bfloat16)
        parts.append(part)
        values = values - part.astype(jnp.float32)
    return parts


def level_of(array, level):
    shape = (1,) + array.shape[1:]
    return array, pl.BlockSpec(shape, lambda step: (level,) + (0,) * (len(shape) - 1))


def call(kernel, shapes, operands, scalars=0, scratch=(), room=VMEM_BYTES):
    arrays, specs = [], []
    for place, operand in enumerate(operands):
        if isinstance(operand, tuple):
            array, spec = operand
        else:
            array = operand
            space = pltpu.SMEM if place < scalars else pltpu.VMEM
            spec = pl.BlockSpec(memory_space=space)
        arrays.append(array)
        specs.append(spec)
    return pl.pallas_call(
        kernel,
        grid=(1,),
        out_shape=shapes,
        in_specs=specs,
        out_specs=jax.tree.map(lambda _: pl.BlockSpec(memory_space=pltpu.VMEM), shapes),
        scratch_shapes=list(scratch),
        compiler_params=pltpu.CompilerParams(vmem_limit_bytes=room),
    )(*arrays)


def share_of(values, turned, share, chip):
    turned[...] = values.T
    return turned[pl.ds(pl.multiple_of(chip * share, share), share), :]


def first_kernel(share, spot, rhs, inverse, out, turned):
    value = exact(inverse[0, 0], rhs[0, 0])
    out[...] = share_of(value, turned, share, spot[CHIP]).astype(out.dtype)


def panel_kernel(share, levels, spot, first, rhs, lower, upper, *rest):
    outs, turned = rest[:-1], rest[-1]
    chip = spot[CHIP]
    mine = spot[CORE] == 0
    value = lax.dot_general(
        first[...], upper[0, 0], (((1,), (1,)), ((), ())), preferred_element_type=jnp.float32
    )
    outs[0][...] = jnp.where(mine, value, 0.0)
    for level in range(1, levels):
        start = exact(lower[level, 0], rhs[level, 0])
        end = sum(exact(upper[level, 0], part) for part in split(start, 3))
        outs[level][...] = jnp.where(mine, share_of(end, turned, share, chip), 0.0)
        if level < levels - 1:
            value = share_of(start, turned, share, chip)
            outs[levels + level - 1][...] = jnp.where(mine, value, 0.0)


def fold_kernel(picks, left_count, spot, pattern, *refs):
    outs = refs[-len(picks) :]
    pieces = refs[left_count : -len(picks)]
    row, chip, core = spot[ROW], spot[CHIP], spot[CORE]
    depth, line = spot[DEPTH], spot[LINE]
    size = outs[0].shape[-1]
    group = pieces[0].shape[-1] // size
    if left_count == 1:
        sides = [refs[0][0, 0]]
    else:
        sides = split(exact(refs[0][0, 0], refs[1][0, 0]), 3)
    for index, piece in enumerate(pieces):
        deep = (chip ^ index) * CORES + core
        turn = (deep // CORES) ^ (depth // CORES)
        for across in range(group):
            block = deep * group + across
            slot = (across ^ line) * len(pieces) + turn
            columns = slice(across * size, (across + 1) * size)
            for pick, out in zip(picks, outs):
                pair, first, is_upper = pick
                keep = pattern[pair, block, row] if is_upper else pattern[pair, row, block]
                matrix = piece[pair - first if index else pair, 0, :, columns]
                matrix = jnp.where(keep > 0, matrix, jnp.zeros_like(matrix))
                folded = sum(exact(part, matrix) for part in sides).T
                for low, part in enumerate(split(folded, 2)):
                    out[slot, low] = part


def step_kernel(lines, base, *refs):
    out = refs[-1]
    refs = refs[:-1]
    total = base[...]
    share = total.shape[0]
    for term in range(len(refs) // (lines + 1)):
        stacks = refs[term * (lines + 1) :][:lines]
        matrix = refs[term * (lines + 1) + lines]
        each = matrix.shape[0] // lines
        for line in range(lines):
            for index in range(each):
                block = stacks[line][index * share : (index + 1) * share, :]
                for low in range(2):
                    total = total - exact(block, matrix[line * each + index, low])
    out[...] = total


def last_kernel(levels, chips, spot, *refs):
    out, turned = refs[-2], refs[-1]
    share = turned.shape[0] // chips
    chip = spot[CHIP]
    at = [pl.ds(pl.multiple_of((chip ^ b) * share, share), share) for b in range(chips)]
    for level in range(levels):
        for b in range(chips):
            if level > 0:
                part = refs[b][(level - 1) * share : level * share, :]
            else:
                part = refs[chips + b][...]
            turned[at[b], :] = part.astype(jnp.float32)
        out[level, 0] = turned[...].T.astype(out.dtype)


def make_body(rows, cols):
    chips = cols // CORES
    lines = chips
    depths = rows // lines
    near = depths // CORES
    assert near == chips

    def send(value, source_of):
        pairs = []
        for z in range(depths):
            for y in range(lines):
                for x in range(chips):
                    for core in range(CORES):
                        a, b, c, d = source_of(z, y, x, core)
                        pairs.append(
                            (
                                (a * lines + b) * cols + c * CORES + d,
                                (z * lines + y) * cols + x * CORES + core,
                            )
                        )
        return lax.ppermute(value, ("prow", "pcol"), pairs)

    def after(value, *signs):
        return lax.optimization_barrier((value,) + signs)[0]

    def body(right_side, lower_blocks, upper_blocks, lower_inverse, upper_inverse, pattern):
        levels, _, size, width = right_side.shape
        share = width // chips
        row = lax.axis_index("prow")
        col = lax.axis_index("pcol")
        line, core = row % lines, col % CORES
        spot = jnp.stack([row, col // CORES, core, row // lines, line]).astype(jnp.int32)
        top = levels - 1
        piece = jax.ShapeDtypeStruct((share, size), jnp.float32)
        chunk = jax.ShapeDtypeStruct((share, size), jnp.bfloat16)
        turned = pltpu.VMEM((width, size), jnp.float32)

        def relay(blocks):
            return [
                send(blocks, lambda z, y, x, core, b=b: (z, y, x ^ b, core))
                for b in range(1, chips)
            ]

        def fold(picks, inverses, pieces, sign):
            shape = jax.ShapeDtypeStruct((near * lines, 2, size, size), jnp.bfloat16)
            return call(
                functools.partial(fold_kernel, picks, len(inverses)),
                [shape] * len(picks),
                [after(spot, sign), pattern] + inverses + pieces,
                scalars=2,
            )

        def deep(value, work=None):
            found = [value]
            for m in range(1, depths):
                found.append(send(value, lambda z, y, x, core, m=m: (z ^ m, y, x, core)))
            parts = [
                jnp.where((row // lines) % CORES == core, found[m], found[m + 1])
                for m in range(0, depths, CORES)
            ]
            stack = jnp.concatenate(parts, axis=0)
            return after(stack, *work(found[1])) if work else stack

        def wide(stack):
            return [stack] + [
                send(stack, lambda z, y, x, core, e=e: (z, y ^ e, x, core)) for e in range(1, lines)
            ]

        def settle(partial_value):
            other = send(partial_value, lambda z, y, x, core: (z, y, x, 1 - core))
            return (partial_value + other).astype(jnp.bfloat16)

        def collect(value):
            return [value] + [
                send(value, lambda z, y, x, core, b=b: (z, y, x ^ b, core)) for b in range(1, chips)
            ]

        def step(base, terms):
            operands = [base]
            for stacks, matrix in terms:
                operands += stacks + [matrix]
            return call(functools.partial(step_kernel, lines), piece, operands)

        first = call(
            functools.partial(first_kernel, share),
            chunk,
            [spot, level_of(right_side, 0), level_of(lower_inverse, 0)],
            scalars=1,
            scratch=[turned],
            room=FULL_BYTES,
        )
        panels = call(
            functools.partial(panel_kernel, share, levels),
            [piece] * (2 * levels - 2),
            [spot, first, right_side, lower_inverse, upper_inverse],
            scalars=1,
            scratch=[turned],
        )
        ends, starts = panels[:levels], [None] + list(panels[levels:])

        low_all = relay(lower_blocks)
        last_pair = pair_index(top, top - 1)
        parts = (upper_blocks[last_pair:], upper_blocks[:last_pair])
        stack = deep(first, lambda sign: panels)
        stack, upper_one, upper_rest = lax.optimization_barrier((stack,) + parts)
        high_one = relay(upper_one)
        high_rest = relay(upper_rest)

        def fold_lower(later, both, sign):
            pairs = [pair_index(later, e) for e in range(later)]
            picks = tuple((pair, 0, False) for pair in pairs)
            inverses = [level_of(lower_inverse, later)]
            if both:
                inverses = [level_of(upper_inverse, later)] + inverses
            found = dict(zip(pairs, fold(picks, inverses, [lower_blocks] + low_all, sign)))
            (backward if both else forward).update(found)
            return list(found.values())

        def fold_upper(later, earlier, sign):
            pair = pair_index(later, earlier)
            picks = ((pair, pair if pair == last_pair else 0, True),)
            moved = high_one if pair == last_pair else high_rest
            inverses = [level_of(upper_inverse, earlier)]
            found = fold(picks, inverses, [upper_blocks] + moved, sign)[0]
            upward[later, earlier] = found
            return [found]

        fetched, back, solved = {}, {}, {}
        forward, backward, upward = {}, {}, {}
        fetched[0] = wide(stack)
        for level in range(1, top):
            fold_lower(level, False, stack)
            value = starts[level]
            for earlier in range(level):
                value = step(value, [(fetched[earlier], forward[pair_index(level, earlier)])])
            stack = deep(settle(value), lambda sign: fold_lower(level, True, sign))
            if level == top - 1:
                stack = after(stack, *high_one)
            fetched[level] = wide(stack)
        fold_lower(top, True, stack)

        for level in reversed(range(levels)):
            value = ends[level]
            if level == 0:
                results = collect(jnp.concatenate([solved[k] for k in range(1, levels)], axis=0))
                value = after(value, *results)
            for earlier in range(level):
                value = step(value, [(fetched[earlier], backward[pair_index(level, earlier)])])
            for later in reversed(range(level + 1, levels)):
                value = step(value, [(back[later], upward[later, level])])
            solved[level] = settle(value)
            if level > 0:
                work = None
                if level < top:
                    work = lambda sign: fold_upper(top, level - 1, sign)
                found = solved[level]
                if level == 1:
                    found = after(found, *high_rest)
                stack = deep(found, work)
                back[level] = wide(stack)
                for later in range(level, levels):
                    if (later, level - 1) not in upward:
                        fold_upper(later, level - 1, stack)
        results += collect(solved[0])
        return call(
            functools.partial(last_kernel, levels, chips),
            jax.ShapeDtypeStruct((levels, 1, size, width), jnp.bfloat16),
            [spot] + results,
            scalars=1,
            scratch=[turned],
        )

    return body


def solution(mesh):
    placed = (
        P(None, "prow", None, None),
        P(None, "prow", None, "pcol"),
        P(None, "prow", None, "pcol"),
        P(None, "prow", None, None),
        P(None, "prow", None, None),
        P(),
    )
    return jax.shard_map(
        make_body(mesh.shape["prow"], mesh.shape["pcol"]),
        mesh=mesh,
        in_specs=placed,
        out_specs=P(None, "prow", None, None),
        check_vma=False,
    )
```

```python
import functools

import jax
import jax.numpy as jnp
from jax import lax
from jax.experimental import pallas as pl
from jax.experimental.pallas import tpu as pltpu
from jax.sharding import PartitionSpec as P

CORES = 2
ROW, CHIP, CORE, DEPTH, LINE = range(5)
VMEM_BYTES = 40 * 1024 * 1024
FULL_BYTES = 58 * 1024 * 1024


def pair_index(later, earlier):
    return later * (later - 1) // 2 + earlier


def exact(left, right):
    return jnp.dot(left, right, preferred_element_type=jnp.float32)


def split(values, count):
    parts = []
    for _ in range(count):
        part = values.astype(jnp.bfloat16)
        parts.append(part)
        values = values - part.astype(jnp.float32)
    return parts


def level_of(array, level):
    shape = (1,) + array.shape[1:]
    return array, pl.BlockSpec(shape, lambda step: (level,) + (0,) * (len(shape) - 1))


def call(kernel, shapes, operands, scalars=0, scratch=(), room=VMEM_BYTES):
    arrays, specs = [], []
    for place, operand in enumerate(operands):
        if isinstance(operand, tuple):
            array, spec = operand
        else:
            array = operand
            space = pltpu.SMEM if place < scalars else pltpu.VMEM
            spec = pl.BlockSpec(memory_space=space)
        arrays.append(array)
        specs.append(spec)
    return pl.pallas_call(
        kernel,
        grid=(1,),
        out_shape=shapes,
        in_specs=specs,
        out_specs=jax.tree.map(lambda _: pl.BlockSpec(memory_space=pltpu.VMEM), shapes),
        scratch_shapes=list(scratch),
        compiler_params=pltpu.CompilerParams(vmem_limit_bytes=room),
    )(*arrays)


def share_of(values, turned, share, chip):
    turned[...] = values.T
    return turned[pl.ds(pl.multiple_of(chip * share, share), share), :]


def first_kernel(share, spot, rhs, inverse, blocks, out, copied, turned):
    copied[...] = blocks[...]
    value = exact(inverse[0, 0], rhs[0, 0])
    out[...] = share_of(value, turned, share, spot[CHIP]).astype(out.dtype)


def panel_kernel(share, levels, spot, first, rhs, lower, upper, *rest):
    outs, turned = rest[:-1], rest[-1]
    chip = spot[CHIP]
    mine = spot[CORE] == 0
    value = lax.dot_general(
        first[...], upper[0, 0], (((1,), (1,)), ((), ())), preferred_element_type=jnp.float32
    )
    outs[0][...] = jnp.where(mine, value, 0.0)
    for level in range(1, levels):
        start = exact(lower[level, 0], rhs[level, 0])
        end = sum(exact(upper[level, 0], part) for part in split(start, 3))
        outs[level][...] = jnp.where(mine, share_of(end, turned, share, chip), 0.0)
        if level < levels - 1:
            value = share_of(start, turned, share, chip)
            outs[levels + level - 1][...] = jnp.where(mine, value, 0.0)


def fold_kernel(picks, left_count, spot, pattern, *refs):
    outs = refs[-len(picks) :]
    pieces = refs[left_count : -len(picks)]
    row, chip, core = spot[ROW], spot[CHIP], spot[CORE]
    depth, line = spot[DEPTH], spot[LINE]
    size = outs[0].shape[-1]
    group = pieces[0].shape[-1] // size
    if left_count == 1:
        sides = [refs[0][0, 0]]
    else:
        sides = split(exact(refs[0][0, 0], refs[1][0, 0]), 3)
    for index, piece in enumerate(pieces):
        deep = (chip ^ index) * CORES + core
        turn = (deep // CORES) ^ (depth // CORES)
        for across in range(group):
            block = deep * group + across
            slot = (across ^ line) * len(pieces) + turn
            columns = slice(across * size, (across + 1) * size)
            for pick, out in zip(picks, outs):
                pair, is_upper = pick
                keep = pattern[pair, block, row] if is_upper else pattern[pair, row, block]
                matrix = piece[0 if index else pair, 0, :, columns]
                matrix = jnp.where(keep > 0, matrix, jnp.zeros_like(matrix))
                folded = sum(exact(part, matrix) for part in sides).T
                for low, part in enumerate(split(folded, 2)):
                    out[slot, low] = part


def pick_kernel(pairs, sign, *refs):
    for (is_upper, pair), out in zip(pairs, refs[2:]):
        out[0] = refs[1 if is_upper else 0][pair]


def step_kernel(lines, base, *refs):
    out = refs[-1]
    refs = refs[:-1]
    total = base[...]
    share = total.shape[0]
    for term in range(len(refs) // (lines + 1)):
        stacks = refs[term * (lines + 1) :][:lines]
        matrix = refs[term * (lines + 1) + lines]
        each = matrix.shape[0] // lines
        for line in range(lines):
            for index in range(each):
                block = stacks[line][index * share : (index + 1) * share, :]
                for low in range(2):
                    total = total - exact(block, matrix[line * each + index, low])
    out[...] = total


def last_kernel(levels, chips, spot, *refs):
    out, turned = refs[-2], refs[-1]
    share = turned.shape[0] // chips
    chip = spot[CHIP]
    at = [pl.ds(pl.multiple_of((chip ^ b) * share, share), share) for b in range(chips)]
    for level in range(levels):
        for b in range(chips):
            if level > 0:
                part = refs[b][(level - 1) * share : level * share, :]
            else:
                part = refs[chips + b][...]
            turned[at[b], :] = part.astype(jnp.float32)
        out[level, 0] = turned[...].T.astype(out.dtype)


def make_body(rows, cols):
    chips = cols // CORES
    lines = chips
    depths = rows // lines
    near = depths // CORES
    assert near == chips

    def send(value, source_of):
        pairs = []
        for z in range(depths):
            for y in range(lines):
                for x in range(chips):
                    for core in range(CORES):
                        a, b, c, d = source_of(z, y, x, core)
                        pairs.append(
                            (
                                (a * lines + b) * cols + c * CORES + d,
                                (z * lines + y) * cols + x * CORES + core,
                            )
                        )
        return lax.ppermute(value, ("prow", "pcol"), pairs)

    def after(value, *signs):
        return lax.optimization_barrier((value,) + signs)[0]

    def body(right_side, lower_blocks, upper_blocks, lower_inverse, upper_inverse, pattern):
        levels, _, size, width = right_side.shape
        share = width // chips
        row = lax.axis_index("prow")
        col = lax.axis_index("pcol")
        line, core = row % lines, col % CORES
        spot = jnp.stack([row, col // CORES, core, row // lines, line]).astype(jnp.int32)
        top = levels - 1
        piece = jax.ShapeDtypeStruct((share, size), jnp.float32)
        chunk = jax.ShapeDtypeStruct((share, size), jnp.bfloat16)
        turned = pltpu.VMEM((width, size), jnp.float32)

        def relay(blocks):
            return [
                send(blocks, lambda z, y, x, core, b=b: (z, y, x ^ b, core))
                for b in range(1, chips)
            ]

        def fold(picks, inverses, pieces, sign):
            shape = jax.ShapeDtypeStruct((near * lines, 2, size, size), jnp.bfloat16)
            return call(
                functools.partial(fold_kernel, picks, len(inverses)),
                [shape] * len(picks),
                [after(spot, sign), pattern] + inverses + pieces,
                scalars=2,
            )

        def deep(value, work=None):
            found = [value]
            for m in range(1, depths):
                found.append(send(value, lambda z, y, x, core, m=m: (z ^ m, y, x, core)))
            parts = [
                jnp.where((row // lines) % CORES == core, found[m], found[m + 1])
                for m in range(0, depths, CORES)
            ]
            stack = jnp.concatenate(parts, axis=0)
            return after(stack, *work(found[1])) if work else stack

        def wide(stack):
            return [stack] + [
                send(stack, lambda z, y, x, core, e=e: (z, y ^ e, x, core)) for e in range(1, lines)
            ]

        def settle(partial_value):
            other = send(partial_value, lambda z, y, x, core: (z, y, x, 1 - core))
            return (partial_value + other).astype(jnp.bfloat16)

        def collect(value):
            return [value] + [
                send(value, lambda z, y, x, core, b=b: (z, y, x ^ b, core)) for b in range(1, chips)
            ]

        def step(base, terms):
            operands = [base]
            for stacks, matrix in terms:
                operands += stacks + [matrix]
            return call(functools.partial(step_kernel, lines), piece, operands)

        single = jax.ShapeDtypeStruct((1,) + lower_blocks.shape[1:], jnp.bfloat16)
        first, first_blocks = call(
            functools.partial(first_kernel, share),
            [chunk, single],
            [spot, level_of(right_side, 0), level_of(lower_inverse, 0), level_of(lower_blocks, 0)],
            scalars=1,
            scratch=[turned],
            room=FULL_BYTES,
        )
        panels = call(
            functools.partial(panel_kernel, share, levels),
            [piece] * (2 * levels - 2),
            [spot, first, right_side, lower_inverse, upper_inverse],
            scalars=1,
            scratch=[turned],
        )
        ends, starts = panels[:levels], [None] + list(panels[levels:])

        order = [(False, a, e) for a in range(1, levels) for e in range(a)]
        order += [(True, a, e) for a in range(top, 0, -1) for e in range(a - 1, a - 2, -1)]
        order += [(True, a, e) for e in reversed(range(top)) for a in range(e + 2, levels)]
        own = [first_blocks]
        picked = tuple((key[0], pair_index(*key[1:])) for key in order[1:])

        def pick(sign):
            operands = [after(spot, first), lower_blocks, upper_blocks]
            own.extend(
                call(
                    functools.partial(pick_kernel, picked),
                    [single] * len(picked),
                    operands,
                    scalars=1,
                )
            )
            return list(panels) + own[1:]

        def fold_one(is_upper, later, earlier, both, sign):
            pair = pair_index(later, earlier)
            inverses = [level_of(lower_inverse, later)]
            if is_upper:
                inverses = [level_of(upper_inverse, earlier)]
            elif both:
                inverses = [level_of(upper_inverse, later)] + inverses
            pieces = [upper_blocks if is_upper else lower_blocks] + moved[is_upper, later, earlier]
            found = fold(((pair, is_upper),), inverses, pieces, sign)[0]
            kept = upward if is_upper else backward if both else forward
            kept[later, earlier] = found
            return [found]

        moved, fetched, back, solved = {}, {}, {}, {}
        forward, backward, upward = {}, {}, {}
        count = sum(1 for key in order if not key[0])
        stack = deep(first, pick)
        fetched[0] = wide(stack)
        previous = []
        for key, value in zip(order[:count], own[:count]):
            previous = moved[key] = relay(after(value, *previous) if previous else value)
        for level in range(1, top):
            for earlier in range(level):
                fold_one(False, level, earlier, False, stack)
            value = starts[level]
            for earlier in range(level):
                value = step(value, [(fetched[earlier], forward[level, earlier])])
            work = None
            if level == top - 1:
                work = lambda sign: fold_one(False, top, 0, True, sign)
            stack = deep(settle(value), work)
            fetched[level] = wide(stack)
        for key, value in zip(order[count:], own[count:]):
            previous = moved[key] = relay(after(value, *previous))
        for is_upper, later, earlier in order[:count]:
            if (later, earlier) not in backward:
                fold_one(False, later, earlier, True, stack)

        for level in reversed(range(levels)):
            value = ends[level]
            if level == 0:
                results = collect(jnp.concatenate([solved[k] for k in range(1, levels)], axis=0))
                value = after(value, *results)
            for earlier in range(level):
                value = step(value, [(fetched[earlier], backward[level, earlier])])
            for later in reversed(range(level + 1, levels)):
                value = step(value, [(back[later], upward[later, level])])
            solved[level] = settle(value)
            if level > 0:
                work = None
                if level < top:
                    work = lambda sign: fold_one(True, level, level - 1, False, sign)
                stack = deep(solved[level], work)
                back[level] = wide(stack)
                for later in range(level, levels):
                    if (later, level - 1) not in upward:
                        fold_one(True, later, level - 1, False, stack)
        results += collect(solved[0])
        return call(
            functools.partial(last_kernel, levels, chips),
            jax.ShapeDtypeStruct((levels, 1, size, width), jnp.bfloat16),
            [spot] + results,
            scalars=1,
            scratch=[turned],
        )

    return body


def solution(mesh):
    placed = (
        P(None, "prow", None, None),
        P(None, "prow", None, "pcol"),
        P(None, "prow", None, "pcol"),
        P(None, "prow", None, None),
        P(None, "prow", None, None),
        P(),
    )
    return jax.shard_map(
        make_body(mesh.shape["prow"], mesh.shape["pcol"]),
        mesh=mesh,
        in_specs=placed,
        out_specs=P(None, "prow", None, None),
        check_vma=False,
    )
```

```python
import functools

import jax
import jax.numpy as jnp
from jax import lax
from jax.experimental import pallas as pl
from jax.experimental.pallas import tpu as pltpu
from jax.sharding import PartitionSpec as P

CORES = 2
ROW, CHIP, CORE, DEPTH, LINE = range(5)
VMEM_BYTES = 40 * 1024 * 1024
FULL_BYTES = 58 * 1024 * 1024


def pair_index(later, earlier):
    return later * (later - 1) // 2 + earlier


def exact(left, right):
    return jnp.dot(left, right, preferred_element_type=jnp.float32)


def split(values, count):
    parts = []
    for _ in range(count):
        part = values.astype(jnp.bfloat16)
        parts.append(part)
        values = values - part.astype(jnp.float32)
    return parts


def level_of(array, level):
    shape = (1,) + array.shape[1:]
    return array, pl.BlockSpec(shape, lambda step: (level,) + (0,) * (len(shape) - 1))


def call(kernel, shapes, operands, scalars=0, scratch=(), room=VMEM_BYTES):
    arrays, specs = [], []
    for place, operand in enumerate(operands):
        if isinstance(operand, tuple):
            array, spec = operand
        else:
            array = operand
            space = pltpu.SMEM if place < scalars else pltpu.VMEM
            spec = pl.BlockSpec(memory_space=space)
        arrays.append(array)
        specs.append(spec)
    return pl.pallas_call(
        kernel,
        grid=(1,),
        out_shape=shapes,
        in_specs=specs,
        out_specs=jax.tree.map(lambda _: pl.BlockSpec(memory_space=pltpu.VMEM), shapes),
        scratch_shapes=list(scratch),
        compiler_params=pltpu.CompilerParams(vmem_limit_bytes=room),
    )(*arrays)


def share_of(values, turned, share, chip):
    turned[...] = values.T
    return turned[pl.ds(pl.multiple_of(chip * share, share), share), :]


def first_kernel(share, spot, rhs, inverse, blocks, out, copied, turned):
    copied[...] = blocks[...]
    value = exact(inverse[0, 0], rhs[0, 0])
    out[...] = share_of(value, turned, share, spot[CHIP]).astype(out.dtype)


def panel_kernel(share, levels, spot, first, rhs, lower, upper, *rest):
    outs, turned = rest[:-1], rest[-1]
    chip = spot[CHIP]
    mine = spot[CORE] == 0
    value = lax.dot_general(
        first[...], upper[0, 0], (((1,), (1,)), ((), ())), preferred_element_type=jnp.float32
    )
    outs[0][...] = jnp.where(mine, value, 0.0)
    for level in range(1, levels):
        start = exact(lower[level, 0], rhs[level, 0])
        end = sum(exact(upper[level, 0], part) for part in split(start, 3))
        outs[level][...] = jnp.where(mine, share_of(end, turned, share, chip), 0.0)
        if level < levels - 1:
            value = share_of(start, turned, share, chip)
            outs[levels + level - 1][...] = jnp.where(mine, value, 0.0)


def fold_kernel(picks, left_count, spot, pattern, *refs):
    outs = refs[-len(picks) :]
    pieces = refs[left_count : -len(picks)]
    row, chip, core = spot[ROW], spot[CHIP], spot[CORE]
    depth, line = spot[DEPTH], spot[LINE]
    size = outs[0].shape[-1]
    group = pieces[0].shape[-1] // size
    if left_count == 1:
        sides = [refs[0][0, 0]]
    else:
        sides = split(exact(refs[0][0, 0], refs[1][0, 0]), 3)
    for index, piece in enumerate(pieces):
        deep = (chip ^ index) * CORES + core
        turn = (deep // CORES) ^ (depth // CORES)
        for across in range(group):
            block = deep * group + across
            slot = (across ^ line) * len(pieces) + turn
            columns = slice(across * size, (across + 1) * size)
            for pick, out in zip(picks, outs):
                pair, first, is_upper = pick
                keep = pattern[pair, block, row] if is_upper else pattern[pair, row, block]
                matrix = piece[pair - first if index else pair, 0, :, columns]
                matrix = jnp.where(keep > 0, matrix, jnp.zeros_like(matrix))
                folded = sum(exact(part, matrix) for part in sides).T
                for low, part in enumerate(split(folded, 2)):
                    out[slot, low] = part


def pick_kernel(parts, sign, *refs):
    for (is_upper, start), out in zip(parts, refs[2:]):
        out[...] = refs[1 if is_upper else 0][start : start + out.shape[0]]


def step_kernel(lines, base, *refs):
    out = refs[-1]
    refs = refs[:-1]
    total = base[...]
    share = total.shape[0]
    for term in range(len(refs) // (lines + 1)):
        stacks = refs[term * (lines + 1) :][:lines]
        matrix = refs[term * (lines + 1) + lines]
        each = matrix.shape[0] // lines
        for line in range(lines):
            for index in range(each):
                block = stacks[line][index * share : (index + 1) * share, :]
                for low in range(2):
                    total = total - exact(block, matrix[line * each + index, low])
    out[...] = total


def last_kernel(levels, chips, spot, *refs):
    out, turned = refs[-2], refs[-1]
    share = turned.shape[0] // chips
    chip = spot[CHIP]
    at = [pl.ds(pl.multiple_of((chip ^ b) * share, share), share) for b in range(chips)]
    for level in range(levels):
        for b in range(chips):
            if level > 0:
                part = refs[b][(level - 1) * share : level * share, :]
            else:
                part = refs[chips + b][...]
            turned[at[b], :] = part.astype(jnp.float32)
        out[level, 0] = turned[...].T.astype(out.dtype)


def make_body(rows, cols):
    chips = cols // CORES
    lines = chips
    depths = rows // lines
    near = depths // CORES
    assert near == chips

    def send(value, source_of):
        pairs = []
        for z in range(depths):
            for y in range(lines):
                for x in range(chips):
                    for core in range(CORES):
                        a, b, c, d = source_of(z, y, x, core)
                        pairs.append(
                            (
                                (a * lines + b) * cols + c * CORES + d,
                                (z * lines + y) * cols + x * CORES + core,
                            )
                        )
        return lax.ppermute(value, ("prow", "pcol"), pairs)

    def after(value, *signs):
        return lax.optimization_barrier((value,) + signs)[0]

    def body(right_side, lower_blocks, upper_blocks, lower_inverse, upper_inverse, pattern):
        levels, _, size, width = right_side.shape
        share = width // chips
        row = lax.axis_index("prow")
        col = lax.axis_index("pcol")
        line, core = row % lines, col % CORES
        spot = jnp.stack([row, col // CORES, core, row // lines, line]).astype(jnp.int32)
        top = levels - 1
        piece = jax.ShapeDtypeStruct((share, size), jnp.float32)
        chunk = jax.ShapeDtypeStruct((share, size), jnp.bfloat16)
        turned = pltpu.VMEM((width, size), jnp.float32)

        def relay(blocks):
            return [
                send(blocks, lambda z, y, x, core, b=b: (z, y, x ^ b, core))
                for b in range(1, chips)
            ]

        def fold(picks, inverses, pieces, sign):
            shape = jax.ShapeDtypeStruct((near * lines, 2, size, size), jnp.bfloat16)
            return call(
                functools.partial(fold_kernel, picks, len(inverses)),
                [shape] * len(picks),
                [after(spot, sign), pattern] + inverses + pieces,
                scalars=2,
            )

        def deep(value, work=None):
            found = [value]
            for m in range(1, depths):
                found.append(send(value, lambda z, y, x, core, m=m: (z ^ m, y, x, core)))
            parts = [
                jnp.where((row // lines) % CORES == core, found[m], found[m + 1])
                for m in range(0, depths, CORES)
            ]
            stack = jnp.concatenate(parts, axis=0)
            return after(stack, *work(found[1])) if work else stack

        def wide(stack):
            return [stack] + [
                send(stack, lambda z, y, x, core, e=e: (z, y ^ e, x, core)) for e in range(1, lines)
            ]

        def settle(partial_value):
            other = send(partial_value, lambda z, y, x, core: (z, y, x, 1 - core))
            return (partial_value + other).astype(jnp.bfloat16)

        def collect(value):
            return [value] + [
                send(value, lambda z, y, x, core, b=b: (z, y, x ^ b, core)) for b in range(1, chips)
            ]

        def step(base, terms):
            operands = [base]
            for stacks, matrix in terms:
                operands += stacks + [matrix]
            return call(functools.partial(step_kernel, lines), piece, operands)

        single = jax.ShapeDtypeStruct((1,) + lower_blocks.shape[1:], jnp.bfloat16)
        first, first_blocks = call(
            functools.partial(first_kernel, share),
            [chunk, single],
            [spot, level_of(right_side, 0), level_of(lower_inverse, 0), level_of(lower_blocks, 0)],
            scalars=1,
            scratch=[turned],
            room=FULL_BYTES,
        )
        panels = call(
            functools.partial(panel_kernel, share, levels),
            [piece] * (2 * levels - 2),
            [spot, first, right_side, lower_inverse, upper_inverse],
            scalars=1,
            scratch=[turned],
        )
        ends, starts = panels[:levels], [None] + list(panels[levels:])

        last_pair = pair_index(top, top - 1)
        parts = ((False, 1), (True, last_pair), (True, 0))
        counts = (lower_blocks.shape[0] - 1, 1, last_pair)
        picked = call(
            functools.partial(pick_kernel, parts),
            [jax.ShapeDtypeStruct((n,) + single.shape[1:], single.dtype) for n in counts],
            [after(spot, first), lower_blocks, upper_blocks],
            scalars=1,
        )
        low_one = relay(first_blocks)
        low_rest = relay(after(picked[0], *low_one))
        high_one = relay(after(picked[1], *low_rest))
        high_rest = relay(after(picked[2], *high_one))

        def fold_lower(later, both, sign):
            moved = low_one if later == 1 else low_rest
            pairs = [pair_index(later, e) for e in range(later)]
            picks = tuple((pair, min(later - 1, 1), False) for pair in pairs)
            inverses = [level_of(lower_inverse, later)]
            if both:
                inverses = [level_of(upper_inverse, later)] + inverses
            found = fold(picks, inverses, [lower_blocks] + moved, sign)
            kept = backward if both else forward
            kept.update({(later, e): value for e, value in enumerate(found)})
            return found

        def fold_upper(later, earlier, sign):
            pair = pair_index(later, earlier)
            moved = high_one if pair == last_pair else high_rest
            picks = ((pair, pair if pair == last_pair else 0, True),)
            inverses = [level_of(upper_inverse, earlier)]
            upward[later, earlier] = fold(picks, inverses, [upper_blocks] + moved, sign)[0]

        fetched, back, solved = {}, {}, {}
        forward, backward, upward = {}, {}, {}
        stack = deep(first, lambda sign: list(panels) + list(picked))
        fetched[0] = wide(stack)
        for level in range(1, top):
            fold_lower(level, False, stack)
            value = starts[level]
            for earlier in range(level):
                value = step(value, [(fetched[earlier], forward[level, earlier])])
            stack = deep(settle(value), lambda sign: fold_lower(level, True, sign))
            fetched[level] = wide(stack)
        fold_lower(top, True, stack)

        for level in reversed(range(levels)):
            value = ends[level]
            if level == 0:
                results = collect(jnp.concatenate([solved[k] for k in range(1, levels)], axis=0))
                value = after(value, *results)
            for earlier in range(level):
                value = step(value, [(fetched[earlier], backward[level, earlier])])
            for later in reversed(range(level + 1, levels)):
                value = step(value, [(back[later], upward[later, level])])
            solved[level] = settle(value)
            if level > 0:
                stack = deep(solved[level])
                back[level] = wide(stack)
                for later in range(level, levels):
                    fold_upper(later, level - 1, stack)
        results += collect(solved[0])
        return call(
            functools.partial(last_kernel, levels, chips),
            jax.ShapeDtypeStruct((levels, 1, size, width), jnp.bfloat16),
            [spot] + results,
            scalars=1,
            scratch=[turned],
        )

    return body


def solution(mesh):
    placed = (
        P(None, "prow", None, None),
        P(None, "prow", None, "pcol"),
        P(None, "prow", None, "pcol"),
        P(None, "prow", None, None),
        P(None, "prow", None, None),
        P(),
    )
    return jax.shard_map(
        make_body(mesh.shape["prow"], mesh.shape["pcol"]),
        mesh=mesh,
        in_specs=placed,
        out_specs=P(None, "prow", None, None),
        check_vma=False,
    )
```

```python
import functools

import jax
import jax.numpy as jnp
from jax import lax
from jax.experimental import pallas as pl
from jax.experimental.pallas import tpu as pltpu
from jax.sharding import PartitionSpec as P

CORES = 2
ROW, CHIP, CORE, DEPTH, LINE = range(5)
VMEM_BYTES = 40 * 1024 * 1024
FULL_BYTES = 58 * 1024 * 1024


def pair_index(later, earlier):
    return later * (later - 1) // 2 + earlier


def exact(left, right):
    return jnp.dot(left, right, preferred_element_type=jnp.float32)


def split(values, count):
    parts = []
    for _ in range(count):
        part = values.astype(jnp.bfloat16)
        parts.append(part)
        values = values - part.astype(jnp.float32)
    return parts


def level_of(array, level):
    shape = (1,) + array.shape[1:]
    return array, pl.BlockSpec(shape, lambda step: (level,) + (0,) * (len(shape) - 1))


def call(kernel, shapes, operands, scalars=0, scratch=(), room=VMEM_BYTES, out_spec=None, aliases=None):
    arrays, specs = [], []
    for place, operand in enumerate(operands):
        if isinstance(operand, tuple):
            array, spec = operand
        else:
            array = operand
            space = pltpu.SMEM if place < scalars else pltpu.VMEM
            spec = pl.BlockSpec(memory_space=space)
        arrays.append(array)
        specs.append(spec)
    return pl.pallas_call(
        kernel,
        grid=(1,),
        out_shape=shapes,
        in_specs=specs,
        out_specs=out_spec
        or jax.tree.map(lambda _: pl.BlockSpec(memory_space=pltpu.VMEM), shapes),
        input_output_aliases=aliases or {},
        scratch_shapes=list(scratch),
        compiler_params=pltpu.CompilerParams(vmem_limit_bytes=room),
    )(*arrays)


def share_of(values, turned, share, chip):
    turned[...] = values.T
    return turned[pl.ds(pl.multiple_of(chip * share, share), share), :]


def first_kernel(share, spot, rhs, inverse, out, turned):
    value = exact(inverse[0, 0], rhs[0, 0])
    out[...] = share_of(value, turned, share, spot[CHIP]).astype(out.dtype)


def panel_kernel(share, levels, spot, first, rhs, lower, upper, *rest):
    outs, turned = rest[:-1], rest[-1]
    chip = spot[CHIP]
    mine = spot[CORE] == 0
    value = lax.dot_general(
        first[...], upper[0, 0], (((1,), (1,)), ((), ())), preferred_element_type=jnp.float32
    )
    outs[0][...] = jnp.where(mine, value, 0.0)
    for level in range(1, levels):
        start = exact(lower[level, 0], rhs[level, 0])
        end = sum(exact(upper[level, 0], part) for part in split(start, 3))
        outs[level][...] = jnp.where(mine, share_of(end, turned, share, chip), 0.0)
        if level < levels - 1:
            value = share_of(start, turned, share, chip)
            outs[levels + level - 1][...] = jnp.where(mine, value, 0.0)


def fold_kernel(picks, left_count, spot, pattern, *refs):
    outs = refs[-len(picks) :]
    pieces = refs[left_count : -len(picks)]
    row, chip, core = spot[ROW], spot[CHIP], spot[CORE]
    depth, line = spot[DEPTH], spot[LINE]
    size = outs[0].shape[-1]
    group = pieces[0].shape[-1] // size
    if left_count == 1:
        sides = [refs[0][0, 0]]
    else:
        sides = split(exact(refs[0][0, 0], refs[1][0, 0]), 3)
    for index, piece in enumerate(pieces):
        deep = (chip ^ index) * CORES + core
        turn = (deep // CORES) ^ (depth // CORES)
        for across in range(group):
            block = deep * group + across
            slot = (across ^ line) * len(pieces) + turn
            columns = slice(across * size, (across + 1) * size)
            for pick, out in zip(picks, outs):
                pair, first, is_upper = pick
                keep = pattern[pair, block, row] if is_upper else pattern[pair, row, block]
                matrix = piece[pair - first if index else pair, 0, :, columns]
                matrix = jnp.where(keep > 0, matrix, jnp.zeros_like(matrix))
                folded = sum(exact(part, matrix) for part in sides).T
                for low, part in enumerate(split(folded, 2)):
                    out[slot, low] = part


def direct_kernel(pair, lines, chips, spot, pattern, base, inverse, *refs):
    pieces, stacks, out, blocks = refs[:chips], refs[chips:-2], refs[-2], refs[-1]
    row, chip, core = spot[ROW], spot[CHIP], spot[CORE]
    depth, line = spot[DEPTH], spot[LINE]
    share, size = base.shape
    for index, stack in enumerate(stacks):
        for turn in range(chips):
            blocks[index * chips + turn] = stack[turn * share : (turn + 1) * share, :]

    def times(left, right):
        return lax.dot_general(
            left, right, (((1,), (1,)), ((), ())), preferred_element_type=jnp.float32
        )

    total = jnp.zeros((share, size), jnp.float32)
    for index, piece in enumerate(pieces):
        deep = (chip ^ index) * CORES + core
        turn = (deep // CORES) ^ (depth // CORES)
        for across in range(lines):
            keep = pattern[pair, row, deep * lines + across]
            matrix = piece[0, 0, :, across * size : (across + 1) * size]
            matrix = jnp.where(keep > 0, matrix, jnp.zeros_like(matrix))
            total = total + times(blocks[(across ^ line) * chips + turn], matrix)
    value = base[...]
    for part in split(total, 3):
        value = value - times(part, inverse[0, 0])
    out[...] = value


def step_kernel(lines, base, *refs):
    out = refs[-1]
    refs = refs[:-1]
    total = base[...]
    share = total.shape[0]
    for term in range(len(refs) // (lines + 1)):
        stacks = refs[term * (lines + 1) :][:lines]
        matrix = refs[term * (lines + 1) + lines]
        each = matrix.shape[0] // lines
        for line in range(lines):
            for index in range(each):
                block = stacks[line][index * share : (index + 1) * share, :]
                for low in range(2):
                    total = total - exact(block, matrix[line * each + index, low])
    out[...] = total


def late_kernel(levels, chips, spot, *refs):
    out, turned = refs[-2], refs[-1]
    share = turned.shape[0] // chips
    out[0] = jnp.zeros_like(out[0])
    for level in range(1, levels):
        for b in range(chips):
            at = pl.ds(pl.multiple_of((spot[CHIP] ^ b) * share, share), share)
            part = refs[b][(level - 1) * share : level * share, :]
            turned[at, :] = part.astype(jnp.float32)
        out[level, 0] = turned[...].T.astype(out.dtype)


def last_kernel(chips, spot, whole, *refs):
    out, turned = refs[-2], refs[-1]
    share = turned.shape[0] // chips
    for b in range(chips):
        at = pl.ds(pl.multiple_of((spot[CHIP] ^ b) * share, share), share)
        turned[at, :] = refs[b][...].astype(jnp.float32)
    out[0, 0] = turned[...].T.astype(out.dtype)


def make_body(rows, cols):
    chips = cols // CORES
    lines = chips
    depths = rows // lines
    near = depths // CORES
    assert near == chips

    def send(value, source_of):
        pairs = []
        for z in range(depths):
            for y in range(lines):
                for x in range(chips):
                    for core in range(CORES):
                        a, b, c, d = source_of(z, y, x, core)
                        pairs.append(
                            (
                                (a * lines + b) * cols + c * CORES + d,
                                (z * lines + y) * cols + x * CORES + core,
                            )
                        )
        return lax.ppermute(value, ("prow", "pcol"), pairs)

    def after(value, *signs):
        return lax.optimization_barrier((value,) + signs)[0]

    def body(right_side, lower_blocks, upper_blocks, lower_inverse, upper_inverse, pattern):
        levels, _, size, width = right_side.shape
        share = width // chips
        row = lax.axis_index("prow")
        col = lax.axis_index("pcol")
        line, core = row % lines, col % CORES
        spot = jnp.stack([row, col // CORES, core, row // lines, line]).astype(jnp.int32)
        top = levels - 1
        piece = jax.ShapeDtypeStruct((share, size), jnp.float32)
        chunk = jax.ShapeDtypeStruct((share, size), jnp.bfloat16)
        turned = pltpu.VMEM((width, size), jnp.float32)

        def relay(blocks):
            return [
                send(blocks, lambda z, y, x, core, b=b: (z, y, x ^ b, core))
                for b in range(1, chips)
            ]

        def fold(picks, inverses, pieces, sign):
            shape = jax.ShapeDtypeStruct((near * lines, 2, size, size), jnp.bfloat16)
            return call(
                functools.partial(fold_kernel, picks, len(inverses)),
                [shape] * len(picks),
                [after(spot, sign), pattern] + inverses + pieces,
                scalars=2,
            )

        def deep(value, work=None):
            found = [value]
            for m in range(1, depths):
                found.append(send(value, lambda z, y, x, core, m=m: (z ^ m, y, x, core)))
            parts = [
                jnp.where((row // lines) % CORES == core, found[m], found[m + 1])
                for m in range(0, depths, CORES)
            ]
            stack = jnp.concatenate(parts, axis=0)
            return after(stack, *work(found[1])) if work else stack

        def wide(stack):
            return [stack] + [
                send(stack, lambda z, y, x, core, e=e: (z, y ^ e, x, core)) for e in range(1, lines)
            ]

        def settle(partial_value):
            other = send(partial_value, lambda z, y, x, core: (z, y, x, 1 - core))
            return (partial_value + other).astype(jnp.bfloat16)

        def collect(value):
            return [value] + [
                send(value, lambda z, y, x, core, b=b: (z, y, x ^ b, core)) for b in range(1, chips)
            ]

        def step(base, terms):
            operands = [base]
            for stacks, matrix in terms:
                operands += stacks + [matrix]
            return call(functools.partial(step_kernel, lines), piece, operands)

        first = call(
            functools.partial(first_kernel, share),
            chunk,
            [spot, level_of(right_side, 0), level_of(lower_inverse, 0)],
            scalars=1,
            scratch=[turned],
            room=FULL_BYTES,
        )
        panels = call(
            functools.partial(panel_kernel, share, levels),
            [piece] * (2 * levels - 2),
            [spot, first, right_side, lower_inverse, upper_inverse],
            scalars=1,
            scratch=[turned],
        )
        ends, starts = panels[:levels], [None] + list(panels[levels:])

        low_all = relay(lower_blocks)
        last_pair = pair_index(top, top - 1)
        parts = (upper_blocks[last_pair:], upper_blocks[:last_pair])
        stack = deep(first, lambda sign: panels)
        stack, upper_one, upper_rest = lax.optimization_barrier((stack,) + parts)
        high_one = relay(upper_one)
        high_rest = relay(upper_rest)

        def fold_lower(later, both, sign):
            pairs = [pair_index(later, e) for e in range(later)]
            picks = tuple((pair, 0, False) for pair in pairs)
            inverses = [level_of(lower_inverse, later)]
            if both:
                inverses = [level_of(upper_inverse, later)] + inverses
            found = dict(zip(pairs, fold(picks, inverses, [lower_blocks] + low_all, sign)))
            (backward if both else forward).update(found)
            return list(found.values())

        def fold_upper(later, earlier, sign):
            pair = pair_index(later, earlier)
            picks = ((pair, pair if pair == last_pair else 0, True),)
            moved = high_one if pair == last_pair else high_rest
            inverses = [level_of(upper_inverse, earlier)]
            found = fold(picks, inverses, [upper_blocks] + moved, sign)[0]
            upward[later, earlier] = found
            return [found]

        fetched, back, solved = {}, {}, {}
        forward, backward, upward = {}, {}, {}
        fetched[0] = wide(stack)
        for level in range(1, top):
            value = starts[level]
            if level == 1:
                pieces = [level_of(blocks, 0) for blocks in [lower_blocks] + low_all]
                value = call(
                    functools.partial(direct_kernel, 0, lines, chips),
                    piece,
                    [spot, pattern, value, level_of(lower_inverse, 1)] + pieces + fetched[0],
                    scalars=2,
                    scratch=[pltpu.VMEM((near * lines, share, size), jnp.bfloat16)],
                )
            else:
                fold_lower(level, False, stack)
                for earlier in range(level):
                    value = step(value, [(fetched[earlier], forward[pair_index(level, earlier)])])
            stack = deep(settle(value), lambda sign: fold_lower(level, True, sign))
            if level == top - 1:
                stack = after(stack, *high_one)
            fetched[level] = wide(stack)
        fold_lower(top, True, stack)

        for level in reversed(range(levels)):
            value = ends[level]
            if level == 0:
                results = collect(jnp.concatenate([solved[k] for k in range(1, levels)], axis=0))
                value = after(value, *results)
            for earlier in range(level):
                value = step(value, [(fetched[earlier], backward[pair_index(level, earlier)])])
            for later in reversed(range(level + 1, levels)):
                value = step(value, [(back[later], upward[later, level])])
            solved[level] = settle(value)
            if level > 0:
                found = solved[level]
                if level == 1:
                    found = after(found, *high_rest)
                stack = deep(found)
                back[level] = wide(stack)
                for later in range(level, levels):
                    fold_upper(later, level - 1, stack)
        shape = jax.ShapeDtypeStruct((levels, 1, size, width), jnp.bfloat16)
        whole = call(
            functools.partial(late_kernel, levels, chips),
            shape,
            [spot] + results,
            scalars=1,
            scratch=[turned],
        )
        operands = [spot, (whole, pl.BlockSpec(memory_space=pl.ANY))] + collect(solved[0])
        return call(
            functools.partial(last_kernel, chips),
            shape,
            operands,
            scalars=1,
            scratch=[turned],
            out_spec=pl.BlockSpec((1, 1, size, width), lambda step: (0, 0, 0, 0)),
            aliases={1: 0},
        )

    return body


def solution(mesh):
    placed = (
        P(None, "prow", None, None),
        P(None, "prow", None, "pcol"),
        P(None, "prow", None, "pcol"),
        P(None, "prow", None, None),
        P(None, "prow", None, None),
        P(),
    )
    return jax.shard_map(
        make_body(mesh.shape["prow"], mesh.shape["pcol"]),
        mesh=mesh,
        in_specs=placed,
        out_specs=P(None, "prow", None, None),
        check_vma=False,
    )
```

```python
import functools

import jax
import jax.numpy as jnp
from jax import lax
from jax.experimental import pallas as pl
from jax.experimental.pallas import tpu as pltpu
from jax.sharding import PartitionSpec as P

CORES = 2
ROW, CHIP, CORE, DEPTH, LINE = range(5)
VMEM_BYTES = 40 * 1024 * 1024
FULL_BYTES = 58 * 1024 * 1024


def pair_index(later, earlier):
    return later * (later - 1) // 2 + earlier


def exact(left, right):
    return jnp.dot(left, right, preferred_element_type=jnp.float32)


def split(values, count):
    parts = []
    for _ in range(count):
        part = values.astype(jnp.bfloat16)
        parts.append(part)
        values = values - part.astype(jnp.float32)
    return parts


def level_of(array, level):
    shape = (1,) + array.shape[1:]
    return array, pl.BlockSpec(shape, lambda step: (level,) + (0,) * (len(shape) - 1))


def call(kernel, shapes, operands, scalars=0, scratch=(), room=VMEM_BYTES, out_spec=None, aliases=None):
    arrays, specs = [], []
    for place, operand in enumerate(operands):
        if isinstance(operand, tuple):
            array, spec = operand
        else:
            array = operand
            space = pltpu.SMEM if place < scalars else pltpu.VMEM
            spec = pl.BlockSpec(memory_space=space)
        arrays.append(array)
        specs.append(spec)
    return pl.pallas_call(
        kernel,
        grid=(1,),
        out_shape=shapes,
        in_specs=specs,
        out_specs=out_spec
        or jax.tree.map(lambda _: pl.BlockSpec(memory_space=pltpu.VMEM), shapes),
        input_output_aliases=aliases or {},
        scratch_shapes=list(scratch),
        compiler_params=pltpu.CompilerParams(vmem_limit_bytes=room),
    )(*arrays)


def share_of(values, turned, share, chip):
    turned[...] = values.T
    return turned[pl.ds(pl.multiple_of(chip * share, share), share), :]


def first_kernel(share, spot, rhs, inverse, out, turned):
    value = exact(inverse[0, 0], rhs[0, 0])
    out[...] = share_of(value, turned, share, spot[CHIP]).astype(out.dtype)


def panel_kernel(share, levels, spot, first, rhs, lower, upper, *rest):
    outs, turned = rest[:-1], rest[-1]
    chip = spot[CHIP]
    mine = spot[CORE] == 0
    value = lax.dot_general(
        first[...], upper[0, 0], (((1,), (1,)), ((), ())), preferred_element_type=jnp.float32
    )
    outs[0][...] = jnp.where(mine, value, 0.0)
    for level in range(1, levels):
        start = exact(lower[level, 0], rhs[level, 0])
        end = sum(exact(upper[level, 0], part) for part in split(start, 3))
        outs[level][...] = jnp.where(mine, share_of(end, turned, share, chip), 0.0)
        if level < levels - 1:
            value = share_of(start, turned, share, chip)
            outs[levels + level - 1][...] = jnp.where(mine, value, 0.0)


def fold_kernel(picks, lefts, spot, pattern, *refs):
    outs = refs[-len(picks) :]
    pieces = refs[len(lefts) : -len(picks)]
    row, chip, core = spot[ROW], spot[CHIP], spot[CORE]
    depth, line = spot[DEPTH], spot[LINE]
    size = outs[0].shape[-1]
    group = pieces[0].shape[-1] // size
    if len(lefts) == 1:
        sides = [refs[0][lefts[0], 0]]
    else:
        sides = split(exact(refs[0][lefts[0], 0], refs[1][lefts[1], 0]), 3)
    for index, piece in enumerate(pieces):
        deep = (chip ^ index) * CORES + core
        turn = (deep // CORES) ^ (depth // CORES)
        for across in range(group):
            block = deep * group + across
            slot = (across ^ line) * len(pieces) + turn
            columns = slice(across * size, (across + 1) * size)
            for pick, out in zip(picks, outs):
                pair, first, is_upper = pick
                keep = pattern[pair, block, row] if is_upper else pattern[pair, row, block]
                matrix = piece[pair - first if index else pair, 0, :, columns]
                matrix = jnp.where(keep > 0, matrix, jnp.zeros_like(matrix))
                folded = sum(exact(part, matrix) for part in sides).T
                for low, part in enumerate(split(folded, 2)):
                    out[slot, low] = part


def direct_kernel(pair, lines, chips, spot, pattern, base, inverse, *refs):
    pieces, stacks, out, blocks = refs[:chips], refs[chips:-2], refs[-2], refs[-1]
    row, chip, core = spot[ROW], spot[CHIP], spot[CORE]
    depth, line = spot[DEPTH], spot[LINE]
    share, size = base.shape
    for index, stack in enumerate(stacks):
        for turn in range(chips):
            blocks[index * chips + turn] = stack[turn * share : (turn + 1) * share, :]

    def times(left, right):
        return lax.dot_general(
            left, right, (((1,), (1,)), ((), ())), preferred_element_type=jnp.float32
        )

    total = jnp.zeros((share, size), jnp.float32)
    for index, piece in enumerate(pieces):
        deep = (chip ^ index) * CORES + core
        turn = (deep // CORES) ^ (depth // CORES)
        for across in range(lines):
            keep = pattern[pair, row, deep * lines + across]
            matrix = piece[pair, 0, :, across * size : (across + 1) * size]
            matrix = jnp.where(keep > 0, matrix, jnp.zeros_like(matrix))
            total = total + times(blocks[(across ^ line) * chips + turn], matrix)
    value = base[...]
    for part in split(total, 3):
        value = value - times(part, inverse[1, 0])
    out[...] = value


def step_kernel(lines, base, *refs):
    out = refs[-1]
    refs = refs[:-1]
    total = base[...]
    share = total.shape[0]
    for term in range(len(refs) // (lines + 1)):
        stacks = refs[term * (lines + 1) :][:lines]
        matrix = refs[term * (lines + 1) + lines]
        each = matrix.shape[0] // lines
        for line in range(lines):
            for index in range(each):
                block = stacks[line][index * share : (index + 1) * share, :]
                for low in range(2):
                    total = total - exact(block, matrix[line * each + index, low])
    out[...] = total


def late_kernel(levels, chips, spot, *refs):
    out, turned = refs[-2], refs[-1]
    share = turned.shape[0] // chips
    out[0] = jnp.zeros_like(out[0])
    for level in range(1, levels):
        for b in range(chips):
            at = pl.ds(pl.multiple_of((spot[CHIP] ^ b) * share, share), share)
            part = refs[b][(level - 1) * share : level * share, :]
            turned[at, :] = part.astype(jnp.float32)
        out[level, 0] = turned[...].T.astype(out.dtype)


def last_kernel(chips, spot, whole, *refs):
    out, turned = refs[-2], refs[-1]
    share = turned.shape[0] // chips
    for b in range(chips):
        at = pl.ds(pl.multiple_of((spot[CHIP] ^ b) * share, share), share)
        turned[at, :] = refs[b][...].astype(jnp.float32)
    out[0, 0] = turned[...].T.astype(out.dtype)


def make_body(rows, cols):
    chips = cols // CORES
    lines = chips
    depths = rows // lines
    near = depths // CORES
    assert near == chips

    def send(value, source_of):
        pairs = []
        for z in range(depths):
            for y in range(lines):
                for x in range(chips):
                    for core in range(CORES):
                        a, b, c, d = source_of(z, y, x, core)
                        pairs.append(
                            (
                                (a * lines + b) * cols + c * CORES + d,
                                (z * lines + y) * cols + x * CORES + core,
                            )
                        )
        return lax.ppermute(value, ("prow", "pcol"), pairs)

    def after(value, *signs):
        return lax.optimization_barrier((value,) + signs)[0]

    def body(right_side, lower_blocks, upper_blocks, lower_inverse, upper_inverse, pattern):
        levels, _, size, width = right_side.shape
        share = width // chips
        row = lax.axis_index("prow")
        col = lax.axis_index("pcol")
        line, core = row % lines, col % CORES
        spot = jnp.stack([row, col // CORES, core, row // lines, line]).astype(jnp.int32)
        top = levels - 1
        piece = jax.ShapeDtypeStruct((share, size), jnp.float32)
        chunk = jax.ShapeDtypeStruct((share, size), jnp.bfloat16)
        turned = pltpu.VMEM((width, size), jnp.float32)

        def relay(blocks):
            return [
                send(blocks, lambda z, y, x, core, b=b: (z, y, x ^ b, core))
                for b in range(1, chips)
            ]

        def fold(picks, lefts, inverses, pieces, sign):
            shape = jax.ShapeDtypeStruct((near * lines, 2, size, size), jnp.bfloat16)
            return call(
                functools.partial(fold_kernel, picks, lefts),
                [shape] * len(picks),
                [after(spot, sign), pattern] + inverses + pieces,
                scalars=2,
            )

        def deep(value, work=None):
            found = [value]
            for m in range(1, depths):
                found.append(send(value, lambda z, y, x, core, m=m: (z ^ m, y, x, core)))
            parts = [
                jnp.where((row // lines) % CORES == core, found[m], found[m + 1])
                for m in range(0, depths, CORES)
            ]
            stack = jnp.concatenate(parts, axis=0)
            return after(stack, *work(found[1])) if work else stack

        def wide(stack):
            return [stack] + [
                send(stack, lambda z, y, x, core, e=e: (z, y ^ e, x, core)) for e in range(1, lines)
            ]

        def settle(partial_value):
            other = send(partial_value, lambda z, y, x, core: (z, y, x, 1 - core))
            return (partial_value + other).astype(jnp.bfloat16)

        def collect(value):
            return [value] + [
                send(value, lambda z, y, x, core, b=b: (z, y, x ^ b, core)) for b in range(1, chips)
            ]

        def step(base, terms):
            operands = [base]
            for stacks, matrix in terms:
                operands += stacks + [matrix]
            return call(functools.partial(step_kernel, lines), piece, operands)

        first = call(
            functools.partial(first_kernel, share),
            chunk,
            [spot, level_of(right_side, 0), level_of(lower_inverse, 0)],
            scalars=1,
            scratch=[turned],
            room=FULL_BYTES,
        )
        panels = call(
            functools.partial(panel_kernel, share, levels),
            [piece] * (2 * levels - 2),
            [spot, first, right_side, lower_inverse, upper_inverse],
            scalars=1,
            scratch=[turned],
        )
        ends, starts = panels[:levels], [None] + list(panels[levels:])

        low_all = relay(lower_blocks)
        last_pair = pair_index(top, top - 1)
        parts = (upper_blocks[last_pair:], upper_blocks[:last_pair])
        stack = deep(first, lambda sign: panels)
        stack, upper_one, upper_rest = lax.optimization_barrier((stack,) + parts)
        high_one = relay(upper_one)
        high_rest = relay(upper_rest)

        def fold_lower(later, both, sign):
            pairs = [pair_index(later, e) for e in range(later)]
            picks = tuple((pair, 0, False) for pair in pairs)
            inverses = [upper_inverse, lower_inverse] if both else [lower_inverse]
            lefts = (later,) * len(inverses)
            found = fold(picks, lefts, inverses, [lower_blocks] + low_all, sign)
            found = dict(zip(pairs, found))
            (backward if both else forward).update(found)
            return list(found.values())

        def fold_upper(later, earlier, sign):
            pair = pair_index(later, earlier)
            picks = ((pair, pair if pair == last_pair else 0, True),)
            moved = high_one if pair == last_pair else high_rest
            found = fold(picks, (earlier,), [upper_inverse], [upper_blocks] + moved, sign)[0]
            upward[later, earlier] = found
            return [found]

        fetched, back, solved = {}, {}, {}
        forward, backward, upward = {}, {}, {}
        fetched[0] = wide(stack)
        for level in range(1, top):
            value = starts[level]
            if level == 1:
                pieces = [lower_blocks] + low_all
                value = call(
                    functools.partial(direct_kernel, 0, lines, chips),
                    piece,
                    [spot, pattern, value, lower_inverse] + pieces + fetched[0],
                    scalars=2,
                    scratch=[pltpu.VMEM((near * lines, share, size), jnp.bfloat16)],
                )
            else:
                fold_lower(level, False, stack)
                for earlier in range(level):
                    value = step(value, [(fetched[earlier], forward[pair_index(level, earlier)])])
            stack = deep(settle(value), lambda sign: fold_lower(level, True, sign))
            if level == top - 1:
                stack = after(stack, *high_one)
            fetched[level] = wide(stack)
        fold_lower(top, True, stack)

        for level in reversed(range(levels)):
            value = ends[level]
            if level == 0:
                results = collect(jnp.concatenate([solved[k] for k in range(1, levels)], axis=0))
                value = after(value, *results)
            for earlier in range(level):
                value = step(value, [(fetched[earlier], backward[pair_index(level, earlier)])])
            for later in reversed(range(level + 1, levels)):
                value = step(value, [(back[later], upward[later, level])])
            solved[level] = settle(value)
            if level > 0:
                found = solved[level]
                if level == 1:
                    found = after(found, *high_rest)
                stack = deep(found)
                back[level] = wide(stack)
                for later in range(level, levels):
                    fold_upper(later, level - 1, stack)
        shape = jax.ShapeDtypeStruct((levels, 1, size, width), jnp.bfloat16)
        whole = call(
            functools.partial(late_kernel, levels, chips),
            shape,
            [spot] + results,
            scalars=1,
            scratch=[turned],
        )
        operands = [spot, (whole, pl.BlockSpec(memory_space=pl.ANY))] + collect(solved[0])
        return call(
            functools.partial(last_kernel, chips),
            shape,
            operands,
            scalars=1,
            scratch=[turned],
            out_spec=pl.BlockSpec((1, 1, size, width), lambda step: (0, 0, 0, 0)),
            aliases={1: 0},
        )

    return body


def solution(mesh):
    placed = (
        P(None, "prow", None, None),
        P(None, "prow", None, "pcol"),
        P(None, "prow", None, "pcol"),
        P(None, "prow", None, None),
        P(None, "prow", None, None),
        P(),
    )
    return jax.shard_map(
        make_body(mesh.shape["prow"], mesh.shape["pcol"]),
        mesh=mesh,
        in_specs=placed,
        out_specs=P(None, "prow", None, None),
        check_vma=False,
    )
```

```python
import functools

import jax
import jax.numpy as jnp
from jax import lax
from jax.experimental import pallas as pl
from jax.experimental.pallas import tpu as pltpu
from jax.sharding import PartitionSpec as P

CORES = 2
ROW, CHIP, CORE, DEPTH, LINE = range(5)
VMEM_BYTES = 40 * 1024 * 1024
FULL_BYTES = 58 * 1024 * 1024


def pair_index(later, earlier):
    return later * (later - 1) // 2 + earlier


def exact(left, right):
    return jnp.dot(left, right, preferred_element_type=jnp.float32)


def split(values, count):
    parts = []
    for _ in range(count):
        part = values.astype(jnp.bfloat16)
        parts.append(part)
        values = values - part.astype(jnp.float32)
    return parts


def level_of(array, level):
    shape = (1,) + array.shape[1:]
    return array, pl.BlockSpec(shape, lambda step: (level,) + (0,) * (len(shape) - 1))


def call(kernel, shapes, operands, scalars=0, scratch=(), room=VMEM_BYTES, out_spec=None, aliases=None):
    arrays, specs = [], []
    for place, operand in enumerate(operands):
        if isinstance(operand, tuple):
            array, spec = operand
        else:
            array = operand
            space = pltpu.SMEM if place < scalars else pltpu.VMEM
            spec = pl.BlockSpec(memory_space=space)
        arrays.append(array)
        specs.append(spec)
    return pl.pallas_call(
        kernel,
        grid=(1,),
        out_shape=shapes,
        in_specs=specs,
        out_specs=out_spec
        or jax.tree.map(lambda _: pl.BlockSpec(memory_space=pltpu.VMEM), shapes),
        input_output_aliases=aliases or {},
        scratch_shapes=list(scratch),
        compiler_params=pltpu.CompilerParams(vmem_limit_bytes=room),
    )(*arrays)


def share_of(values, turned, share, chip):
    turned[...] = values.T
    return turned[pl.ds(pl.multiple_of(chip * share, share), share), :]


def first_kernel(share, spot, rhs, inverse, out, turned):
    value = exact(inverse[0, 0], rhs[0, 0])
    out[...] = share_of(value, turned, share, spot[CHIP]).astype(out.dtype)


def panel_kernel(share, levels, spot, first, rhs, lower, upper, *rest):
    outs, turned = rest[:-1], rest[-1]
    chip = spot[CHIP]
    mine = spot[CORE] == 0
    value = lax.dot_general(
        first[...], upper[0, 0], (((1,), (1,)), ((), ())), preferred_element_type=jnp.float32
    )
    outs[0][...] = jnp.where(mine, value, 0.0)
    for level in range(1, levels):
        start = exact(lower[level, 0], rhs[level, 0])
        end = sum(exact(upper[level, 0], part) for part in split(start, 3))
        outs[level][...] = jnp.where(mine, share_of(end, turned, share, chip), 0.0)
        if level < levels - 1:
            value = share_of(start, turned, share, chip)
            outs[levels + level - 1][...] = jnp.where(mine, value, 0.0)


def fold_kernel(picks, left_count, spot, pattern, *refs):
    outs = refs[-len(picks) :]
    pieces = refs[left_count : -len(picks)]
    row, chip, core = spot[ROW], spot[CHIP], spot[CORE]
    depth, line = spot[DEPTH], spot[LINE]
    size = outs[0].shape[-1]
    group = pieces[0].shape[-1] // size
    if left_count == 1:
        sides = [refs[0][0, 0]]
    else:
        sides = split(exact(refs[0][0, 0], refs[1][0, 0]), 3)
    for index, piece in enumerate(pieces):
        deep = (chip ^ index) * CORES + core
        turn = (deep // CORES) ^ (depth // CORES)
        for across in range(group):
            block = deep * group + across
            slot = (across ^ line) * len(pieces) + turn
            columns = slice(across * size, (across + 1) * size)
            for pick, out in zip(picks, outs):
                pair, first, is_upper = pick
                keep = pattern[pair, block, row] if is_upper else pattern[pair, row, block]
                matrix = piece[pair - first if index else pair, 0, :, columns]
                matrix = jnp.where(keep > 0, matrix, jnp.zeros_like(matrix))
                folded = sum(exact(part, matrix) for part in sides).T
                for low, part in enumerate(split(folded, 2)):
                    out[slot, low] = part


def direct_kernel(pair, lines, chips, spot, pattern, base, inverse, *refs):
    pieces, stacks, out, blocks = refs[:chips], refs[chips:-2], refs[-2], refs[-1]
    row, chip, core = spot[ROW], spot[CHIP], spot[CORE]
    depth, line = spot[DEPTH], spot[LINE]
    share = base.shape[0]
    size = base.shape[1]
    for index, stack in enumerate(stacks):
        for turn in range(chips):
            block = stack[turn * share : (turn + 1) * share, :].astype(jnp.float32)
            blocks[index * chips + turn] = block.T.astype(jnp.bfloat16)
    total = jnp.zeros((size, share), jnp.float32)
    for index, piece in enumerate(pieces):
        deep = (chip ^ index) * CORES + core
        turn = (deep // CORES) ^ (depth // CORES)
        for across in range(lines):
            keep = pattern[pair, row, deep * lines + across]
            block = blocks[(across ^ line) * chips + turn]
            block = jnp.where(keep > 0, block, jnp.zeros_like(block))
            columns = slice(across * size, (across + 1) * size)
            total = total + exact(piece[0, 0, :, columns], block)
    value = sum(exact(inverse[0, 0], part) for part in split(total, 3))
    out[...] = base[...] - value.T


def step_kernel(lines, base, *refs):
    out = refs[-1]
    refs = refs[:-1]
    total = base[...]
    share = total.shape[0]
    for term in range(len(refs) // (lines + 1)):
        stacks = refs[term * (lines + 1) :][:lines]
        matrix = refs[term * (lines + 1) + lines]
        each = matrix.shape[0] // lines
        for line in range(lines):
            for index in range(each):
                block = stacks[line][index * share : (index + 1) * share, :]
                for low in range(2):
                    total = total - exact(block, matrix[line * each + index, low])
    out[...] = total


def late_kernel(levels, chips, spot, *refs):
    out, turned = refs[-2], refs[-1]
    share = turned.shape[0] // chips
    out[0] = jnp.zeros_like(out[0])
    for level in range(1, levels):
        for b in range(chips):
            at = pl.ds(pl.multiple_of((spot[CHIP] ^ b) * share, share), share)
            part = refs[b][(level - 1) * share : level * share, :]
            turned[at, :] = part.astype(jnp.float32)
        out[level, 0] = turned[...].T.astype(out.dtype)


def last_kernel(chips, spot, whole, *refs):
    out, turned = refs[-2], refs[-1]
    share = turned.shape[0] // chips
    for b in range(chips):
        at = pl.ds(pl.multiple_of((spot[CHIP] ^ b) * share, share), share)
        turned[at, :] = refs[b][...].astype(jnp.float32)
    out[0, 0] = turned[...].T.astype(out.dtype)


def make_body(rows, cols):
    chips = cols // CORES
    lines = chips
    depths = rows // lines
    near = depths // CORES
    assert near == chips

    def send(value, source_of):
        pairs = []
        for z in range(depths):
            for y in range(lines):
                for x in range(chips):
                    for core in range(CORES):
                        a, b, c, d = source_of(z, y, x, core)
                        pairs.append(
                            (
                                (a * lines + b) * cols + c * CORES + d,
                                (z * lines + y) * cols + x * CORES + core,
                            )
                        )
        return lax.ppermute(value, ("prow", "pcol"), pairs)

    def after(value, *signs):
        return lax.optimization_barrier((value,) + signs)[0]

    def body(right_side, lower_blocks, upper_blocks, lower_inverse, upper_inverse, pattern):
        levels, _, size, width = right_side.shape
        share = width // chips
        row = lax.axis_index("prow")
        col = lax.axis_index("pcol")
        line, core = row % lines, col % CORES
        spot = jnp.stack([row, col // CORES, core, row // lines, line]).astype(jnp.int32)
        top = levels - 1
        piece = jax.ShapeDtypeStruct((share, size), jnp.float32)
        chunk = jax.ShapeDtypeStruct((share, size), jnp.bfloat16)
        turned = pltpu.VMEM((width, size), jnp.float32)

        def relay(blocks):
            return [
                send(blocks, lambda z, y, x, core, b=b: (z, y, x ^ b, core))
                for b in range(1, chips)
            ]

        def fold(picks, inverses, pieces, sign):
            shape = jax.ShapeDtypeStruct((near * lines, 2, size, size), jnp.bfloat16)
            return call(
                functools.partial(fold_kernel, picks, len(inverses)),
                [shape] * len(picks),
                [after(spot, sign), pattern] + inverses + pieces,
                scalars=2,
            )

        def deep(value, work=None):
            found = [value]
            for m in range(1, depths):
                found.append(send(value, lambda z, y, x, core, m=m: (z ^ m, y, x, core)))
            parts = [
                jnp.where((row // lines) % CORES == core, found[m], found[m + 1])
                for m in range(0, depths, CORES)
            ]
            stack = jnp.concatenate(parts, axis=0)
            return after(stack, *work(found[1])) if work else stack

        def wide(stack):
            return [stack] + [
                send(stack, lambda z, y, x, core, e=e: (z, y ^ e, x, core)) for e in range(1, lines)
            ]

        def settle(partial_value):
            other = send(partial_value, lambda z, y, x, core: (z, y, x, 1 - core))
            return (partial_value + other).astype(jnp.bfloat16)

        def collect(value):
            return [value] + [
                send(value, lambda z, y, x, core, b=b: (z, y, x ^ b, core)) for b in range(1, chips)
            ]

        def step(base, terms):
            operands = [base]
            for stacks, matrix in terms:
                operands += stacks + [matrix]
            return call(functools.partial(step_kernel, lines), piece, operands)

        first = call(
            functools.partial(first_kernel, share),
            chunk,
            [spot, level_of(right_side, 0), level_of(lower_inverse, 0)],
            scalars=1,
            scratch=[turned],
            room=FULL_BYTES,
        )
        panels = call(
            functools.partial(panel_kernel, share, levels),
            [piece] * (2 * levels - 2),
            [spot, first, right_side, lower_inverse, upper_inverse],
            scalars=1,
            scratch=[turned],
        )
        ends, starts = panels[:levels], [None] + list(panels[levels:])

        low_all = relay(lower_blocks)
        last_pair = pair_index(top, top - 1)
        parts = (upper_blocks[last_pair:], upper_blocks[:last_pair])
        stack = deep(first, lambda sign: panels)
        stack, upper_one, upper_rest = lax.optimization_barrier((stack,) + parts)
        high_one = relay(upper_one)
        high_rest = relay(upper_rest)

        def fold_lower(later, both, sign):
            pairs = [pair_index(later, e) for e in range(later)]
            picks = tuple((pair, 0, False) for pair in pairs)
            inverses = [level_of(lower_inverse, later)]
            if both:
                inverses = [level_of(upper_inverse, later)] + inverses
            found = dict(zip(pairs, fold(picks, inverses, [lower_blocks] + low_all, sign)))
            (backward if both else forward).update(found)
            return list(found.values())

        def fold_upper(later, earlier, sign):
            pair = pair_index(later, earlier)
            picks = ((pair, pair if pair == last_pair else 0, True),)
            moved = high_one if pair == last_pair else high_rest
            inverses = [level_of(upper_inverse, earlier)]
            found = fold(picks, inverses, [upper_blocks] + moved, sign)[0]
            upward[later, earlier] = found
            return [found]

        fetched, back, solved = {}, {}, {}
        forward, backward, upward = {}, {}, {}
        fetched[0] = wide(stack)
        for level in range(1, top):
            value = starts[level]
            if level == 1:
                pieces = [level_of(blocks, 0) for blocks in [lower_blocks] + low_all]
                value = call(
                    functools.partial(direct_kernel, 0, lines, chips),
                    piece,
                    [spot, pattern, value, level_of(lower_inverse, 1)] + pieces + fetched[0],
                    scalars=2,
                    scratch=[pltpu.VMEM((near * lines, size, share), jnp.bfloat16)],
                )
            else:
                fold_lower(level, False, stack)
                for earlier in range(level):
                    value = step(value, [(fetched[earlier], forward[pair_index(level, earlier)])])
            stack = deep(settle(value), lambda sign: fold_lower(level, True, sign))
            if level == top - 1:
                stack = after(stack, *high_one)
            fetched[level] = wide(stack)
        fold_lower(top, True, stack)

        for level in reversed(range(levels)):
            value = ends[level]
            if level == 0:
                results = collect(jnp.concatenate([solved[k] for k in range(1, levels)], axis=0))
                value = after(value, *results)
            for earlier in range(level):
                value = step(value, [(fetched[earlier], backward[pair_index(level, earlier)])])
            for later in reversed(range(level + 1, levels)):
                value = step(value, [(back[later], upward[later, level])])
            solved[level] = settle(value)
            if level > 0:
                found = solved[level]
                if level == 1:
                    found = after(found, *high_rest)
                stack = deep(found)
                back[level] = wide(stack)
                for later in range(level, levels):
                    fold_upper(later, level - 1, stack)
        shape = jax.ShapeDtypeStruct((levels, 1, size, width), jnp.bfloat16)
        whole = call(
            functools.partial(late_kernel, levels, chips),
            shape,
            [spot] + results,
            scalars=1,
            scratch=[turned],
        )
        operands = [spot, (whole, pl.BlockSpec(memory_space=pl.ANY))] + collect(solved[0])
        return call(
            functools.partial(last_kernel, chips),
            shape,
            operands,
            scalars=1,
            scratch=[turned],
            out_spec=pl.BlockSpec((1, 1, size, width), lambda step: (0, 0, 0, 0)),
            aliases={1: 0},
        )

    return body


def solution(mesh):
    placed = (
        P(None, "prow", None, None),
        P(None, "prow", None, "pcol"),
        P(None, "prow", None, "pcol"),
        P(None, "prow", None, None),
        P(None, "prow", None, None),
        P(),
    )
    return jax.shard_map(
        make_body(mesh.shape["prow"], mesh.shape["pcol"]),
        mesh=mesh,
        in_specs=placed,
        out_specs=P(None, "prow", None, None),
        check_vma=False,
    )
```

```python
import functools

import jax
import jax.numpy as jnp
from jax import lax
from jax.experimental import pallas as pl
from jax.experimental.pallas import tpu as pltpu
from jax.sharding import PartitionSpec as P

CORES = 2
ROW, CHIP, CORE, DEPTH, LINE = range(5)
VMEM_BYTES = 40 * 1024 * 1024
FULL_BYTES = 58 * 1024 * 1024


def pair_index(later, earlier):
    return later * (later - 1) // 2 + earlier


def exact(left, right):
    return jnp.dot(left, right, preferred_element_type=jnp.float32)


def split(values, count):
    parts = []
    for _ in range(count):
        part = values.astype(jnp.bfloat16)
        parts.append(part)
        values = values - part.astype(jnp.float32)
    return parts


def level_of(array, level):
    shape = (1,) + array.shape[1:]
    return array, pl.BlockSpec(shape, lambda step: (level,) + (0,) * (len(shape) - 1))


def call(kernel, shapes, operands, scalars=0, scratch=(), room=VMEM_BYTES, out_spec=None, aliases=None):
    arrays, specs = [], []
    for place, operand in enumerate(operands):
        if isinstance(operand, tuple):
            array, spec = operand
        else:
            array = operand
            space = pltpu.SMEM if place < scalars else pltpu.VMEM
            spec = pl.BlockSpec(memory_space=space)
        arrays.append(array)
        specs.append(spec)
    return pl.pallas_call(
        kernel,
        grid=(1,),
        out_shape=shapes,
        in_specs=specs,
        out_specs=out_spec
        or jax.tree.map(lambda _: pl.BlockSpec(memory_space=pltpu.VMEM), shapes),
        input_output_aliases=aliases or {},
        scratch_shapes=list(scratch),
        compiler_params=pltpu.CompilerParams(vmem_limit_bytes=room),
    )(*arrays)


def share_of(values, turned, share, chip):
    turned[...] = values.T
    return turned[pl.ds(pl.multiple_of(chip * share, share), share), :]


def first_kernel(share, spot, rhs, inverse, out, turned):
    value = exact(inverse[0, 0], rhs[0, 0])
    out[...] = share_of(value, turned, share, spot[CHIP]).astype(out.dtype)


def panel_kernel(share, levels, spot, first, rhs, lower, upper, *rest):
    outs, turned = rest[:-1], rest[-1]
    chip = spot[CHIP]
    mine = spot[CORE] == 0
    value = lax.dot_general(
        first[...], upper[0, 0], (((1,), (1,)), ((), ())), preferred_element_type=jnp.float32
    )
    outs[0][...] = jnp.where(mine, value, 0.0)
    for level in range(1, levels):
        start = exact(lower[level, 0], rhs[level, 0])
        end = sum(exact(upper[level, 0], part) for part in split(start, 3))
        outs[level][...] = jnp.where(mine, share_of(end, turned, share, chip), 0.0)
        if level < levels - 1:
            value = share_of(start, turned, share, chip)
            outs[levels + level - 1][...] = jnp.where(mine, value, 0.0)


def fold_kernel(picks, left_count, spot, pattern, *refs):
    outs = refs[-len(picks) :]
    pieces = refs[left_count : -len(picks)]
    row, chip, core = spot[ROW], spot[CHIP], spot[CORE]
    depth, line = spot[DEPTH], spot[LINE]
    size = outs[0].shape[-1]
    group = pieces[0].shape[-1] // size
    if left_count == 1:
        sides = [refs[0][0, 0]]
    else:
        sides = split(exact(refs[0][0, 0], refs[1][0, 0]), 3)
    for index, piece in enumerate(pieces):
        deep = (chip ^ index) * CORES + core
        turn = (deep // CORES) ^ (depth // CORES)
        for across in range(group):
            block = deep * group + across
            slot = (across ^ line) * len(pieces) + turn
            columns = slice(across * size, (across + 1) * size)
            for pick, out in zip(picks, outs):
                pair, first, is_upper = pick
                keep = pattern[pair, block, row] if is_upper else pattern[pair, row, block]
                matrix = piece[pair - first if index else pair, 0, :, columns]
                matrix = jnp.where(keep > 0, matrix, jnp.zeros_like(matrix))
                folded = sum(exact(part, matrix) for part in sides).T
                for low, part in enumerate(split(folded, 2)):
                    out[slot, low] = part


def direct_kernel(pair, lines, chips, spot, pattern, base, inverse, *refs):
    pieces, stacks, out, blocks = refs[:chips], refs[chips:-2], refs[-2], refs[-1]
    row, chip, core = spot[ROW], spot[CHIP], spot[CORE]
    depth, line = spot[DEPTH], spot[LINE]
    share, size = base.shape
    for index, stack in enumerate(stacks):
        for turn in range(chips):
            blocks[index * chips + turn] = stack[turn * share : (turn + 1) * share, :]

    def times(left, right):
        return lax.dot_general(
            left, right, (((1,), (1,)), ((), ())), preferred_element_type=jnp.float32
        )

    total = jnp.zeros((share, size), jnp.float32)
    for index, piece in enumerate(pieces):
        deep = (chip ^ index) * CORES + core
        turn = (deep // CORES) ^ (depth // CORES)
        for across in range(lines):
            keep = pattern[pair, row, deep * lines + across]
            matrix = piece[0, 0, :, across * size : (across + 1) * size]
            matrix = jnp.where(keep > 0, matrix, jnp.zeros_like(matrix))
            total = total + times(blocks[(across ^ line) * chips + turn], matrix)
    value = base[...]
    for part in split(total, 3):
        value = value - times(part, inverse[0, 0])
    out[...] = value


def step_kernel(lines, base, *refs):
    out = refs[-1]
    refs = refs[:-1]
    total = base[...]
    share = total.shape[0]
    for term in range(len(refs) // (lines + 1)):
        stacks = refs[term * (lines + 1) :][:lines]
        matrix = refs[term * (lines + 1) + lines]
        each = matrix.shape[0] // lines
        for line in range(lines):
            for index in range(each):
                block = stacks[line][index * share : (index + 1) * share, :]
                for low in range(2):
                    total = total - exact(block, matrix[line * each + index, low])
    out[...] = total


def late_kernel(levels, chips, spot, *refs):
    out, turned = refs[-2], refs[-1]
    share = turned.shape[0] // chips
    out[0] = jnp.zeros_like(out[0])
    for level in range(1, levels):
        for b in range(chips):
            at = pl.ds(pl.multiple_of((spot[CHIP] ^ b) * share, share), share)
            part = refs[b][(level - 1) * share : level * share, :]
            turned[at, :] = part.astype(jnp.float32)
        out[level, 0] = turned[...].T.astype(out.dtype)


def last_kernel(chips, spot, whole, *refs):
    out, turned = refs[-2], refs[-1]
    share = turned.shape[0] // chips
    for b in range(chips):
        at = pl.ds(pl.multiple_of((spot[CHIP] ^ b) * share, share), share)
        turned[at, :] = refs[b][...].astype(jnp.float32)
    out[0, 0] = turned[...].T.astype(out.dtype)


def make_body(rows, cols):
    chips = cols // CORES
    lines = chips
    depths = rows // lines
    near = depths // CORES
    assert near == chips

    def send(value, source_of):
        pairs = []
        for z in range(depths):
            for y in range(lines):
                for x in range(chips):
                    for core in range(CORES):
                        a, b, c, d = source_of(z, y, x, core)
                        pairs.append(
                            (
                                (a * lines + b) * cols + c * CORES + d,
                                (z * lines + y) * cols + x * CORES + core,
                            )
                        )
        return lax.ppermute(value, ("prow", "pcol"), pairs)

    def after(value, *signs):
        return lax.optimization_barrier((value,) + signs)[0]

    def body(right_side, lower_blocks, upper_blocks, lower_inverse, upper_inverse, pattern):
        levels, _, size, width = right_side.shape
        share = width // chips
        row = lax.axis_index("prow")
        col = lax.axis_index("pcol")
        line, core = row % lines, col % CORES
        spot = jnp.stack([row, col // CORES, core, row // lines, line]).astype(jnp.int32)
        top = levels - 1
        piece = jax.ShapeDtypeStruct((share, size), jnp.float32)
        chunk = jax.ShapeDtypeStruct((share, size), jnp.bfloat16)
        turned = pltpu.VMEM((width, size), jnp.float32)

        def relay(blocks):
            return [
                send(blocks, lambda z, y, x, core, b=b: (z, y, x ^ b, core))
                for b in range(1, chips)
            ]

        def fold(picks, inverses, pieces, sign):
            shape = jax.ShapeDtypeStruct((near * lines, 2, size, size), jnp.bfloat16)
            return call(
                functools.partial(fold_kernel, picks, len(inverses)),
                [shape] * len(picks),
                [after(spot, sign), pattern] + inverses + pieces,
                scalars=2,
            )

        def deep(value, work=None):
            even = (row // lines) % CORES == core
            found = []
            for t in range(near):

                def source(z, y, x, core, t=t):
                    m = CORES * t + 1
                    if z % CORES == core and t < near - 1:
                        return z ^ (m + 1), y, x, core
                    return z ^ m, y, x, 1 - core

                found.append(send(value, source))
            parts = [jnp.where(even, ([value] + found)[t], found[t]) for t in range(near)]
            stack = jnp.concatenate(parts, axis=0)
            return after(stack, *work(found[0])) if work else stack

        def wide(stack):
            return [stack] + [
                send(stack, lambda z, y, x, core, e=e: (z, y ^ e, x, core)) for e in range(1, lines)
            ]

        def settle(partial_value):
            other = send(partial_value, lambda z, y, x, core: (z, y, x, 1 - core))
            return (partial_value + other).astype(jnp.bfloat16)

        def collect(value):
            return [value] + [
                send(value, lambda z, y, x, core, b=b: (z, y, x ^ b, core)) for b in range(1, chips)
            ]

        def step(base, terms):
            operands = [base]
            for stacks, matrix in terms:
                operands += stacks + [matrix]
            return call(functools.partial(step_kernel, lines), piece, operands)

        first = call(
            functools.partial(first_kernel, share),
            chunk,
            [spot, level_of(right_side, 0), level_of(lower_inverse, 0)],
            scalars=1,
            scratch=[turned],
            room=FULL_BYTES,
        )
        panels = call(
            functools.partial(panel_kernel, share, levels),
            [piece] * (2 * levels - 2),
            [spot, first, right_side, lower_inverse, upper_inverse],
            scalars=1,
            scratch=[turned],
        )
        ends, starts = panels[:levels], [None] + list(panels[levels:])

        low_all = relay(lower_blocks)
        last_pair = pair_index(top, top - 1)
        parts = (upper_blocks[last_pair:], upper_blocks[:last_pair])
        stack = deep(first, lambda sign: panels)
        stack, upper_one, upper_rest = lax.optimization_barrier((stack,) + parts)
        high_one = relay(upper_one)
        high_rest = relay(upper_rest)

        def fold_lower(later, both, sign):
            pairs = [pair_index(later, e) for e in range(later)]
            picks = tuple((pair, 0, False) for pair in pairs)
            inverses = [level_of(lower_inverse, later)]
            if both:
                inverses = [level_of(upper_inverse, later)] + inverses
            found = dict(zip(pairs, fold(picks, inverses, [lower_blocks] + low_all, sign)))
            (backward if both else forward).update(found)
            return list(found.values())

        def fold_upper(later, earlier, sign):
            pair = pair_index(later, earlier)
            picks = ((pair, pair if pair == last_pair else 0, True),)
            moved = high_one if pair == last_pair else high_rest
            inverses = [level_of(upper_inverse, earlier)]
            found = fold(picks, inverses, [upper_blocks] + moved, sign)[0]
            upward[later, earlier] = found
            return [found]

        fetched, back, solved = {}, {}, {}
        forward, backward, upward = {}, {}, {}
        fetched[0] = wide(stack)
        for level in range(1, top):
            value = starts[level]
            if level == 1:
                pieces = [level_of(blocks, 0) for blocks in [lower_blocks] + low_all]
                value = call(
                    functools.partial(direct_kernel, 0, lines, chips),
                    piece,
                    [spot, pattern, value, level_of(lower_inverse, 1)] + pieces + fetched[0],
                    scalars=2,
                    scratch=[pltpu.VMEM((near * lines, share, size), jnp.bfloat16)],
                )
            else:
                fold_lower(level, False, stack)
                for earlier in range(level):
                    value = step(value, [(fetched[earlier], forward[pair_index(level, earlier)])])
            stack = deep(settle(value), lambda sign: fold_lower(level, True, sign))
            if level == top - 1:
                stack = after(stack, *high_one)
            fetched[level] = wide(stack)
        fold_lower(top, True, stack)

        for level in reversed(range(levels)):
            value = ends[level]
            if level == 0:
                results = collect(jnp.concatenate([solved[k] for k in range(1, levels)], axis=0))
                value = after(value, *results)
            for earlier in range(level):
                value = step(value, [(fetched[earlier], backward[pair_index(level, earlier)])])
            for later in reversed(range(level + 1, levels)):
                value = step(value, [(back[later], upward[later, level])])
            solved[level] = settle(value)
            if level > 0:
                found = solved[level]
                if level == 1:
                    found = after(found, *high_rest)
                stack = deep(found)
                back[level] = wide(stack)
                for later in range(level, levels):
                    fold_upper(later, level - 1, stack)
        shape = jax.ShapeDtypeStruct((levels, 1, size, width), jnp.bfloat16)
        whole = call(
            functools.partial(late_kernel, levels, chips),
            shape,
            [spot] + results,
            scalars=1,
            scratch=[turned],
        )
        operands = [spot, (whole, pl.BlockSpec(memory_space=pl.ANY))] + collect(solved[0])
        return call(
            functools.partial(last_kernel, chips),
            shape,
            operands,
            scalars=1,
            scratch=[turned],
            out_spec=pl.BlockSpec((1, 1, size, width), lambda step: (0, 0, 0, 0)),
            aliases={1: 0},
        )

    return body


def solution(mesh):
    placed = (
        P(None, "prow", None, None),
        P(None, "prow", None, "pcol"),
        P(None, "prow", None, "pcol"),
        P(None, "prow", None, None),
        P(None, "prow", None, None),
        P(),
    )
    return jax.shard_map(
        make_body(mesh.shape["prow"], mesh.shape["pcol"]),
        mesh=mesh,
        in_specs=placed,
        out_specs=P(None, "prow", None, None),
        check_vma=False,
    )
```

```python
import functools

import jax
import jax.numpy as jnp
from jax import lax
from jax.experimental import pallas as pl
from jax.experimental.pallas import tpu as pltpu
from jax.sharding import PartitionSpec as P

CORES = 2
ROW, CHIP, CORE, DEPTH, LINE = range(5)
VMEM_BYTES = 40 * 1024 * 1024
FULL_BYTES = 58 * 1024 * 1024


def pair_index(later, earlier):
    return later * (later - 1) // 2 + earlier


def exact(left, right):
    return jnp.dot(left, right, preferred_element_type=jnp.float32)


def split(values, count):
    parts = []
    for _ in range(count):
        part = values.astype(jnp.bfloat16)
        parts.append(part)
        values = values - part.astype(jnp.float32)
    return parts


def level_of(array, level):
    shape = (1,) + array.shape[1:]
    return array, pl.BlockSpec(shape, lambda step: (level,) + (0,) * (len(shape) - 1))


def call(kernel, shapes, operands, scalars=0, scratch=(), room=VMEM_BYTES, out_spec=None, aliases=None):
    arrays, specs = [], []
    for place, operand in enumerate(operands):
        if isinstance(operand, tuple):
            array, spec = operand
        else:
            array = operand
            space = pltpu.SMEM if place < scalars else pltpu.VMEM
            spec = pl.BlockSpec(memory_space=space)
        arrays.append(array)
        specs.append(spec)
    return pl.pallas_call(
        kernel,
        grid=(1,),
        out_shape=shapes,
        in_specs=specs,
        out_specs=out_spec
        or jax.tree.map(lambda _: pl.BlockSpec(memory_space=pltpu.VMEM), shapes),
        input_output_aliases=aliases or {},
        scratch_shapes=list(scratch),
        compiler_params=pltpu.CompilerParams(vmem_limit_bytes=room),
    )(*arrays)


def share_of(values, turned, share, chip):
    turned[...] = values.T
    return turned[pl.ds(pl.multiple_of(chip * share, share), share), :]


def first_kernel(share, spot, rhs, inverse, out, turned):
    value = exact(inverse[0, 0], rhs[0, 0])
    out[...] = share_of(value, turned, share, spot[CHIP]).astype(out.dtype)


def panel_kernel(share, levels, spot, first, rhs, lower, upper, *rest):
    outs, turned = rest[:-1], rest[-1]
    chip = spot[CHIP]
    mine = spot[CORE] == 0
    value = lax.dot_general(
        first[...], upper[0, 0], (((1,), (1,)), ((), ())), preferred_element_type=jnp.float32
    )
    outs[0][...] = jnp.where(mine, value, 0.0)
    for level in range(1, levels):
        start = exact(lower[level, 0], rhs[level, 0])
        end = sum(exact(upper[level, 0], part) for part in split(start, 3))
        outs[level][...] = jnp.where(mine, share_of(end, turned, share, chip), 0.0)
        if level < levels - 1:
            value = share_of(start, turned, share, chip)
            outs[levels + level - 1][...] = jnp.where(mine, value, 0.0)


def fold_kernel(picks, left_count, spot, pattern, *refs):
    outs = refs[-len(picks) :]
    pieces = refs[left_count : -len(picks)]
    row, chip, core = spot[ROW], spot[CHIP], spot[CORE]
    depth, line = spot[DEPTH], spot[LINE]
    size = outs[0].shape[-1]
    group = pieces[0].shape[-1] // size
    if left_count == 1:
        sides = [refs[0][0, 0]]
    else:
        sides = split(exact(refs[0][0, 0], refs[1][0, 0]), 3)
    for index, piece in enumerate(pieces):
        deep = (chip ^ index) * CORES + core
        turn = (deep // CORES) ^ (depth // CORES)
        for across in range(group):
            block = deep * group + across
            slot = (across ^ line) * len(pieces) + turn
            columns = slice(across * size, (across + 1) * size)
            for pick, out in zip(picks, outs):
                pair, first, is_upper = pick
                keep = pattern[pair, block, row] if is_upper else pattern[pair, row, block]
                matrix = piece[pair - first if index else pair, 0, :, columns]
                matrix = jnp.where(keep > 0, matrix, jnp.zeros_like(matrix))
                folded = sum(exact(part, matrix) for part in sides).T
                for low, part in enumerate(split(folded, 2)):
                    out[slot, low] = part


def direct_kernel(pair, lines, chips, spot, pattern, base, inverse, *refs):
    pieces, stacks, out, blocks = refs[:chips], refs[chips:-2], refs[-2], refs[-1]
    row, chip, core = spot[ROW], spot[CHIP], spot[CORE]
    depth, line = spot[DEPTH], spot[LINE]
    share, size = base.shape
    for index, stack in enumerate(stacks):
        for turn in range(chips):
            blocks[index * chips + turn] = stack[turn * share : (turn + 1) * share, :]

    def times(left, right):
        return lax.dot_general(
            left, right, (((1,), (1,)), ((), ())), preferred_element_type=jnp.float32
        )

    total = jnp.zeros((share, size), jnp.float32)
    for index, piece in enumerate(pieces):
        deep = (chip ^ index) * CORES + core
        turn = (deep // CORES) ^ (depth // CORES)
        for across in range(lines):
            keep = pattern[pair, row, deep * lines + across]
            matrix = piece[0, 0, :, across * size : (across + 1) * size]
            matrix = jnp.where(keep > 0, matrix, jnp.zeros_like(matrix))
            total = total + times(blocks[(across ^ line) * chips + turn], matrix)
    value = base[...]
    for part in split(total, 3):
        value = value - times(part, inverse[0, 0])
    out[...] = value


def step_kernel(lines, base, *refs):
    out = refs[-1]
    refs = refs[:-1]
    total = base[...]
    share = total.shape[0]
    for term in range(len(refs) // (lines + 1)):
        stacks = refs[term * (lines + 1) :][:lines]
        matrix = refs[term * (lines + 1) + lines]
        each = matrix.shape[0] // lines
        for line in range(lines):
            for index in range(each):
                block = stacks[line][index * share : (index + 1) * share, :]
                for low in range(2):
                    total = total - exact(block, matrix[line * each + index, low])
    out[...] = total


def late_kernel(levels, chips, spot, *refs):
    out, turned = refs[-2], refs[-1]
    share = turned.shape[0] // chips
    out[0] = jnp.zeros_like(out[0])
    for level in range(1, levels):
        for b in range(chips):
            at = pl.ds(pl.multiple_of((spot[CHIP] ^ b) * share, share), share)
            part = refs[b][(level - 1) * share : level * share, :]
            turned[at, :] = part.astype(jnp.float32)
        out[level, 0] = turned[...].T.astype(out.dtype)


def last_kernel(chips, spot, whole, *refs):
    out, turned = refs[-2], refs[-1]
    share = turned.shape[0] // chips
    for b in range(chips):
        at = pl.ds(pl.multiple_of((spot[CHIP] ^ b) * share, share), share)
        turned[at, :] = refs[b][...].astype(jnp.float32)
    out[0, 0] = turned[...].T.astype(out.dtype)


def make_body(rows, cols):
    chips = cols // CORES
    lines = chips
    depths = rows // lines
    near = depths // CORES
    assert near == chips

    def send(value, source_of):
        pairs = []
        for z in range(depths):
            for y in range(lines):
                for x in range(chips):
                    for core in range(CORES):
                        a, b, c, d = source_of(z, y, x, core)
                        pairs.append(
                            (
                                (a * lines + b) * cols + c * CORES + d,
                                (z * lines + y) * cols + x * CORES + core,
                            )
                        )
        return lax.ppermute(value, ("prow", "pcol"), pairs)

    def after(value, *signs):
        return lax.optimization_barrier((value,) + signs)[0]

    def body(right_side, lower_blocks, upper_blocks, lower_inverse, upper_inverse, pattern):
        levels, _, size, width = right_side.shape
        share = width // chips
        row = lax.axis_index("prow")
        col = lax.axis_index("pcol")
        line, core = row % lines, col % CORES
        spot = jnp.stack([row, col // CORES, core, row // lines, line]).astype(jnp.int32)
        top = levels - 1
        piece = jax.ShapeDtypeStruct((share, size), jnp.float32)
        chunk = jax.ShapeDtypeStruct((share, size), jnp.bfloat16)
        turned = pltpu.VMEM((width, size), jnp.float32)

        def relay(blocks):
            return [
                send(blocks, lambda z, y, x, core, b=b: (z, y, x ^ b, core))
                for b in range(1, chips)
            ]

        def fold(picks, inverses, pieces, sign):
            shape = jax.ShapeDtypeStruct((near * lines, 2, size, size), jnp.bfloat16)
            return call(
                functools.partial(fold_kernel, picks, len(inverses)),
                [shape] * len(picks),
                [after(spot, sign), pattern] + inverses + pieces,
                scalars=2,
            )

        def deep(value, work=None):
            even = (row // lines) % CORES == core
            found = []
            for t in range(near):

                def source(z, y, x, core, t=t):
                    m = CORES * t + 1
                    if z % CORES == core and t < near - 1:
                        return z ^ (m + 1), y, x, core
                    return z ^ m, y, x, 1 - core

                found.append(send(value, source))
            parts = [jnp.where(even, ([value] + found)[t], found[t]) for t in range(near)]
            stack = jnp.concatenate(parts, axis=0)
            return after(stack, *work(found[0])) if work else stack

        def wide(stack):
            return [stack] + [
                send(stack, lambda z, y, x, core, e=e: (z, y ^ e, x, core)) for e in range(1, lines)
            ]

        def settle(partial_value):
            other = send(partial_value, lambda z, y, x, core: (z, y, x, 1 - core))
            return (partial_value + other).astype(jnp.bfloat16)

        def collect(value):
            return [value] + [
                send(value, lambda z, y, x, core, b=b: (z, y, x ^ b, core)) for b in range(1, chips)
            ]

        def step(base, terms):
            operands = [base]
            for stacks, matrix in terms:
                operands += stacks + [matrix]
            return call(functools.partial(step_kernel, lines), piece, operands)

        first = call(
            functools.partial(first_kernel, share),
            chunk,
            [spot, level_of(right_side, 0), level_of(lower_inverse, 0)],
            scalars=1,
            scratch=[turned],
            room=FULL_BYTES,
        )
        panels = call(
            functools.partial(panel_kernel, share, levels),
            [piece] * (2 * levels - 2),
            [spot, first, right_side, lower_inverse, upper_inverse],
            scalars=1,
            scratch=[turned],
        )
        ends, starts = panels[:levels], [None] + list(panels[levels:])

        low_all = relay(lower_blocks)
        last_pair = pair_index(top, top - 1)
        parts = (upper_blocks[last_pair:], upper_blocks[:last_pair])
        stack = deep(first, lambda sign: panels)
        stack, upper_one, upper_rest = lax.optimization_barrier((stack,) + parts)
        high_one = relay(upper_one)
        high_rest = relay(upper_rest)

        def fold_lower(later, both, sign):
            pairs = [pair_index(later, e) for e in range(later)]
            picks = tuple((pair, 0, False) for pair in pairs)
            inverses = [level_of(lower_inverse, later)]
            if both:
                inverses = [level_of(upper_inverse, later)] + inverses
            found = dict(zip(pairs, fold(picks, inverses, [lower_blocks] + low_all, sign)))
            (backward if both else forward).update(found)
            return list(found.values())

        def fold_upper(later, earlier, sign):
            pair = pair_index(later, earlier)
            picks = ((pair, pair if pair == last_pair else 0, True),)
            moved = high_one if pair == last_pair else high_rest
            inverses = [level_of(upper_inverse, earlier)]
            found = fold(picks, inverses, [upper_blocks] + moved, sign)[0]
            upward[later, earlier] = found
            return [found]

        fetched, back, solved = {}, {}, {}
        forward, backward, upward = {}, {}, {}
        fetched[0] = wide(stack)
        for level in range(1, top):
            value = starts[level]
            if level == 1:
                pieces = [level_of(blocks, 0) for blocks in [lower_blocks] + low_all]
                value = call(
                    functools.partial(direct_kernel, 0, lines, chips),
                    piece,
                    [spot, pattern, value, level_of(lower_inverse, 1)] + pieces + fetched[0],
                    scalars=2,
                    scratch=[pltpu.VMEM((near * lines, share, size), jnp.bfloat16)],
                )
            else:
                fold_lower(level, False, stack)
                for earlier in range(level):
                    value = step(value, [(fetched[earlier], forward[pair_index(level, earlier)])])
            stack = deep(settle(value), lambda sign: fold_lower(level, True, sign))
            fetched[level] = wide(stack)
        fold_lower(top, True, stack)

        for level in reversed(range(levels)):
            value = ends[level]
            if level == 0:
                results = collect(jnp.concatenate([solved[k] for k in range(1, levels)], axis=0))
                value = after(value, *results)
            for earlier in range(level):
                if level == top and earlier == top - 1:
                    value = after(value, *high_one)
                value = step(value, [(fetched[earlier], backward[pair_index(level, earlier)])])
            for later in reversed(range(level + 1, levels)):
                value = step(value, [(back[later], upward[later, level])])
            solved[level] = settle(value)
            if level > 0:
                found = solved[level]
                if level == 1:
                    found = after(found, *high_rest)
                stack = deep(found)
                back[level] = wide(stack)
                for later in range(level, levels):
                    fold_upper(later, level - 1, stack)
        shape = jax.ShapeDtypeStruct((levels, 1, size, width), jnp.bfloat16)
        whole = call(
            functools.partial(late_kernel, levels, chips),
            shape,
            [spot] + results,
            scalars=1,
            scratch=[turned],
        )
        operands = [spot, (whole, pl.BlockSpec(memory_space=pl.ANY))] + collect(solved[0])
        return call(
            functools.partial(last_kernel, chips),
            shape,
            operands,
            scalars=1,
            scratch=[turned],
            out_spec=pl.BlockSpec((1, 1, size, width), lambda step: (0, 0, 0, 0)),
            aliases={1: 0},
        )

    return body


def solution(mesh):
    placed = (
        P(None, "prow", None, None),
        P(None, "prow", None, "pcol"),
        P(None, "prow", None, "pcol"),
        P(None, "prow", None, None),
        P(None, "prow", None, None),
        P(),
    )
    return jax.shard_map(
        make_body(mesh.shape["prow"], mesh.shape["pcol"]),
        mesh=mesh,
        in_specs=placed,
        out_specs=P(None, "prow", None, None),
        check_vma=False,
    )
```

```python
import functools

import jax
import jax.numpy as jnp
from jax import lax
from jax.experimental import pallas as pl
from jax.experimental.pallas import tpu as pltpu
from jax.sharding import PartitionSpec as P

CORES = 2
ROW, CHIP, CORE, DEPTH, LINE = range(5)
VMEM_BYTES = 40 * 1024 * 1024
FULL_BYTES = 58 * 1024 * 1024


def pair_index(later, earlier):
    return later * (later - 1) // 2 + earlier


def exact(left, right):
    return jnp.dot(left, right, preferred_element_type=jnp.float32)


def split(values, count):
    parts = []
    for _ in range(count):
        part = values.astype(jnp.bfloat16)
        parts.append(part)
        values = values - part.astype(jnp.float32)
    return parts


def level_of(array, level):
    shape = (1,) + array.shape[1:]
    return array, pl.BlockSpec(shape, lambda step: (level,) + (0,) * (len(shape) - 1))


def call(kernel, shapes, operands, scalars=0, scratch=(), room=VMEM_BYTES, out_spec=None, aliases=None):
    arrays, specs = [], []
    for place, operand in enumerate(operands):
        if isinstance(operand, tuple):
            array, spec = operand
        else:
            array = operand
            space = pltpu.SMEM if place < scalars else pltpu.VMEM
            spec = pl.BlockSpec(memory_space=space)
        arrays.append(array)
        specs.append(spec)
    return pl.pallas_call(
        kernel,
        grid=(1,),
        out_shape=shapes,
        in_specs=specs,
        out_specs=out_spec
        or jax.tree.map(lambda _: pl.BlockSpec(memory_space=pltpu.VMEM), shapes),
        input_output_aliases=aliases or {},
        scratch_shapes=list(scratch),
        compiler_params=pltpu.CompilerParams(vmem_limit_bytes=room),
    )(*arrays)


def share_of(values, turned, share, chip):
    turned[...] = values.T
    return turned[pl.ds(pl.multiple_of(chip * share, share), share), :]


def first_kernel(share, spot, rhs, inverse, out, turned):
    value = exact(inverse[0, 0], rhs[0, 0])
    out[...] = share_of(value, turned, share, spot[CHIP]).astype(out.dtype)


def panel_kernel(share, levels, spot, first, rhs, lower, upper, *rest):
    outs, turned = rest[:-1], rest[-1]
    chip = spot[CHIP]
    mine = spot[CORE] == 0
    value = lax.dot_general(
        first[...], upper[0, 0], (((1,), (1,)), ((), ())), preferred_element_type=jnp.float32
    )
    outs[0][...] = jnp.where(mine, value, 0.0)
    for level in range(1, levels):
        start = exact(lower[level, 0], rhs[level, 0])
        end = sum(exact(upper[level, 0], part) for part in split(start, 3))
        outs[level][...] = jnp.where(mine, share_of(end, turned, share, chip), 0.0)
        if level < levels - 1:
            value = share_of(start, turned, share, chip)
            outs[levels + level - 1][...] = jnp.where(mine, value, 0.0)


def fold_kernel(picks, left_count, spot, pattern, *refs):
    outs = refs[-len(picks) :]
    pieces = refs[left_count : -len(picks)]
    row, chip, core = spot[ROW], spot[CHIP], spot[CORE]
    depth, line = spot[DEPTH], spot[LINE]
    size = outs[0].shape[-1]
    group = pieces[0].shape[-1] // size
    if left_count == 1:
        sides = [refs[0][0, 0]]
    else:
        sides = split(exact(refs[0][0, 0], refs[1][0, 0]), 3)
    for index, piece in enumerate(pieces):
        deep = (chip ^ index) * CORES + core
        turn = (deep // CORES) ^ (depth // CORES)
        for across in range(group):
            block = deep * group + across
            slot = (across ^ line) * len(pieces) + turn
            columns = slice(across * size, (across + 1) * size)
            for pick, out in zip(picks, outs):
                pair, first, is_upper = pick
                keep = pattern[pair, block, row] if is_upper else pattern[pair, row, block]
                matrix = piece[pair - first if index else pair, 0, :, columns]
                matrix = jnp.where(keep > 0, matrix, jnp.zeros_like(matrix))
                folded = sum(exact(part, matrix) for part in sides).T
                for low, part in enumerate(split(folded, 2)):
                    out[slot, low] = part


def direct_kernel(pair, lines, chips, spot, pattern, base, inverse, *refs):
    pieces, stacks, out, blocks = refs[:chips], refs[chips:-2], refs[-2], refs[-1]
    row, chip, core = spot[ROW], spot[CHIP], spot[CORE]
    depth, line = spot[DEPTH], spot[LINE]
    share, size = base.shape
    for index, stack in enumerate(stacks):
        for turn in range(chips):
            blocks[index * chips + turn] = stack[turn * share : (turn + 1) * share, :]

    def times(left, right):
        return lax.dot_general(
            left, right, (((1,), (1,)), ((), ())), preferred_element_type=jnp.float32
        )

    total = jnp.zeros((share, size), jnp.float32)
    for index, piece in enumerate(pieces):
        deep = (chip ^ index) * CORES + core
        turn = (deep // CORES) ^ (depth // CORES)
        for across in range(lines):
            keep = pattern[pair, row, deep * lines + across]
            matrix = piece[0, 0, :, across * size : (across + 1) * size]
            matrix = jnp.where(keep > 0, matrix, jnp.zeros_like(matrix))
            total = total + times(blocks[(across ^ line) * chips + turn], matrix)
    value = base[...]
    for part in split(total, 3):
        value = value - times(part, inverse[0, 0])
    out[...] = value


def step_kernel(lines, base, *refs):
    out = refs[-1]
    refs = refs[:-1]
    total = base[...]
    share = total.shape[0]
    for term in range(len(refs) // (lines + 1)):
        stacks = refs[term * (lines + 1) :][:lines]
        matrix = refs[term * (lines + 1) + lines]
        each = matrix.shape[0] // lines
        for line in range(lines):
            for index in range(each):
                block = stacks[line][index * share : (index + 1) * share, :]
                for low in range(2):
                    total = total - exact(block, matrix[line * each + index, low])
    out[...] = total


def late_kernel(levels, chips, spot, *refs):
    out, turned = refs[-2], refs[-1]
    share = turned.shape[0] // chips
    out[0] = jnp.zeros_like(out[0])
    for level in range(1, levels):
        for b in range(chips):
            at = pl.ds(pl.multiple_of((spot[CHIP] ^ b) * share, share), share)
            part = refs[b][(level - 1) * share : level * share, :]
            turned[at, :] = part.astype(jnp.float32)
        out[level, 0] = turned[...].T.astype(out.dtype)


def last_kernel(chips, spot, whole, *refs):
    out, turned = refs[-2], refs[-1]
    share = turned.shape[0] // chips
    for b in range(chips):
        at = pl.ds(pl.multiple_of((spot[CHIP] ^ b) * share, share), share)
        turned[at, :] = refs[b][...].astype(jnp.float32)
    out[0, 0] = turned[...].T.astype(out.dtype)


def make_body(rows, cols):
    chips = cols // CORES
    lines = chips
    depths = rows // lines
    near = depths // CORES
    assert near == chips

    def send(value, source_of):
        pairs = []
        for z in range(depths):
            for y in range(lines):
                for x in range(chips):
                    for core in range(CORES):
                        a, b, c, d = source_of(z, y, x, core)
                        pairs.append(
                            (
                                (a * lines + b) * cols + c * CORES + d,
                                (z * lines + y) * cols + x * CORES + core,
                            )
                        )
        return lax.ppermute(value, ("prow", "pcol"), pairs)

    def after(value, *signs):
        return lax.optimization_barrier((value,) + signs)[0]

    def body(right_side, lower_blocks, upper_blocks, lower_inverse, upper_inverse, pattern):
        levels, _, size, width = right_side.shape
        share = width // chips
        row = lax.axis_index("prow")
        col = lax.axis_index("pcol")
        line, core = row % lines, col % CORES
        spot = jnp.stack([row, col // CORES, core, row // lines, line]).astype(jnp.int32)
        top = levels - 1
        piece = jax.ShapeDtypeStruct((share, size), jnp.float32)
        chunk = jax.ShapeDtypeStruct((share, size), jnp.bfloat16)
        turned = pltpu.VMEM((width, size), jnp.float32)

        def relay(blocks):
            return [
                send(blocks, lambda z, y, x, core, b=b: (z, y, x ^ b, core))
                for b in range(1, chips)
            ]

        def fold(picks, inverses, pieces, sign):
            shape = jax.ShapeDtypeStruct((near * lines, 2, size, size), jnp.bfloat16)
            return call(
                functools.partial(fold_kernel, picks, len(inverses)),
                [shape] * len(picks),
                [after(spot, sign), pattern] + inverses + pieces,
                scalars=2,
            )

        def deep(value, work=None):
            even = (row // lines) % CORES == core
            found = []
            for t in range(near):

                def source(z, y, x, core, t=t):
                    m = CORES * t + 1
                    if z % CORES == core and t < near - 1:
                        return z ^ (m + 1), y, x, core
                    return z ^ m, y, x, 1 - core

                found.append(send(value, source))
            parts = [jnp.where(even, ([value] + found)[t], found[t]) for t in range(near)]
            stack = jnp.concatenate(parts, axis=0)
            return after(stack, *work(found[0])) if work else stack

        def wide(stack):
            return [stack] + [
                send(stack, lambda z, y, x, core, e=e: (z, y ^ e, x, core)) for e in range(1, lines)
            ]

        def settle(partial_value):
            other = send(partial_value, lambda z, y, x, core: (z, y, x, 1 - core))
            return (partial_value + other).astype(jnp.bfloat16)

        def collect(value):
            return [value] + [
                send(value, lambda z, y, x, core, b=b: (z, y, x ^ b, core)) for b in range(1, chips)
            ]

        def step(base, terms):
            operands = [base]
            for stacks, matrix in terms:
                operands += stacks + [matrix]
            return call(functools.partial(step_kernel, lines), piece, operands)

        first = call(
            functools.partial(first_kernel, share),
            chunk,
            [spot, level_of(right_side, 0), level_of(lower_inverse, 0)],
            scalars=1,
            scratch=[turned],
            room=FULL_BYTES,
        )
        panels = call(
            functools.partial(panel_kernel, share, levels),
            [piece] * (2 * levels - 2),
            [spot, first, right_side, lower_inverse, upper_inverse],
            scalars=1,
            scratch=[turned],
        )
        ends, starts = panels[:levels], [None] + list(panels[levels:])

        low_all = relay(lower_blocks)
        last_pair = pair_index(top, top - 1)
        parts = (upper_blocks[last_pair:], upper_blocks[:last_pair])
        stack = deep(first, lambda sign: panels)
        stack, upper_one, upper_rest = lax.optimization_barrier((stack,) + parts)
        high_one = relay(upper_one)
        high_rest = relay(upper_rest)

        def fold_lower(later, both, sign):
            pairs = [pair_index(later, e) for e in range(later)]
            picks = tuple((pair, 0, False) for pair in pairs)
            inverses = [level_of(lower_inverse, later)]
            if both:
                inverses = [level_of(upper_inverse, later)] + inverses
            found = dict(zip(pairs, fold(picks, inverses, [lower_blocks] + low_all, sign)))
            (backward if both else forward).update(found)
            return list(found.values())

        def fold_upper(later, earlier, sign):
            pair = pair_index(later, earlier)
            picks = ((pair, pair if pair == last_pair else 0, True),)
            moved = high_one if pair == last_pair else high_rest
            inverses = [level_of(upper_inverse, earlier)]
            found = fold(picks, inverses, [upper_blocks] + moved, sign)[0]
            upward[later, earlier] = found
            return [found]

        fetched, back, solved = {}, {}, {}
        forward, backward, upward = {}, {}, {}
        fetched[0] = wide(stack)
        for level in range(1, top):
            value = starts[level]
            if level == 1:
                pieces = [level_of(blocks, 0) for blocks in [lower_blocks] + low_all]
                value = call(
                    functools.partial(direct_kernel, 0, lines, chips),
                    piece,
                    [spot, pattern, value, level_of(lower_inverse, 1)] + pieces + fetched[0],
                    scalars=2,
                    scratch=[pltpu.VMEM((near * lines, share, size), jnp.bfloat16)],
                )
            else:
                fold_lower(level, False, stack)
                for earlier in range(level):
                    value = step(value, [(fetched[earlier], forward[pair_index(level, earlier)])])
            stack = deep(settle(value))
            fold_lower(level, True, stack)
            fetched[level] = wide(stack)
        fold_lower(top, True, stack)

        for level in reversed(range(levels)):
            value = ends[level]
            if level == 0:
                results = collect(jnp.concatenate([solved[k] for k in range(1, levels)], axis=0))
                value = after(value, *results)
            for earlier in range(level):
                if level == top and earlier == top - 1:
                    value = after(value, *high_one)
                value = step(value, [(fetched[earlier], backward[pair_index(level, earlier)])])
            for later in reversed(range(level + 1, levels)):
                value = step(value, [(back[later], upward[later, level])])
            solved[level] = settle(value)
            if level > 0:
                found = solved[level]
                if level == 1:
                    found = after(found, *high_rest)
                stack = deep(found)
                back[level] = wide(stack)
                for later in range(level, levels):
                    fold_upper(later, level - 1, stack)
        shape = jax.ShapeDtypeStruct((levels, 1, size, width), jnp.bfloat16)
        whole = call(
            functools.partial(late_kernel, levels, chips),
            shape,
            [spot] + results,
            scalars=1,
            scratch=[turned],
        )
        operands = [spot, (whole, pl.BlockSpec(memory_space=pl.ANY))] + collect(solved[0])
        return call(
            functools.partial(last_kernel, chips),
            shape,
            operands,
            scalars=1,
            scratch=[turned],
            out_spec=pl.BlockSpec((1, 1, size, width), lambda step: (0, 0, 0, 0)),
            aliases={1: 0},
        )

    return body


def solution(mesh):
    placed = (
        P(None, "prow", None, None),
        P(None, "prow", None, "pcol"),
        P(None, "prow", None, "pcol"),
        P(None, "prow", None, None),
        P(None, "prow", None, None),
        P(),
    )
    return jax.shard_map(
        make_body(mesh.shape["prow"], mesh.shape["pcol"]),
        mesh=mesh,
        in_specs=placed,
        out_specs=P(None, "prow", None, None),
        check_vma=False,
    )
```

```python
import functools

import jax
import jax.numpy as jnp
from jax import lax
from jax.experimental import pallas as pl
from jax.experimental.pallas import tpu as pltpu
from jax.sharding import PartitionSpec as P

CORES = 2
ROW, CHIP, CORE, DEPTH, LINE = range(5)
VMEM_BYTES = 40 * 1024 * 1024
FULL_BYTES = 58 * 1024 * 1024


def pair_index(later, earlier):
    return later * (later - 1) // 2 + earlier


def exact(left, right):
    return jnp.dot(left, right, preferred_element_type=jnp.float32)


def split(values, count):
    parts = []
    for _ in range(count):
        part = values.astype(jnp.bfloat16)
        parts.append(part)
        values = values - part.astype(jnp.float32)
    return parts


def level_of(array, level):
    shape = (1,) + array.shape[1:]
    return array, pl.BlockSpec(shape, lambda step: (level,) + (0,) * (len(shape) - 1))


def call(kernel, shapes, operands, scalars=0, scratch=(), room=VMEM_BYTES, out_spec=None, aliases=None):
    arrays, specs = [], []
    for place, operand in enumerate(operands):
        if isinstance(operand, tuple):
            array, spec = operand
        else:
            array = operand
            space = pltpu.SMEM if place < scalars else pltpu.VMEM
            spec = pl.BlockSpec(memory_space=space)
        arrays.append(array)
        specs.append(spec)
    return pl.pallas_call(
        kernel,
        grid=(1,),
        out_shape=shapes,
        in_specs=specs,
        out_specs=out_spec
        or jax.tree.map(lambda _: pl.BlockSpec(memory_space=pltpu.VMEM), shapes),
        input_output_aliases=aliases or {},
        scratch_shapes=list(scratch),
        compiler_params=pltpu.CompilerParams(vmem_limit_bytes=room),
    )(*arrays)


def share_of(values, turned, share, chip):
    turned[...] = values.T
    return turned[pl.ds(pl.multiple_of(chip * share, share), share), :]


def first_kernel(share, spot, rhs, inverse, out, turned):
    value = exact(inverse[0, 0], rhs[0, 0])
    out[...] = share_of(value, turned, share, spot[CHIP]).astype(out.dtype)


def panel_kernel(share, levels, spot, first, rhs, lower, upper, *rest):
    outs, turned = rest[:-1], rest[-1]
    chip = spot[CHIP]
    mine = spot[CORE] == 0
    value = lax.dot_general(
        first[...], upper[0, 0], (((1,), (1,)), ((), ())), preferred_element_type=jnp.float32
    )
    outs[0][...] = jnp.where(mine, value, 0.0)
    for level in range(1, levels):
        start = exact(lower[level, 0], rhs[level, 0])
        end = sum(exact(upper[level, 0], part) for part in split(start, 3))
        outs[level][...] = jnp.where(mine, share_of(end, turned, share, chip), 0.0)
        if level < levels - 1:
            value = share_of(start, turned, share, chip)
            outs[levels + level - 1][...] = jnp.where(mine, value, 0.0)


def fold_kernel(picks, left_count, spot, pattern, *refs):
    outs = refs[-len(picks) :]
    pieces = refs[left_count : -len(picks)]
    row, chip, core = spot[ROW], spot[CHIP], spot[CORE]
    depth, line = spot[DEPTH], spot[LINE]
    size = outs[0].shape[-1]
    group = pieces[0].shape[-1] // size
    if left_count == 1:
        sides = [refs[0][0, 0]]
    else:
        sides = split(exact(refs[0][0, 0], refs[1][0, 0]), 3)
    for index, piece in enumerate(pieces):
        deep = (chip ^ index) * CORES + core
        turn = (deep // CORES) ^ (depth // CORES)
        for across in range(group):
            block = deep * group + across
            slot = (across ^ line) * len(pieces) + turn
            columns = slice(across * size, (across + 1) * size)
            for pick, out in zip(picks, outs):
                pair, first, is_upper = pick
                keep = pattern[pair, block, row] if is_upper else pattern[pair, row, block]
                matrix = piece[pair - first if index else pair, 0, :, columns]
                matrix = jnp.where(keep > 0, matrix, jnp.zeros_like(matrix))
                folded = sum(exact(part, matrix) for part in sides).T
                for low, part in enumerate(split(folded, 2)):
                    out[slot, low] = part


def direct_kernel(pair, lines, chips, spot, pattern, base, inverse, *refs):
    pieces, stacks, out, blocks = refs[:chips], refs[chips:-2], refs[-2], refs[-1]
    row, chip, core = spot[ROW], spot[CHIP], spot[CORE]
    depth, line = spot[DEPTH], spot[LINE]
    share, size = base.shape
    for index, stack in enumerate(stacks):
        for turn in range(chips):
            blocks[index * chips + turn] = stack[turn * share : (turn + 1) * share, :]

    def times(left, right):
        return lax.dot_general(
            left, right, (((1,), (1,)), ((), ())), preferred_element_type=jnp.float32
        )

    total = jnp.zeros((share, size), jnp.float32)
    for index, piece in enumerate(pieces):
        deep = (chip ^ index) * CORES + core
        turn = (deep // CORES) ^ (depth // CORES)
        for across in range(lines):
            keep = pattern[pair, row, deep * lines + across]
            matrix = piece[0, 0, :, across * size : (across + 1) * size]
            matrix = jnp.where(keep > 0, matrix, jnp.zeros_like(matrix))
            total = total + times(blocks[(across ^ line) * chips + turn], matrix)
    value = base[...]
    for part in split(total, 3):
        value = value - times(part, inverse[0, 0])
    out[...] = value


def step_kernel(lines, base, *refs):
    out = refs[-1]
    refs = refs[:-1]
    total = base[...]
    share = total.shape[0]
    for term in range(len(refs) // (lines + 1)):
        stacks = refs[term * (lines + 1) :][:lines]
        matrix = refs[term * (lines + 1) + lines]
        each = matrix.shape[0] // lines
        for line in range(lines):
            for index in range(each):
                block = stacks[line][index * share : (index + 1) * share, :]
                for low in range(2):
                    total = total - exact(block, matrix[line * each + index, low])
    out[...] = total


def late_kernel(levels, chips, spot, *refs):
    out, turned = refs[-2], refs[-1]
    share = turned.shape[0] // chips
    out[0] = jnp.zeros_like(out[0])
    for level in range(1, levels):
        for b in range(chips):
            at = pl.ds(pl.multiple_of((spot[CHIP] ^ b) * share, share), share)
            part = refs[b][(level - 1) * share : level * share, :]
            turned[at, :] = part.astype(jnp.float32)
        out[level, 0] = turned[...].T.astype(out.dtype)


def last_kernel(chips, spot, whole, *refs):
    out, turned = refs[-2], refs[-1]
    share = turned.shape[0] // chips
    for b in range(chips):
        at = pl.ds(pl.multiple_of((spot[CHIP] ^ b) * share, share), share)
        turned[at, :] = refs[b][...].astype(jnp.float32)
    out[0, 0] = turned[...].T.astype(out.dtype)


def make_body(rows, cols):
    chips = cols // CORES
    lines = chips
    depths = rows // lines
    near = depths // CORES
    assert near == chips

    def send(value, source_of):
        pairs = []
        for z in range(depths):
            for y in range(lines):
                for x in range(chips):
                    for core in range(CORES):
                        a, b, c, d = source_of(z, y, x, core)
                        pairs.append(
                            (
                                (a * lines + b) * cols + c * CORES + d,
                                (z * lines + y) * cols + x * CORES + core,
                            )
                        )
        return lax.ppermute(value, ("prow", "pcol"), pairs)

    def after(value, *signs):
        return lax.optimization_barrier((value,) + signs)[0]

    def body(right_side, lower_blocks, upper_blocks, lower_inverse, upper_inverse, pattern):
        levels, _, size, width = right_side.shape
        share = width // chips
        row = lax.axis_index("prow")
        col = lax.axis_index("pcol")
        line, core = row % lines, col % CORES
        spot = jnp.stack([row, col // CORES, core, row // lines, line]).astype(jnp.int32)
        top = levels - 1
        piece = jax.ShapeDtypeStruct((share, size), jnp.float32)
        chunk = jax.ShapeDtypeStruct((share, size), jnp.bfloat16)
        turned = pltpu.VMEM((width, size), jnp.float32)

        def relay(blocks):
            return [
                send(blocks, lambda z, y, x, core, b=b: (z, y, x ^ b, core))
                for b in range(1, chips)
            ]

        def fold(picks, inverses, pieces, sign):
            shape = jax.ShapeDtypeStruct((near * lines, 2, size, size), jnp.bfloat16)
            return call(
                functools.partial(fold_kernel, picks, len(inverses)),
                [shape] * len(picks),
                [after(spot, sign), pattern] + inverses + pieces,
                scalars=2,
            )

        def deep(value, work=None):
            even = (row // lines) % CORES == core
            found = []
            for t in range(near):

                def source(z, y, x, core, t=t):
                    m = CORES * t + 1
                    if z % CORES == core and t < near - 1:
                        return z ^ (m + 1), y, x, core
                    return z ^ m, y, x, 1 - core

                found.append(send(value, source))
            parts = [jnp.where(even, ([value] + found)[t], found[t]) for t in range(near)]
            stack = jnp.concatenate(parts, axis=0)
            return after(stack, *work(found[0])) if work else stack

        def wide(stack):
            return [stack] + [
                send(stack, lambda z, y, x, core, e=e: (z, y ^ e, x, core)) for e in range(1, lines)
            ]

        def settle(partial_value):
            other = send(partial_value, lambda z, y, x, core: (z, y, x, 1 - core))
            return (partial_value + other).astype(jnp.bfloat16)

        def collect(value):
            return [value] + [
                send(value, lambda z, y, x, core, b=b: (z, y, x ^ b, core)) for b in range(1, chips)
            ]

        def step(base, terms):
            operands = [base]
            for stacks, matrix in terms:
                operands += stacks + [matrix]
            return call(functools.partial(step_kernel, lines), piece, operands)

        first = call(
            functools.partial(first_kernel, share),
            chunk,
            [spot, level_of(right_side, 0), level_of(lower_inverse, 0)],
            scalars=1,
            scratch=[turned],
            room=FULL_BYTES,
        )
        panels = call(
            functools.partial(panel_kernel, share, levels),
            [piece] * (2 * levels - 2),
            [spot, first, right_side, lower_inverse, upper_inverse],
            scalars=1,
            scratch=[turned],
        )
        ends, starts = panels[:levels], [None] + list(panels[levels:])

        low_all = relay(lower_blocks)
        last_pair = pair_index(top, top - 1)
        parts = (upper_blocks[last_pair:], upper_blocks[:last_pair])
        stack = deep(first, lambda sign: panels)
        stack, upper_one, upper_rest = lax.optimization_barrier((stack,) + parts)
        high_one = relay(upper_one)
        high_rest = relay(upper_rest)

        def fold_lower(later, both, sign):
            pairs = [pair_index(later, e) for e in range(later)]
            picks = tuple((pair, 0, False) for pair in pairs)
            inverses = [level_of(lower_inverse, later)]
            if both:
                inverses = [level_of(upper_inverse, later)] + inverses
            found = dict(zip(pairs, fold(picks, inverses, [lower_blocks] + low_all, sign)))
            (backward if both else forward).update(found)
            return list(found.values())

        def fold_upper(later, earlier, sign):
            pair = pair_index(later, earlier)
            picks = ((pair, pair if pair == last_pair else 0, True),)
            moved = high_one if pair == last_pair else high_rest
            inverses = [level_of(upper_inverse, earlier)]
            found = fold(picks, inverses, [upper_blocks] + moved, sign)[0]
            upward[later, earlier] = found
            return [found]

        fetched, back, solved = {}, {}, {}
        forward, backward, upward = {}, {}, {}
        fetched[0] = wide(stack)
        for level in range(1, top):
            value = starts[level]
            if level == 1:
                pieces = [level_of(blocks, 0) for blocks in [lower_blocks] + low_all]
                value = call(
                    functools.partial(direct_kernel, 0, lines, chips),
                    piece,
                    [spot, pattern, value, level_of(lower_inverse, 1)] + pieces + fetched[0],
                    scalars=2,
                    scratch=[pltpu.VMEM((near * lines, share, size), jnp.bfloat16)],
                )
            else:
                fold_lower(level, False, stack)
                for earlier in range(level):
                    value = step(value, [(fetched[earlier], forward[pair_index(level, earlier)])])
            stack = deep(settle(value))
            fold_lower(level, True, stack)
            fetched[level] = wide(stack)
        fold_lower(top, True, stack)

        for level in reversed(range(levels)):
            value = ends[level]
            if level == 0:
                results = collect(jnp.concatenate([solved[k] for k in range(1, levels)], axis=0))
                value = after(value, *results)
            for earlier in range(level):
                if level == top and earlier == top - 1:
                    value = after(value, *high_one)
                value = step(value, [(fetched[earlier], backward[pair_index(level, earlier)])])
            for later in reversed(range(level + 1, levels)):
                value = step(value, [(back[later], upward[later, level])])
            if level == 1:
                value = after(value, *high_rest)
            solved[level] = settle(value)
            if level > 0:
                found = solved[level]
                stack = deep(found)
                back[level] = wide(stack)
                for later in range(level, levels):
                    fold_upper(later, level - 1, stack)
        shape = jax.ShapeDtypeStruct((levels, 1, size, width), jnp.bfloat16)
        whole = call(
            functools.partial(late_kernel, levels, chips),
            shape,
            [spot] + results,
            scalars=1,
            scratch=[turned],
        )
        operands = [spot, (whole, pl.BlockSpec(memory_space=pl.ANY))] + collect(solved[0])
        return call(
            functools.partial(last_kernel, chips),
            shape,
            operands,
            scalars=1,
            scratch=[turned],
            out_spec=pl.BlockSpec((1, 1, size, width), lambda step: (0, 0, 0, 0)),
            aliases={1: 0},
        )

    return body


def solution(mesh):
    placed = (
        P(None, "prow", None, None),
        P(None, "prow", None, "pcol"),
        P(None, "prow", None, "pcol"),
        P(None, "prow", None, None),
        P(None, "prow", None, None),
        P(),
    )
    return jax.shard_map(
        make_body(mesh.shape["prow"], mesh.shape["pcol"]),
        mesh=mesh,
        in_specs=placed,
        out_specs=P(None, "prow", None, None),
        check_vma=False,
    )
```
